128 devices in a mesh: dev: 128 (over z, y, x, core).
Axes of the slice: x: 4, y: 4, z: 4, core: 2. Of those that a mesh axis runs over, the one named last changes fastest.
Arguments:
- leaves: float32 [2, 1000, 59392], P(None, None, 'dev'), may hold values from -6 to 6
- send_slot: int32 [4, 32768], P(None, 'dev'), may hold values from 0 to 128, as said below
- recv_slot: int32 [4, 32768], P(None, 'dev'), may hold values from 0 to 128, as said below
- filter_up: float32 [20, 20], replicated, may hold values from -1 to 1.05
- filter_down: float32 [20, 20], replicated, may hold values from -1 to 1.05
Outputs:
- leaves_out: float32 [2, 1000, 59392], P(None, None, 'dev')
The draws below stay inside these ranges and needn't reach their ends.
Inputs may be any that keep to these rules, and one draw needn't show every extreme that they name: `send_slot`: for each level and each device's block of 256 entries, every local child 0 .. 127 stands in exactly one slot and all other slots hold 128; the number of children one device sends to one device at one level varies from pair to pair and reaches 2 in every level. `recv_slot`: for each level and each device's block of 256 entries, the slots that its sources fill hold each of 0 .. 127 exactly once, and exactly the empty slots hold 128.
All inputs are finite; a program needn't handle non-finite values.
Results may differ from the reference program's by a relative error of at most 0.0001.
Values sent between devices are 32-bit elements; how exact they have to be, the bound alone decides.
No kernel may reach another device: no remote copies, remote signals or barrier semaphores. Data moves between devices by JAX's collectives and lax.ppermute only.
A program may use at most 128 MiB of HBM per device.

```python
import jax
import jax.numpy as jnp
from jax import lax

K = 10
ORBITALS = 2
STEPS = 4
PER = 128
CAP = 2
LEAVES = 59392
N_DEV = 128


def level_routes(level_key):
    keys = jax.random.split(level_key, 6)
    half = N_DEV // 2
    middle = PER // N_DEV
    swings = jax.random.randint(keys[0], (half,), 0, middle + 1).astype(jnp.int32)
    swings = swings.at[0].set(middle)
    counts = jnp.concatenate([middle + swings, middle - swings]).astype(jnp.int32)
    counts = jax.random.permutation(keys[1], counts)
    sender_perm = jax.random.permutation(keys[2], N_DEV).astype(jnp.int32)
    target_perm = jax.random.permutation(keys[3], N_DEV).astype(jnp.int32)
    pairs = counts[(target_perm[None, :] - sender_perm[:, None]) % N_DEV]
    within = jnp.arange(CAP, dtype=jnp.int32)
    live = within[None, None, :] < pairs[:, :, None]
    send_start = jnp.cumsum(pairs, axis=1) - pairs
    send_pos = jnp.clip(send_start[:, :, None] + within, 0, PER - 1).reshape(N_DEV, N_DEV * CAP)
    child_perm = jax.vmap(lambda one_key: jax.random.permutation(one_key, PER))(jax.random.split(keys[4], N_DEV)).astype(jnp.int32)
    sent = jnp.take_along_axis(child_perm, send_pos, axis=1).reshape(N_DEV, N_DEV, CAP)
    send = jnp.where(live, sent, PER).reshape(-1)
    recv_start = jnp.cumsum(pairs, axis=0) - pairs
    recv_pos = jnp.clip(recv_start[:, :, None] + within, 0, PER - 1)
    recv_pos = jnp.transpose(recv_pos, (1, 0, 2)).reshape(N_DEV, N_DEV * CAP)
    parent_perm = jax.vmap(lambda one_key: jax.random.permutation(one_key, PER))(jax.random.split(keys[5], N_DEV)).astype(jnp.int32)
    arrived = jnp.take_along_axis(parent_perm, recv_pos, axis=1).reshape(N_DEV, N_DEV, CAP)
    recv = jnp.where(jnp.transpose(live, (1, 0, 2)), arrived, PER).reshape(-1)
    return (send.astype(jnp.int32), recv.astype(jnp.int32))


def all_routes(key):
    sends = []
    recvs = []
    for level in range(STEPS):
        send, recv = level_routes(jax.random.fold_in(key, 101 + level))
        sends.append(send)
        recvs.append(recv)
    return (jnp.stack(sends), jnp.stack(recvs))


def draw_send_slot(key, part):
    return all_routes(key)[0]


def draw_recv_slot(key, part):
    return all_routes(key)[1]


def assemble(diagonal, spread):
    identity = jnp.eye(diagonal.shape[0], dtype=jnp.float32)
    return identity * diagonal[:, None] + (1.0 - identity) * spread


def draw_filter_up(key, part):
    key = jax.random.fold_in(key, 37)
    key_diag, key_rest = jax.random.split(key)
    diagonal = jax.random.uniform(key_diag, (2 * K,), jnp.float32, 0.85, 1.05)
    spread = 0.07 * jax.random.normal(key_rest, (2 * K, 2 * K), jnp.float32)
    return assemble(diagonal, spread)


def draw_filter_down(key, part):
    key = jax.random.fold_in(key, 53)
    key_diag, key_rest = jax.random.split(key)
    diagonal = jax.random.uniform(key_diag, (2 * K,), jnp.float32, 0.85, 1.05)
    spread = 0.07 * jax.random.normal(key_rest, (2 * K, 2 * K), jnp.float32)
    return assemble(diagonal, spread)


def block_scale(rng, shape, cuts, least, top_value):
    def one(position, parts):
        steps = jax.random.uniform(jax.random.fold_in(jax.random.fold_in(rng, 6), position), (parts,), jnp.float32, least / len(cuts), top_value / len(cuts))
        return jnp.repeat(jnp.exp(steps), shape[position] // parts).reshape((-1,) + (1,) * (len(shape) - position - 1))

    gain = one(*cuts[0])
    for cut in cuts[1:]:
        gain = gain * one(*cut)
    return gain


def noise(stream_key, extent, scale, reach, cuts=(), kind=jnp.bfloat16):
    values = scale * jax.random.normal(stream_key, extent, jnp.float32)
    if cuts:
        values = values * block_scale(stream_key, extent, cuts, -0.22, 0.18)
    return jnp.clip(values, -reach, reach).astype(kind)


def setup_inputs(seed: int = 0) -> dict:
    key_list = jax.random.split(jax.random.key(seed), 6)
    leaves = noise(key_list[0], (ORBITALS, K ** 3, LEAVES), 1.0, 6.0, ((2, 128),), jnp.float32)
    send_slot = draw_send_slot(jax.random.fold_in(key_list[5], 71), 0)
    recv_slot = draw_recv_slot(jax.random.fold_in(key_list[5], 71), 0)
    filter_up = draw_filter_up(jax.random.fold_in(key_list[5], 71), 0)
    filter_down = draw_filter_down(jax.random.fold_in(key_list[5], 71), 0)
    return {"leaves": leaves, "send_slot": send_slot, "recv_slot": recv_slot, "filter_up": filter_up, "filter_down": filter_down}


highest = lax.Precision.HIGHEST


def analyse(children, filters, degree):
    number = children.shape[-1] // 8
    blocks = children.reshape(children.shape[0], degree, degree, degree, number, 2, 2, 2)
    halves = filters.reshape(2 * degree, 2, degree)
    partial_sum = jnp.einsum("axi,nijkpxyz->najkpyz", halves, blocks, precision=highest)
    partial_sum = jnp.einsum("byj,najkpyz->nabkpz", halves, partial_sum, precision=highest)
    return jnp.einsum("czk,nabkpz->nabcp", halves, partial_sum, precision=highest)


def synthesise(source, filters, degree):
    row_parts = filters.reshape(2, degree, 2 * degree)
    partial_sum = jnp.einsum("xia,nabcp->nibcpx", row_parts, source, precision=highest)
    partial_sum = jnp.einsum("yjb,nibcpx->nijcpxy", row_parts, partial_sum, precision=highest)
    partial_sum = jnp.einsum("zkc,nijcpxy->nijkpxyz", row_parts, partial_sum, precision=highest)
    return partial_sum.reshape(source.shape[0], degree ** 3, source.shape[-1] * 8)


def invert(mapping, width):
    positions = jnp.broadcast_to(jnp.arange(mapping.shape[-1], dtype=jnp.int32), mapping.shape)
    row_ids = jnp.arange(mapping.shape[0], dtype=jnp.int32)[:, None]
    table = jnp.zeros((mapping.shape[0], width + 1), jnp.int32).at[row_ids, mapping].set(positions)
    return table[:, :width]


def leaf_range(height, parents):
    if height == 0:
        return 0, 8 * parents
    return 8 * parents + 7 * parents * (height - 1), 7 * parents


def pick_columns(blocks, mapping):
    return jax.vmap(lambda slab, index_row: jnp.take(slab, index_row, axis=2), in_axes=(2, 0), out_axes=2)(blocks, mapping)


def with_empty(blocks):
    empty = jnp.zeros(blocks.shape[:-1] + (1,), blocks.dtype)
    return jnp.concatenate([blocks, empty], axis=-1)


def reference(leaves, send_slot, recv_slot, filter_up, filter_down):
    orbitals, cells, total = leaves.shape
    degree = filter_up.shape[0] // 2
    devices = N_DEV
    slot_count = send_slot.shape[1] // devices
    capacity = slot_count // devices
    per_dev = PER
    parents = per_dev // 8
    leaf_dev = leaves.reshape(orbitals, cells, devices, total // devices)
    senders = send_slot.reshape(STEPS, devices, slot_count)
    slotted = recv_slot.reshape(STEPS, devices, slot_count)

    def ascend(blocks, height):
        picked = pick_columns(with_empty(blocks), senders[height])
        picked = picked.reshape(orbitals, cells, devices, devices, capacity)
        arrived = jnp.swapaxes(picked, 2, 3).reshape(orbitals, cells, devices, slot_count)
        placed = pick_columns(arrived, invert(slotted[height], per_dev))
        return placed.reshape(orbitals, cells, devices * per_dev)

    def descend(slot_blocks, height):
        blocks = slot_blocks.reshape(orbitals, cells, devices, per_dev)
        going = pick_columns(with_empty(blocks), slotted[height])
        going = going.reshape(orbitals, cells, devices, devices, capacity)
        returned = jnp.swapaxes(going, 2, 3).reshape(orbitals, cells, devices, slot_count)
        return pick_columns(returned, invert(senders[height], per_dev))

    fulls = []
    below = None
    for height in range(STEPS):
        start, number = leaf_range(height, parents)
        fresh = leaf_dev[:, :, :, start:start + number]
        if below is None:
            children = fresh
        else:
            children = jnp.concatenate([below, fresh], axis=3)
        full = analyse(ascend(children, height), filter_up, degree)
        fulls.append(full)
        below = full[:, :degree, :degree, :degree, :].reshape(orbitals, cells, devices, parents)
    pieces = [None] * STEPS
    coarse = None
    for height in reversed(range(STEPS)):
        source = fulls[height]
        if coarse is not None:
            corner = coarse.reshape(orbitals, degree, degree, degree, devices * parents)
            source = source.at[:, :degree, :degree, :degree, :].set(corner)
        local = descend(synthesise(source, filter_down, degree), height)
        if height > 0:
            coarse = local[:, :, :, :parents]
            pieces[height] = local[:, :, :, parents:]
        else:
            pieces[height] = local
    return jnp.concatenate(pieces, axis=3).reshape(orbitals, cells, total)
```

```python
import functools

import jax
import jax.numpy as jnp
from jax import lax
from jax.experimental import pallas as pl
from jax.experimental.pallas import tpu as pltpu
from jax.sharding import PartitionSpec as P

PER = 128
PARENTS = 16
DEGREE = 10
CELLS = 1000
PLANE = 100
ROWS = 32
SLOTS = 256
LIMIT = 40 * 1024 * 1024

highest = lax.Precision.HIGHEST
f32 = jnp.float32
bf16 = jnp.bfloat16
VMEM = pl.BlockSpec(memory_space=pltpu.VMEM)
SMEM = pl.BlockSpec(memory_space=pltpu.SMEM)
ANY = pl.BlockSpec(memory_space=pl.ANY)


def leaf_range(height):
    if height == 0:
        return (0, PER)
    return (PER + 7 * PARENTS * (height - 1), 7 * PARENTS)


def split(value):
    high = value.astype(bf16)
    return high, (value - high.astype(f32)).astype(bf16)


def split_outside(value):
    high = lax.reduce_precision(value, exponent_bits=8, mantissa_bits=7)
    return high.astype(bf16), (value - high).astype(bf16)


def product(left, right):
    dot = functools.partial(jnp.dot, preferred_element_type=f32)
    return dot(left[0], right[0]) + (dot(left[0], right[1]) + dot(left[1], right[0]))


def windows(chunks):
    lane = lax.broadcasted_iota(jnp.int32, (ROWS, 128), 1)
    result = []
    for i in range(DEGREE):
        first, offset = divmod(PLANE * i, 128)
        value = chunks[first]
        if offset:
            value = pltpu.roll(value, 128 - offset, 1)
            if offset + PLANE > 128:
                later = pltpu.roll(chunks[first + 1], 128 - offset, 1)
                value = jnp.where(lane < 128 - offset, value, later)
        result.append(value)
    return result


def merge(parts):
    lane = lax.broadcasted_iota(jnp.int32, (ROWS, 128), 1)
    result = []
    for part in range(8):
        value = None
        for i in range(DEGREE):
            start = PLANE * i - 128 * part
            if start >= 128 or start + PLANE <= 0:
                continue
            piece = parts[i]
            if start % 128:
                piece = pltpu.roll(piece, start % 128, 1)
            if value is None:
                value = piece
            else:
                value = jnp.where(lane < start, value, piece)
        if part == 7:
            value = jnp.where(lane < CELLS - 896, value, 0.0)
        result.append(value)
    return result


def pack_rows(rows, count, flat_ref):
    for first in range(0, count, 8):
        for n in range(2):
            for part in range(8):
                if part < 7:
                    value = rows[n, first : first + 8, 128 * part : 128 * part + 128]
                else:
                    value = rows[n, first : first + 8, 896:CELLS]
                    value = jnp.concatenate([value, jnp.zeros((8, 1024 - CELLS), f32)], axis=1)
                flat_ref[pl.ds(first * 16 + n * 8 + part, 8, stride=16), :] = value


def first_kernel(send_ref, leaves_ref, out_ref, rows, flat, sem):
    copy = pltpu.make_async_copy(leaves_ref.at[:, 0:PER, :], rows, sem)
    copy.start()
    copy.wait()
    pack_rows(rows, PER, flat)
    for slot in range(SLOTS):
        start = pl.multiple_of(jnp.minimum(send_ref[0, slot], PER - 1) * 16, 16)
        out_ref[slot] = flat[pl.ds(start, 16), :]


def rest_kernel(leaves_ref, out_ref, rows, sem):
    count = 3 * 7 * PARENTS
    copy = pltpu.make_async_copy(leaves_ref.at[:, PER : PER + count, :], rows, sem)
    copy.start()
    copy.wait()
    pack_rows(rows, count, out_ref)


def place_and_window(height, place_ref, arrived_ref, placed, high_ref, low_ref):
    for child in range(PER):
        octant, parent = (child % 8, child // 8)
        slot = place_ref[height, child]
        for n in range(2):
            value = arrived_ref[slot, n * 8 : n * 8 + 8, :]
            placed[pl.ds(octant * 8 * ROWS + n * 16 + parent, 8, stride=ROWS), :] = value
    for octant in range(8):
        chunks = [placed[(octant * 8 + part) * ROWS : (octant * 8 + part + 1) * ROWS, :] for part in range(8)]
        x, w = divmod(octant, 4)
        for i, value in enumerate(windows(chunks)):
            high, low = split(value)
            start = (x * DEGREE + i) * ROWS
            high_ref[start : start + ROWS, w * 128 : w * 128 + 128] = high
            low_ref[start : start + ROWS, w * 128 : w * 128 + 128] = low


def pair(high_ref, low_ref):
    return (high_ref[...], low_ref[...])


def up_kernel(
    height,
    place_ref,
    take_ref,
    arrived_ref,
    leaves_ref,
    plane_high,
    plane_low,
    row_high,
    row_low,
    out_ref,
    corner_ref,
    high_ref,
    low_ref,
    placed,
    blocks,
):
    place_and_window(height, place_ref, arrived_ref, placed, high_ref, low_ref)
    half = product(pair(high_ref, low_ref), pair(plane_high, plane_low))
    corner = product(pair(row_high, row_low), split(half))
    corner_ref[...] = corner
    parts = [corner[i * ROWS : (i + 1) * ROWS, :] for i in range(DEGREE)]
    for part, value in enumerate(merge(parts)):
        for n in range(2):
            blocks[pl.ds(n * 8 + part, 16, stride=16), :] = value[n * 16 : n * 16 + 16]
    for child in range(PER):
        slot = take_ref[height + 1, child]
        if child < PARENTS:
            out_ref[slot] = blocks[child * 16 : child * 16 + 16, :]
        else:
            start = (leaf_range(height + 1)[0] - PER + child - PARENTS) * 16
            out_ref[slot] = leaves_ref[start : start + 16, :]


def emit(height, place_ref, refined, blocks, out_ref):
    for octant in range(8):
        x, w = divmod(octant, 4)
        parts = []
        for i in range(DEGREE):
            start = (x * DEGREE + i) * ROWS
            parts.append(refined[start : start + ROWS, w * 128 : w * 128 + 128])
        for part, value in enumerate(merge(parts)):
            for n in range(2):
                blocks[pl.ds(octant * 16 + n * 8 + part, 16, stride=128), :] = value[n * 16 : n * 16 + 16]
    for child in range(PER):
        out_ref[place_ref[height, child]] = blocks[child * 16 : child * 16 + 16, :]


def top_kernel(
    height, place_ref, arrived_ref, plane_high, plane_low, row_high, row_low, out_ref, placed, high_ref, low_ref, refined, blocks
):
    place_and_window(height, place_ref, arrived_ref, placed, high_ref, low_ref)
    half = product(pair(high_ref, low_ref), pair(plane_high, plane_low))
    refined[...] = product(pair(row_high, row_low), split(half))
    emit(height, place_ref, refined, blocks, out_ref)


def base_kernel(high_ref, low_ref, plane_high, plane_low, row_high, row_low, out_ref):
    half = product(pair(high_ref, low_ref), pair(plane_high, plane_low))
    out_ref[...] = product(pair(row_high, row_low), split(half))


def down_kernel(
    height,
    take_ref,
    place_ref,
    returned_ref,
    corner_ref,
    base_ref,
    plane_high,
    plane_low,
    row_high,
    row_low,
    out_ref,
    placed,
    delta,
    refined,
    blocks,
):
    for child in range(PARENTS):
        slot = take_ref[height + 1, child]
        for n in range(2):
            placed[pl.ds(n * 16 + child, 8, stride=ROWS), :] = returned_ref[slot, n * 8 : n * 8 + 8, :]
    lane = lax.broadcasted_iota(jnp.int32, (ROWS, 128), 1)
    chunks = [placed[part * ROWS : (part + 1) * ROWS, :] for part in range(8)]
    for i, value in enumerate(windows(chunks)):
        change = value - corner_ref[i * ROWS : (i + 1) * ROWS, :]
        delta[i * ROWS : (i + 1) * ROWS, :] = jnp.where(lane < PLANE, change, 0.0)
    half = product(split(delta[...]), pair(plane_high, plane_low))
    refined[...] = base_ref[...] + product(pair(row_high, row_low), split(half))
    emit(height, place_ref, refined, blocks, out_ref)


def store_kernel(height, take_ref, returned_ref, *rest):
    out_ref, flat, rows, sem = rest[-4:]
    start, number = leaf_range(height)
    skip = PER - number
    for child in range(number):
        slot = take_ref[height, child + skip]
        flat[child * 16 : child * 16 + 16, :] = returned_ref[slot]
    for first in range(0, number, 8):
        for n in range(2):
            for part in range(8):
                value = flat[pl.ds(first * 16 + n * 8 + part, 8, stride=16), :]
                if part < 7:
                    rows[n, first : first + 8, 128 * part : 128 * part + 128] = value
                else:
                    rows[n, first : first + 8, 896:CELLS] = value[:, : CELLS - 896]
    copy = pltpu.make_async_copy(rows, out_ref.at[:, start : start + number, :], sem)
    copy.start()
    copy.wait()


def shape(*dims, dtype=f32):
    return jax.ShapeDtypeStruct(dims, dtype)


def call(kernel, out_shape, in_specs, out_specs, scratch, operands, flops, name, aliases=None):
    moved = sum(4 * one.size for one in operands)
    return pl.pallas_call(
        kernel,
        out_shape=out_shape,
        in_specs=in_specs,
        out_specs=out_specs,
        scratch_shapes=scratch,
        input_output_aliases=aliases or {},
        compiler_params=pltpu.CompilerParams(vmem_limit_bytes=LIMIT),
        cost_estimate=pl.CostEstimate(flops=flops, bytes_accessed=moved, transcendentals=0),
        name=name,
    )(*operands)


def lanes(matrix, axis, groups):
    dims = list(matrix.shape)
    dims[axis : axis + 1] = [groups, PLANE]
    wide = matrix.reshape(dims)
    pads = [(0, 0)] * len(dims)
    pads[axis + 1] = (0, 128 - PLANE)
    wide = jnp.pad(wide, pads)
    dims = list(matrix.shape)
    dims[axis] = groups * 128
    return wide.reshape(dims)


def planes(filters, outs, ins):
    o, i = (outs // DEGREE, ins // DEGREE)
    part = filters[:outs, :ins].reshape(o, DEGREE, i, DEGREE)
    both = jnp.einsum("YJyj,ZKzk->yzjkYZJK", part, part, precision=highest)
    both = both.reshape(i * i * PLANE, o * o * PLANE)
    return split_outside(lanes(lanes(both, 0, i * i), 1, o * o))


def spread(filters, outs, ins):
    part = filters[:outs, :ins]
    eye = jnp.eye(ROWS, dtype=f32)
    return split_outside((part[:, None, :, None] * eye[None, :, None, :]).reshape(outs * ROWS, ins * ROWS))


def invert(mapping):
    match = mapping[:, None, :] == jnp.arange(PER, dtype=jnp.int32)[None, :, None]
    return jnp.sum(jnp.where(match, jnp.arange(mapping.shape[1], dtype=jnp.int32)[None, None, :], 0), axis=2)


def exchange(blocks):
    return lax.all_to_all(blocks, "dev", split_axis=0, concat_axis=0, tiled=True)


def transform(leaves, send_slot, recv_slot, filter_up, filter_down):
    levels = send_slot.shape[0]
    rows = jnp.swapaxes(leaves, 1, 2)
    slots = shape(SLOTS, 16, 128)
    flat = lambda count: pltpu.VMEM((count * 16, 128), f32)
    going = call(
        first_kernel,
        slots,
        [SMEM, ANY],
        VMEM,
        [pltpu.VMEM((2, PER, CELLS), f32), flat(PER), pltpu.SemaphoreType.DMA],
        (send_slot, rows),
        0,
        "pack_first",
    )
    arrived = exchange(going)
    fresh = call(
        rest_kernel,
        shape(336 * 16, 128),
        [ANY],
        VMEM,
        [pltpu.VMEM((2, 336, CELLS), f32), pltpu.SemaphoreType.DMA],
        (rows,),
        0,
        "pack_rest",
    )
    place = invert(recv_slot)
    take = invert(send_slot)
    both = jnp.dot(filter_down, filter_up, precision=highest)
    up_plane, up_row = (planes(filter_up, 10, 20), spread(filter_up, 10, 20))
    both_plane, both_row = (planes(both, 20, 20), spread(both, 20, 20))
    down_plane, down_row = (planes(filter_down, 20, 10), spread(filter_down, 20, 10))
    wide = (640, 512)
    placed = pltpu.VMEM((8 * 8 * ROWS, 128), f32)
    corners = []
    bases = []
    for height in range(levels - 1):
        going, corner, high, low = call(
            functools.partial(up_kernel, height),
            (slots, shape(320, 128), shape(*wide, dtype=bf16), shape(*wide, dtype=bf16)),
            [SMEM, SMEM] + [VMEM] * 6,
            (VMEM,) * 4,
            [placed, flat(PARENTS)],
            (place, take, arrived, fresh) + up_plane + up_row,
            600_000_000,
            "up",
        )
        arrived = exchange(going)
        corners.append(corner)
        bases.append(
            call(
                base_kernel,
                shape(*wide),
                [VMEM] * 6,
                VMEM,
                [],
                (high, low) + both_plane + both_row,
                2_400_000_000,
                "base",
            )
        )
    height = levels - 1
    going = call(
        functools.partial(top_kernel, height),
        slots,
        [SMEM] + [VMEM] * 5,
        VMEM,
        [placed, pltpu.VMEM(wide, bf16), pltpu.VMEM(wide, bf16), pltpu.VMEM(wide, f32), flat(PER)],
        (place, arrived) + both_plane + both_row,
        2_400_000_000,
        "top",
    )
    result = None
    while True:
        returned = exchange(going)
        start, number = leaf_range(height)
        final = shape(2, PER + 336, CELLS)
        scratch = [flat(number), pltpu.VMEM((2, number, CELLS), f32), pltpu.SemaphoreType.DMA]
        if result is None:
            result = call(functools.partial(store_kernel, height), final, [SMEM, VMEM], ANY, scratch, (take, returned), 0, "store")
        else:
            result = call(
                functools.partial(store_kernel, height),
                final,
                [SMEM, VMEM, ANY],
                ANY,
                scratch,
                (take, returned, result),
                0,
                "store",
                {2: 0},
            )
        if height == 0:
            break
        height -= 1
        going = call(
            functools.partial(down_kernel, height),
            slots,
            [SMEM, SMEM] + [VMEM] * 7,
            VMEM,
            [pltpu.VMEM((8 * ROWS, 128), f32), pltpu.VMEM((320, 128), f32), pltpu.VMEM(wide, f32), flat(PER)],
            (take, place, returned, corners[height], bases[height]) + down_plane + down_row,
            800_000_000,
            "down",
        )
    return jnp.swapaxes(result, 1, 2)


def solution(mesh):
    in_specs = (P(None, None, "dev"), P(None, "dev"), P(None, "dev"), P(), P())
    out_specs = P(None, None, "dev")
    return jax.shard_map(transform, mesh=mesh, in_specs=in_specs, out_specs=out_specs, check_vma=False)
```

```python
import functools

import jax
import jax.numpy as jnp
from jax import lax
from jax.experimental import pallas as pl
from jax.experimental.pallas import tpu as pltpu
from jax.sharding import PartitionSpec as P

PER = 128
PARENTS = 16
DEGREE = 10
CELLS = 1000
PLANE = 100
ROWS = 32
SLOTS = 256
LIMIT = 32 * 1024 * 1024
TAKE = 0
PLACE = 4

highest = lax.Precision.HIGHEST
f32 = jnp.float32
bf16 = jnp.bfloat16
VMEM = pl.BlockSpec(memory_space=pltpu.VMEM)
SMEM = pl.BlockSpec(memory_space=pltpu.SMEM)
HBM = pl.BlockSpec(memory_space=pltpu.HBM)
DMA = pltpu.SemaphoreType.DMA


def leaf_range(height):
    if height == 0:
        return (0, PER)
    return (PER + 7 * PARENTS * (height - 1), 7 * PARENTS)


def split(value):
    high = value.astype(bf16)
    return high, (value - high.astype(f32)).astype(bf16)


def product(left, right):
    dot = functools.partial(jnp.dot, preferred_element_type=f32)
    return dot(left[0], right[0]) + (dot(left[0], right[1]) + dot(left[1], right[0]))


def windows(chunks):
    lane = lax.broadcasted_iota(jnp.int32, (ROWS, 128), 1)
    result = []
    for i in range(DEGREE):
        first, offset = divmod(PLANE * i, 128)
        value = chunks[first]
        if offset:
            value = pltpu.roll(value, 128 - offset, 1)
            if offset + PLANE > 128:
                later = pltpu.roll(chunks[first + 1], 128 - offset, 1)
                value = jnp.where(lane < 128 - offset, value, later)
        result.append(value)
    return result


def merge(parts):
    lane = lax.broadcasted_iota(jnp.int32, (ROWS, 128), 1)
    result = []
    for part in range(8):
        value = None
        for i in range(DEGREE):
            start = PLANE * i - 128 * part
            if start >= 128 or start + PLANE <= 0:
                continue
            piece = parts[i]
            if start % 128:
                piece = pltpu.roll(piece, start % 128, 1)
            if value is None:
                value = piece
            else:
                value = jnp.where(lane < start, value, piece)
        if part == 7:
            value = jnp.where(lane < CELLS - 896, value, 0.0)
        result.append(value)
    return result


def pack_rows(rows, start, count, flat_ref):
    for first in range(start, start + count, 8):
        for n in range(2):
            for part in range(8):
                if part < 7:
                    value = rows[n, first : first + 8, 128 * part : 128 * part + 128]
                else:
                    value = rows[n, first : first + 8, 896:CELLS]
                    value = jnp.concatenate([value, jnp.zeros((8, 1024 - CELLS), f32)], axis=1)
                flat_ref[pl.ds(first * 16 + n * 8 + part, 8, stride=16), :] = value


def block(flat, index):
    return flat[index * 16 : index * 16 + 16, :]


def fetch(pairs, sems):
    copies = [pltpu.make_async_copy(source, target, sems.at[i]) for i, (source, target) in enumerate(pairs)]
    for copy in copies:
        copy.start()
    return copies


def first_kernel(send_ref, leaves_ref, out_ref, send, rows, flat, sems):
    quarter = PER // 4
    pairs = [(send_ref, send)]
    for i in range(4):
        span = slice(i * quarter, (i + 1) * quarter)
        pairs.append((leaves_ref.at[:, span, :], rows.at[:, span, :]))
    copies = fetch(pairs, sems)
    for i in range(4):
        copies[i + 1].wait()
        pack_rows(rows, i * quarter, quarter, flat)
    copies[0].wait()
    for slot in range(SLOTS):
        start = pl.multiple_of(jnp.minimum(send[0, slot], PER - 1) * 16, 16)
        out_ref[slot] = flat[pl.ds(start, 16), :]


def rest_kernel(maps, leaves_ref, out_ref, rows, flat, filled, sems):
    number = 7 * PARENTS
    pairs = []
    for i in range(3):
        span = slice(i * number, (i + 1) * number)
        pairs.append((leaves_ref.at[:, PER + i * number : PER + (i + 1) * number, :], rows.at[:, span, :]))
    copies = fetch(pairs, sems)
    outs = []
    for i in range(3):
        copies[i].wait()
        pack_rows(rows, i * number, number, flat)
        for child in range(number):
            filled[i, maps[TAKE + i + 1, PARENTS + child]] = block(flat, i * number + child)
        out = pltpu.make_async_copy(filled.at[i], out_ref.at[i], sems.at[3 + i])
        out.start()
        outs.append(out)
    for out in outs:
        out.wait()


def one_hot(dims, axis, index):
    return (lax.broadcasted_iota(jnp.int32, dims, axis) == index).astype(f32)


def plane_index(dims, axis, size):
    position = lax.broadcasted_iota(jnp.int32, dims, axis)
    w, cell = (position >> 7, position & 127)
    j = (cell * 205) >> 11
    k = cell - DEGREE * j
    if size > DEGREE:
        j, k = (j + DEGREE * (w >> 1), k + DEGREE * (w & 1))
    dead = cell >= PLANE
    return jnp.where(dead, -1, j), jnp.where(dead, -1, k)


def exact(left, right, dims=((1,), (0,))):
    return lax.dot_general(left, right, (dims, ((), ())), precision=highest, preferred_element_type=f32)


def planes(filters, outs, ins):
    rows, columns = ((ins // DEGREE) ** 2 * 128, (outs // DEGREE) ** 2 * 128)
    factors = []
    for left, right in zip(plane_index((rows, ins), 0, ins), plane_index((outs, columns), 1, outs)):
        half = exact(one_hot((rows, ins), 1, left), filters, ((1,), (1,)))
        factors.append(exact(half, one_hot((outs, columns), 0, right)))
    return split(factors[0] * factors[1])


def spread(filters, outs, ins):
    rows, columns = (outs * ROWS, ins * ROWS)
    left = one_hot((rows, outs), 1, lax.broadcasted_iota(jnp.int32, (rows, outs), 0) >> 5)
    right = one_hot((ins, columns), 0, lax.broadcasted_iota(jnp.int32, (ins, columns), 1) >> 5)
    row = lax.broadcasted_iota(jnp.int32, (rows, columns), 0) & (ROWS - 1)
    column = lax.broadcasted_iota(jnp.int32, (rows, columns), 1) & (ROWS - 1)
    return split(jnp.where(row == column, exact(exact(left, filters), right), 0.0))


def weight_kernel(up_ref, down_ref, *out_refs):
    both = exact(down_ref[...], up_ref[...])
    up, down = (up_ref[0:DEGREE, :], down_ref[:, 0:DEGREE])
    sizes = ((up, 10, 20), (both, 20, 20), (down, 20, 10))
    for i, (filters, outs, ins) in enumerate(sizes):
        values = planes(filters, outs, ins) + spread(filters, outs, ins)
        for j, value in enumerate(values):
            out_refs[4 * i + j][...] = value


def window_octants(placed, high_ref, low_ref):
    for octant in range(8):
        chunks = [placed[(octant * 8 + part) * ROWS : (octant * 8 + part + 1) * ROWS, :] for part in range(8)]
        x, w = divmod(octant, 4)
        for i, value in enumerate(windows(chunks)):
            high, low = split(value)
            start = (x * DEGREE + i) * ROWS
            high_ref[start : start + ROWS, w * 128 : w * 128 + 128] = high
            low_ref[start : start + ROWS, w * 128 : w * 128 + 128] = low


def place_children(height, maps, arrived_ref, placed):
    for child in range(PER):
        octant, parent = (child % 8, child // 8)
        slot = maps[PLACE + height, child]
        for n in range(2):
            value = arrived_ref[slot, n * 8 : n * 8 + 8, :]
            placed[pl.ds(octant * 8 * ROWS + n * 16 + parent, 8, stride=ROWS), :] = value


def filtered(data, weights):
    half = product(data, (weights[0][...], weights[1][...]))
    return product((weights[2][...], weights[3][...]), split(half))


def up_kernel(height, arrived_ref, maps_ref, filled_ref, w0, w1, w2, w3, out_ref, corner_ref, high_ref, low_ref, *scratch):
    maps, corner, high, low, placed, blocks, v0, v1, v2, v3, sems = scratch
    weights = (v0, v1, v2, v3)
    pairs = [(maps_ref, maps), (filled_ref.at[height], out_ref)] + list(zip((w0, w1, w2, w3), weights))
    copies = fetch(pairs, sems)
    copies[0].wait()
    place_children(height, maps, arrived_ref, placed)
    window_octants(placed, high, low)
    outs = [pltpu.make_async_copy(high, high_ref, sems.at[6]), pltpu.make_async_copy(low, low_ref, sems.at[7])]
    for out in outs:
        out.start()
    for copy in copies[2:]:
        copy.wait()
    value = filtered((high[...], low[...]), weights)
    corner[...] = value
    out = pltpu.make_async_copy(corner, corner_ref, sems.at[8])
    out.start()
    outs.append(out)
    parts = [value[i * ROWS : (i + 1) * ROWS, :] for i in range(DEGREE)]
    for part, chunk in enumerate(merge(parts)):
        for n in range(2):
            blocks[pl.ds(n * 8 + part, 16, stride=16), :] = chunk[n * 16 : n * 16 + 16]
    copies[1].wait()
    for child in range(PARENTS):
        out_ref[maps[TAKE + height + 1, child]] = block(blocks, child)
    for out in outs:
        out.wait()


def emit(height, maps, refined, blocks, out_ref):
    for octant in range(8):
        x, w = divmod(octant, 4)
        parts = []
        for i in range(DEGREE):
            start = (x * DEGREE + i) * ROWS
            parts.append(refined[start : start + ROWS, w * 128 : w * 128 + 128])
        for part, value in enumerate(merge(parts)):
            for n in range(2):
                blocks[pl.ds(octant * 16 + n * 8 + part, 16, stride=128), :] = value[n * 16 : n * 16 + 16]
    for child in range(PER):
        out_ref[maps[PLACE + height, child]] = block(blocks, child)


def top_kernel(height, arrived_ref, maps_ref, w0, w1, w2, w3, out_ref, *scratch):
    maps, high, low, placed, refined, blocks, v0, v1, v2, v3, sems = scratch
    weights = (v0, v1, v2, v3)
    copies = fetch([(maps_ref, maps)] + list(zip((w0, w1, w2, w3), weights)), sems)
    copies[0].wait()
    place_children(height, maps, arrived_ref, placed)
    window_octants(placed, high, low)
    for copy in copies[1:]:
        copy.wait()
    refined[...] = filtered((high[...], low[...]), weights)
    emit(height, maps, refined, blocks, out_ref)


def base_kernel(*refs):
    sources, w, out_ref = (refs[0:6], refs[6:10], refs[10])
    data, weights, refined, sems = (refs[11:17], refs[17:21], refs[21], refs[22])
    copies = fetch(list(zip(tuple(w) + tuple(sources), tuple(weights) + tuple(data))), sems)
    for copy in copies[:4]:
        copy.wait()
    outs = []
    for i in range(3):
        copies[4 + 2 * i].wait()
        copies[5 + 2 * i].wait()
        refined[i] = filtered((data[2 * i][...], data[2 * i + 1][...]), weights)
        out = pltpu.make_async_copy(refined.at[i], out_ref.at[i], sems.at[10 + i])
        out.start()
        outs.append(out)
    for out in outs:
        out.wait()


def down_kernel(height, returned_ref, maps_ref, corner_ref, base_ref, w0, w1, w2, w3, out_ref, *scratch):
    maps, corner, base, placed, delta, refined, blocks, v0, v1, v2, v3, sems = scratch
    weights = (v0, v1, v2, v3)
    pairs = [(maps_ref, maps), (corner_ref, corner)] + list(zip((w0, w1, w2, w3), weights)) + [(base_ref.at[height], base)]
    copies = fetch(pairs, sems)
    copies[0].wait()
    for child in range(PARENTS):
        slot = maps[TAKE + height + 1, child]
        for n in range(2):
            placed[pl.ds(n * 16 + child, 8, stride=ROWS), :] = returned_ref[slot, n * 8 : n * 8 + 8, :]
    lane = lax.broadcasted_iota(jnp.int32, (ROWS, 128), 1)
    chunks = [placed[part * ROWS : (part + 1) * ROWS, :] for part in range(8)]
    copies[1].wait()
    for i, value in enumerate(windows(chunks)):
        change = value - corner[i * ROWS : (i + 1) * ROWS, :]
        delta[i * ROWS : (i + 1) * ROWS, :] = jnp.where(lane < PLANE, change, 0.0)
    for copy in copies[2:]:
        copy.wait()
    refined[...] = base[...] + filtered(split(delta[...]), weights)
    emit(height, maps, refined, blocks, out_ref)


def store_kernel(height, returned_ref, maps_ref, *rest):
    out_ref, maps, flat, rows, sems = rest[-5:]
    start, number = leaf_range(height)
    skip = PER - number
    copy = fetch([(maps_ref, maps)], sems)[0]
    copy.wait()
    outs = []
    step = 16
    for base in range(0, number, step):
        for child in range(base, base + step):
            flat[child * 16 : child * 16 + 16, :] = returned_ref[maps[TAKE + height, child + skip]]
        for first in range(base, base + step, 8):
            for n in range(2):
                for part in range(8):
                    value = flat[pl.ds(first * 16 + n * 8 + part, 8, stride=16), :]
                    if part < 7:
                        rows[n, first : first + 8, 128 * part : 128 * part + 128] = value
                    else:
                        rows[n, first : first + 8, 896:CELLS] = value[:, : CELLS - 896]
        span = slice(base, base + step)
        target = out_ref.at[:, start + base : start + base + step, :]
        out = pltpu.make_async_copy(rows.at[:, span, :], target, sems.at[1 + base // step])
        out.start()
        outs.append(out)
    for out in outs:
        out.wait()


def shape(*dims, dtype=f32):
    return jax.ShapeDtypeStruct(dims, dtype)


def call(kernel, out_shape, in_specs, out_specs, scratch, operands, flops, name, aliases=None):
    moved = sum(4 * one.size for one in operands)
    return pl.pallas_call(
        kernel,
        out_shape=out_shape,
        in_specs=in_specs,
        out_specs=out_specs,
        scratch_shapes=scratch,
        input_output_aliases=aliases or {},
        compiler_params=pltpu.CompilerParams(vmem_limit_bytes=LIMIT),
        cost_estimate=pl.CostEstimate(flops=flops, bytes_accessed=moved, transcendentals=0),
        name=name,
    )(*operands)


def invert(mapping):
    match = mapping[:, None, :] == jnp.arange(PER, dtype=jnp.int32)[None, :, None]
    return jnp.sum(jnp.where(match, jnp.arange(mapping.shape[1], dtype=jnp.int32)[None, None, :], 0), axis=2)


def exchange(blocks):
    return lax.all_to_all(blocks, "dev", split_axis=0, concat_axis=0, tiled=True)


def transform(leaves, send_slot, recv_slot, filter_up, filter_down):
    levels = send_slot.shape[0]
    rows = jnp.swapaxes(leaves, 1, 2)
    slots = shape(SLOTS, 16, 128)
    flat = lambda count: pltpu.VMEM((count * 16, 128), f32)
    sizes = lambda weights: [pltpu.VMEM(one.shape, bf16) for one in weights]
    going = call(
        first_kernel,
        slots,
        [HBM, HBM],
        VMEM,
        [pltpu.SMEM(send_slot.shape, jnp.int32), pltpu.VMEM((2, PER, CELLS), f32), flat(PER), DMA((5,))],
        (send_slot, rows),
        0,
        "pack_first",
    )
    arrived = exchange(going)
    maps = jnp.concatenate([invert(send_slot), invert(recv_slot)], axis=0)
    maps_smem = pltpu.SMEM(maps.shape, jnp.int32)
    filled = call(
        rest_kernel,
        shape(3, SLOTS, 16, 128),
        [SMEM, HBM],
        HBM,
        [pltpu.VMEM((2, 336, CELLS), f32), flat(336), pltpu.VMEM((3, SLOTS, 16, 128), f32), DMA((6,))],
        (maps, rows),
        0,
        "pack_rest",
    )
    halves = lambda *dims: [shape(*dims, dtype=bf16)] * 2
    pieces = halves(512, 128) + halves(320, 640) + halves(512, 512) + halves(640, 640) + halves(128, 512) + halves(640, 320)
    weights = call(weight_kernel, pieces, [VMEM, VMEM], [VMEM] * 12, [], (filter_up, filter_down), 50_000_000, "weights")
    weights = tuple(weights)
    up, both, down = (weights[0:4], weights[4:8], weights[8:12])
    wide = (640, 512)
    placed = pltpu.VMEM((8 * 8 * ROWS, 128), f32)
    split_wide = [pltpu.VMEM(wide, bf16)] * 2
    corners = []
    splits = []
    for height in range(levels - 1):
        going, corner, high, low = call(
            functools.partial(up_kernel, height),
            (slots, shape(320, 128), shape(*wide, dtype=bf16), shape(*wide, dtype=bf16)),
            [VMEM] + [HBM] * 6,
            (VMEM, HBM, HBM, HBM),
            [maps_smem, pltpu.VMEM((320, 128), f32)] + split_wide + [placed, flat(PARENTS)] + sizes(up) + [DMA((9,))],
            (arrived, maps, filled) + up,
            600_000_000,
            "up",
        )
        arrived = exchange(going)
        corners.append(corner)
        splits += [high, low]
    bases = call(
        base_kernel,
        shape(3, *wide),
        [HBM] * 10,
        HBM,
        split_wide * 3 + sizes(both) + [pltpu.VMEM((3, *wide), f32), DMA((13,))],
        tuple(splits) + both,
        7_200_000_000,
        "base",
    )
    height = levels - 1
    going = call(
        functools.partial(top_kernel, height),
        slots,
        [VMEM] + [HBM] * 5,
        VMEM,
        [maps_smem] + split_wide + [placed, pltpu.VMEM(wide, f32), flat(PER)] + sizes(both) + [DMA((5,))],
        (arrived, maps) + both,
        2_400_000_000,
        "top",
    )
    result = None
    while True:
        returned = exchange(going)
        start, number = leaf_range(height)
        final = shape(2, PER + 336, CELLS)
        scratch = [maps_smem, flat(number), pltpu.VMEM((2, number, CELLS), f32), DMA((1 + number // 16,))]
        kernel = functools.partial(store_kernel, height)
        if result is None:
            result = call(kernel, final, [VMEM, HBM], HBM, scratch, (returned, maps), 0, "store")
        else:
            result = call(kernel, final, [VMEM, HBM, HBM], HBM, scratch, (returned, maps, result), 0, "store", {2: 0})
        if height == 0:
            break
        height -= 1
        going = call(
            functools.partial(down_kernel, height),
            slots,
            [VMEM] + [HBM] * 7,
            VMEM,
            [maps_smem, pltpu.VMEM((320, 128), f32), pltpu.VMEM(wide, f32), pltpu.VMEM((8 * ROWS, 128), f32)]
            + [pltpu.VMEM((320, 128), f32), pltpu.VMEM(wide, f32), flat(PER)]
            + sizes(down)
            + [DMA((7,))],
            (returned, maps, corners[height], bases) + down,
            800_000_000,
            "down",
        )
    return jnp.swapaxes(result, 1, 2)


def solution(mesh):
    in_specs = (P(None, None, "dev"), P(None, "dev"), P(None, "dev"), P(), P())
    out_specs = P(None, None, "dev")
    return jax.shard_map(transform, mesh=mesh, in_specs=in_specs, out_specs=out_specs, check_vma=False)
```

```python
import functools

import jax
import jax.numpy as jnp
from jax import lax
from jax.experimental import pallas as pl
from jax.experimental.pallas import tpu as pltpu
from jax.sharding import PartitionSpec as P

PER = 128
PARENTS = 16
DEGREE = 10
CELLS = 1000
PLANE = 100
ROWS = 32
SLOTS = 256
LIMIT = 42_000_000
FULL = 63_400_000
UP_ROW, BOTH_ROW, DOWN_ROW, PLANE_ROW, DOWN_PLANE, SPLIT = (0, 640, 1920, 3200, 4224, 4480)
BANK = 16384
CORNER = 20
TAKE = 0
PLACE = 4

highest = lax.Precision.HIGHEST
f32 = jnp.float32
bf16 = jnp.bfloat16
VMEM = pl.BlockSpec(memory_space=pltpu.VMEM)
SMEM = pl.BlockSpec(memory_space=pltpu.SMEM)
HBM = pl.BlockSpec(memory_space=pltpu.HBM)
DMA = pltpu.SemaphoreType.DMA


def leaf_range(height):
    if height == 0:
        return (0, PER)
    return (PER + 7 * PARENTS * (height - 1), 7 * PARENTS)


def split(value):
    high = value.astype(bf16)
    return high, (value - high.astype(f32)).astype(bf16)


def product(left, right):
    dot = functools.partial(jnp.dot, preferred_element_type=f32)
    return dot(left[0], right[0]) + (dot(left[0], right[1]) + dot(left[1], right[0]))


def windows(chunks):
    lane = lax.broadcasted_iota(jnp.int32, (ROWS, 128), 1)
    result = []
    for i in range(DEGREE):
        first, offset = divmod(PLANE * i, 128)
        value = chunks[first]
        if offset:
            value = pltpu.roll(value, 128 - offset, 1)
            if offset + PLANE > 128:
                later = pltpu.roll(chunks[first + 1], 128 - offset, 1)
                value = jnp.where(lane < 128 - offset, value, later)
        result.append(value)
    return result


def merge(parts):
    lane = lax.broadcasted_iota(jnp.int32, (ROWS, 128), 1)
    result = []
    for part in range(8):
        value = None
        for i in range(DEGREE):
            start = PLANE * i - 128 * part
            if start >= 128 or start + PLANE <= 0:
                continue
            piece = parts[i]
            if start % 128:
                piece = pltpu.roll(piece, start % 128, 1)
            if value is None:
                value = piece
            else:
                value = jnp.where(lane < start, value, piece)
        if part == 7:
            value = jnp.where(lane < CELLS - 896, value, 0.0)
        result.append(value)
    return result


def pack_rows(rows, start, count, flat_ref):
    for first in range(start, start + count, 8):
        for n in range(2):
            for part in range(8):
                if part < 7:
                    value = rows[n, first : first + 8, 128 * part : 128 * part + 128]
                else:
                    value = rows[n, first : first + 8, 896:CELLS]
                    value = jnp.concatenate([value, jnp.zeros((8, 1024 - CELLS), f32)], axis=1)
                flat_ref[pl.ds(first * 16 + n * 8 + part, 8, stride=16), :] = value


def block(flat, index):
    return flat[index * 16 : index * 16 + 16, :]


def fetch(pairs, sems):
    copies = [pltpu.make_async_copy(source, target, sems.at[i]) for i, (source, target) in enumerate(pairs)]
    for copy in copies:
        copy.start()
    return copies


def first_kernel(send_ref, leaves_ref, out_ref, send, rows, flat, sems):
    quarter = PER // 4
    pairs = [(send_ref, send)]
    for i in range(4):
        span = slice(i * quarter, (i + 1) * quarter)
        pairs.append((leaves_ref.at[:, span, :], rows.at[:, span, :]))
    copies = fetch(pairs, sems)
    for i in range(4):
        copies[i + 1].wait()
        pack_rows(rows, i * quarter, quarter, flat)
    copies[0].wait()
    for slot in range(SLOTS):
        start = pl.multiple_of(jnp.minimum(send[0, slot], PER - 1) * 16, 16)
        out_ref[slot] = flat[pl.ds(start, 16), :]


def rest_kernel(maps, leaves_ref, out_ref, rows, flat, filled, sems):
    number = 7 * PARENTS
    pairs = []
    for i in range(3):
        span = slice(i * number, (i + 1) * number)
        pairs.append((leaves_ref.at[:, PER + i * number : PER + (i + 1) * number, :], rows.at[:, span, :]))
    copies = fetch(pairs, sems)
    outs = []
    for i in range(3):
        copies[i].wait()
        pack_rows(rows, i * number, number, flat)
        for child in range(number):
            filled[i, maps[TAKE + i + 1, PARENTS + child]] = block(flat, i * number + child)
        out = pltpu.make_async_copy(filled.at[i], out_ref.at[i, 0:SLOTS], sems.at[3 + i])
        out.start()
        outs.append(out)
    for out in outs:
        out.wait()


def one_hot(dims, axis, index):
    return (lax.broadcasted_iota(jnp.int32, dims, axis) == index).astype(f32)


def plane_index(dims, axis, size):
    position = lax.broadcasted_iota(jnp.int32, dims, axis)
    w, cell = (position >> 7, position & 127)
    j = (cell * 205) >> 11
    k = cell - DEGREE * j
    if size > DEGREE:
        j, k = (j + DEGREE * (w >> 1), k + DEGREE * (w & 1))
    dead = cell >= PLANE
    return jnp.where(dead, -1, j), jnp.where(dead, -1, k)


def exact(left, right, dims=((1,), (0,))):
    return lax.dot_general(left, right, (dims, ((), ())), precision=highest, preferred_element_type=f32)


def planes(filters, outs, ins):
    rows, columns = ((ins // DEGREE) ** 2 * 128, (outs // DEGREE) ** 2 * 128)
    factors = []
    for left, right in zip(plane_index((rows, ins), 0, ins), plane_index((outs, columns), 1, outs)):
        half = exact(one_hot((rows, ins), 1, left), filters, ((1,), (1,)))
        factors.append(exact(half, one_hot((outs, columns), 0, right)))
    return split(factors[0] * factors[1])


def spread(filters, outs, ins):
    rows, columns = (outs * ROWS, ins * ROWS)
    left = one_hot((rows, outs), 1, lax.broadcasted_iota(jnp.int32, (rows, outs), 0) >> 5)
    right = one_hot((ins, columns), 0, lax.broadcasted_iota(jnp.int32, (ins, columns), 1) >> 5)
    row = lax.broadcasted_iota(jnp.int32, (rows, columns), 0) & (ROWS - 1)
    column = lax.broadcasted_iota(jnp.int32, (rows, columns), 1) & (ROWS - 1)
    return split(jnp.where(row == column, exact(exact(left, filters), right), 0.0))


def weight_kernel(up_ref, down_ref, bank_ref, bank, sem):
    both = exact(down_ref[...], up_ref[...])
    up, down = (up_ref[0:DEGREE, :], down_ref[:, 0:DEGREE])
    for i in range(2):
        bank[PLANE_ROW + 512 * i : PLANE_ROW + 512 * (i + 1), 512:640] = planes(up, 10, 20)[i]
        bank[PLANE_ROW + 512 * i : PLANE_ROW + 512 * (i + 1), 0:512] = planes(both, 20, 20)[i]
        bank[DOWN_PLANE + 128 * i : DOWN_PLANE + 128 * (i + 1), 0:512] = planes(down, 20, 10)[i]
        bank[UP_ROW + 320 * i : UP_ROW + 320 * (i + 1), :] = spread(up, 10, 20)[i]
        bank[BOTH_ROW + 640 * i : BOTH_ROW + 640 * (i + 1), :] = spread(both, 20, 20)[i]
        bank[DOWN_ROW + 640 * i : DOWN_ROW + 640 * (i + 1), 0:320] = spread(down, 20, 10)[i]
    copy = pltpu.make_async_copy(bank, bank_ref.at[0:SPLIT, :], sem)
    copy.start()
    copy.wait()


def section(bank_ref, start, rows, first, columns):
    return [bank_ref.at[start + i * rows : start + (i + 1) * rows, first : first + columns] for i in range(2)]


def up_weights(bank_ref):
    return section(bank_ref, PLANE_ROW, 512, 512, 128) + section(bank_ref, UP_ROW, 320, 0, 640)


def both_weights(bank_ref):
    return section(bank_ref, PLANE_ROW, 512, 0, 512) + section(bank_ref, BOTH_ROW, 640, 0, 640)


def down_weights(bank_ref):
    return section(bank_ref, DOWN_PLANE, 128, 0, 512) + section(bank_ref, DOWN_ROW, 640, 0, 384)


def split_children(bank_ref, height):
    return section(bank_ref, SPLIT + 1280 * height, 640, 0, 512)


def window_octants(placed, high_ref, low_ref):
    for octant in range(8):
        chunks = [placed[(octant * 8 + part) * ROWS : (octant * 8 + part + 1) * ROWS, :] for part in range(8)]
        x, w = divmod(octant, 4)
        for i, value in enumerate(windows(chunks)):
            high, low = split(value)
            start = (x * DEGREE + i) * ROWS
            high_ref[start : start + ROWS, w * 128 : w * 128 + 128] = high
            low_ref[start : start + ROWS, w * 128 : w * 128 + 128] = low


def place_children(height, maps, arrived_ref, placed):
    for child in range(PER):
        octant, parent = (child % 8, child // 8)
        slot = maps[PLACE + height, child]
        for n in range(2):
            value = arrived_ref[slot, n * 8 : n * 8 + 8, :]
            placed[pl.ds(octant * 8 * ROWS + n * 16 + parent, 8, stride=ROWS), :] = value


def filtered(data, weights):
    half = product(data, (weights[0][...], weights[1][...]))
    depth = half.shape[0]
    return product((weights[2][:, :depth], weights[3][:, :depth]), split(half))


def up_kernel(height, arrived_ref, maps_ref, filled_ref, bank_ref, out_ref, state_ref, kept_ref, *scratch):
    maps, corner, high, low, placed, blocks, v0, v1, v2, v3, sems = scratch
    weights = (v0, v1, v2, v3)
    pairs = [(maps_ref, maps), (filled_ref.at[height, 0:SLOTS], out_ref)] + list(zip(up_weights(bank_ref), weights))
    copies = fetch(pairs, sems)
    copies[0].wait()
    place_children(height, maps, arrived_ref, placed)
    window_octants(placed, high, low)
    targets = split_children(kept_ref, height)
    outs = [pltpu.make_async_copy(high, targets[0], sems.at[6]), pltpu.make_async_copy(low, targets[1], sems.at[7])]
    for out in outs:
        out.start()
    for copy in copies[2:]:
        copy.wait()
    value = filtered((high[...], low[...]), weights)
    corner[...] = value.reshape(CORNER, 16, 128)
    out = pltpu.make_async_copy(corner, state_ref.at[height, SLOTS : SLOTS + CORNER], sems.at[8])
    out.start()
    outs.append(out)
    parts = [value[i * ROWS : (i + 1) * ROWS, :] for i in range(DEGREE)]
    for part, chunk in enumerate(merge(parts)):
        for n in range(2):
            blocks[pl.ds(n * 8 + part, 16, stride=16), :] = chunk[n * 16 : n * 16 + 16]
    copies[1].wait()
    for child in range(PARENTS):
        out_ref[maps[TAKE + height + 1, child]] = block(blocks, child)
    for out in outs:
        out.wait()


def emit(height, maps, refined, blocks, out_ref):
    for octant in range(8):
        x, w = divmod(octant, 4)
        parts = []
        for i in range(DEGREE):
            start = (x * DEGREE + i) * ROWS
            parts.append(refined[start : start + ROWS, w * 128 : w * 128 + 128])
        for part, value in enumerate(merge(parts)):
            for n in range(2):
                blocks[pl.ds(octant * 16 + n * 8 + part, 16, stride=128), :] = value[n * 16 : n * 16 + 16]
    for child in range(PER):
        out_ref[maps[PLACE + height, child]] = block(blocks, child)


def top_kernel(height, arrived_ref, maps_ref, bank_ref, out_ref, *scratch):
    maps, high, low, placed, refined, blocks, v0, v1, v2, v3, sems = scratch
    weights = (v0, v1, v2, v3)
    copies = fetch([(maps_ref, maps)] + list(zip(both_weights(bank_ref), weights)), sems)
    copies[0].wait()
    place_children(height, maps, arrived_ref, placed)
    window_octants(placed, high, low)
    for copy in copies[1:]:
        copy.wait()
    refined[...] = filtered((high[...], low[...]), weights)
    emit(height, maps, refined, blocks, out_ref)


def base_kernel(bank_ref, out_ref, *scratch):
    data, weights, refined, sems = (scratch[0:6], scratch[6:10], scratch[10], scratch[11])
    pairs = list(zip(both_weights(bank_ref), weights))
    for height in range(3):
        pairs += list(zip(split_children(bank_ref, height), data[2 * height : 2 * height + 2]))
    copies = fetch(pairs, sems)
    for copy in copies[:4]:
        copy.wait()
    outs = []
    for i in range(3):
        copies[4 + 2 * i].wait()
        copies[5 + 2 * i].wait()
        refined[i] = filtered((data[2 * i][...], data[2 * i + 1][...]), weights)
        out = pltpu.make_async_copy(refined.at[i], out_ref.at[i], sems.at[10 + i])
        out.start()
        outs.append(out)
    for out in outs:
        out.wait()


def down_kernel(height, returned_ref, maps_ref, state_ref, base_ref, bank_ref, out_ref, *scratch):
    maps, corner, base, placed, delta, refined, blocks, v0, v1, v2, v3, sems = scratch
    weights = (v0, v1, v2, v3)
    pairs = [(maps_ref, maps), (state_ref.at[height, SLOTS : SLOTS + CORNER], corner)]
    pairs += list(zip(down_weights(bank_ref), weights)) + [(base_ref.at[height], base)]
    copies = fetch(pairs, sems)
    copies[0].wait()
    for child in range(PARENTS):
        slot = maps[TAKE + height + 1, child]
        for n in range(2):
            placed[pl.ds(n * 16 + child, 8, stride=ROWS), :] = returned_ref[slot, n * 8 : n * 8 + 8, :]
    lane = lax.broadcasted_iota(jnp.int32, (ROWS, 128), 1)
    chunks = [placed[part * ROWS : (part + 1) * ROWS, :] for part in range(8)]
    copies[1].wait()
    for i, value in enumerate(windows(chunks)):
        change = value - corner[2 * i : 2 * i + 2].reshape(ROWS, 128)
        delta[i * ROWS : (i + 1) * ROWS, :] = jnp.where(lane < PLANE, change, 0.0)
    for copy in copies[2:]:
        copy.wait()
    refined[...] = base[...] + filtered(split(delta[...]), weights)
    emit(height, maps, refined, blocks, out_ref)


def store_kernel(height, returned_ref, maps_ref, *rest):
    out_ref, maps, flat, rows, sems = rest[-5:]
    start, number = leaf_range(height)
    skip = PER - number
    copy = fetch([(maps_ref, maps)], sems)[0]
    copy.wait()
    outs = []
    step = 16
    for base in range(0, number, step):
        for child in range(base, base + step):
            flat[child * 16 : child * 16 + 16, :] = returned_ref[maps[TAKE + height, child + skip]]
        for first in range(base, base + step, 8):
            for n in range(2):
                for part in range(8):
                    value = flat[pl.ds(first * 16 + n * 8 + part, 8, stride=16), :]
                    if part < 7:
                        rows[n, first : first + 8, 128 * part : 128 * part + 128] = value
                    else:
                        rows[n, first : first + 8, 896:CELLS] = value[:, : CELLS - 896]
        span = slice(base, base + step)
        target = out_ref.at[:, start + base : start + base + step, :]
        out = pltpu.make_async_copy(rows.at[:, span, :], target, sems.at[1 + base // step])
        out.start()
        outs.append(out)
    for out in outs:
        out.wait()


def shape(*dims, dtype=f32):
    return jax.ShapeDtypeStruct(dims, dtype)


def call(kernel, out_shape, in_specs, out_specs, scratch, operands, flops, name, aliases=None, limit=LIMIT):
    moved = sum(4 * one.size for one in operands)
    return pl.pallas_call(
        kernel,
        out_shape=out_shape,
        in_specs=in_specs,
        out_specs=out_specs,
        scratch_shapes=scratch,
        input_output_aliases=aliases or {},
        compiler_params=pltpu.CompilerParams(vmem_limit_bytes=limit),
        cost_estimate=pl.CostEstimate(flops=flops, bytes_accessed=moved, transcendentals=0),
        name=name,
    )(*operands)


def invert(mapping):
    match = mapping[:, None, :] == jnp.arange(PER, dtype=jnp.int32)[None, :, None]
    return jnp.sum(jnp.where(match, jnp.arange(mapping.shape[1], dtype=jnp.int32)[None, None, :], 0), axis=2)


def exchange(blocks):
    return lax.all_to_all(blocks, "dev", split_axis=0, concat_axis=0, tiled=True)


def transform(leaves, send_slot, recv_slot, filter_up, filter_down):
    levels = send_slot.shape[0]
    rows = jnp.swapaxes(leaves, 1, 2)
    slots = shape(SLOTS, 16, 128)
    flat = lambda count: pltpu.VMEM((count * 16, 128), f32)
    going = call(
        first_kernel,
        slots,
        [HBM, HBM],
        VMEM,
        [pltpu.SMEM(send_slot.shape, jnp.int32), pltpu.VMEM((2, PER, CELLS), f32), flat(PER), DMA((5,))],
        (send_slot, rows),
        0,
        "pack_first",
        limit=FULL,
    )
    arrived = exchange(going)
    maps = jnp.concatenate([invert(send_slot), invert(recv_slot)], axis=0)
    maps_smem = pltpu.SMEM(maps.shape, jnp.int32)
    filled = call(
        rest_kernel,
        shape(8, SLOTS + CORNER, 16, 128),
        [SMEM, HBM],
        HBM,
        [pltpu.VMEM((2, 336, CELLS), f32), flat(336), pltpu.VMEM((3, SLOTS, 16, 128), f32), DMA((6,))],
        (maps, rows),
        0,
        "pack_rest",
        limit=FULL,
    )
    bank = call(
        weight_kernel,
        shape(BANK, 640, dtype=bf16),
        [VMEM, VMEM],
        HBM,
        [pltpu.VMEM((SPLIT, 640), bf16), DMA],
        (filter_up, filter_down),
        50_000_000,
        "weights",
        limit=FULL,
    )
    sizes = lambda *dims: [pltpu.VMEM(one, bf16) for one in dims for _ in range(2)]
    up, both, down = (sizes((512, 128), (320, 640)), sizes((512, 512), (640, 640)), sizes((128, 512), (640, 384)))
    wide = (640, 512)
    placed = pltpu.VMEM((8 * 8 * ROWS, 128), f32)
    split_wide = [pltpu.VMEM(wide, bf16)] * 2
    for height in range(levels - 1):
        going, filled, bank = call(
            functools.partial(up_kernel, height),
            (slots, shape(*filled.shape), shape(*bank.shape, dtype=bf16)),
            [VMEM] + [HBM] * 3,
            (VMEM, HBM, HBM),
            [maps_smem, pltpu.VMEM((CORNER, 16, 128), f32)] + split_wide + [placed, flat(PARENTS)] + up + [DMA((9,))],
            (arrived, maps, filled, bank),
            600_000_000,
            "up",
            {2: 1, 3: 2},
        )
        arrived = exchange(going)
    bases = call(
        base_kernel,
        shape(13, *wide),
        [HBM],
        HBM,
        split_wide * 3 + both + [pltpu.VMEM((3, *wide), f32), DMA((13,))],
        (bank,),
        7_200_000_000,
        "base",
        limit=FULL,
    )
    height = levels - 1
    going = call(
        functools.partial(top_kernel, height),
        slots,
        [VMEM, HBM, HBM],
        VMEM,
        [maps_smem] + split_wide + [placed, pltpu.VMEM(wide, f32), flat(PER)] + both + [DMA((5,))],
        (arrived, maps, bank),
        2_400_000_000,
        "top",
    )
    result = None
    while True:
        returned = exchange(going)
        start, number = leaf_range(height)
        final = shape(2, PER + 336, CELLS)
        scratch = [maps_smem, flat(number), pltpu.VMEM((2, number, CELLS), f32), DMA((1 + number // 16,))]
        kernel = functools.partial(store_kernel, height)
        if result is None:
            result = call(kernel, final, [VMEM, HBM], HBM, scratch, (returned, maps), 0, "store")
        else:
            result = call(kernel, final, [VMEM, HBM, HBM], HBM, scratch, (returned, maps, result), 0, "store", {2: 0})
        if height == 0:
            break
        height -= 1
        going = call(
            functools.partial(down_kernel, height),
            slots,
            [VMEM] + [HBM] * 4,
            VMEM,
            [maps_smem, pltpu.VMEM((CORNER, 16, 128), f32), pltpu.VMEM(wide, f32), pltpu.VMEM((8 * ROWS, 128), f32)]
            + [pltpu.VMEM((320, 128), f32), pltpu.VMEM(wide, f32), flat(PER)]
            + down
            + [DMA((7,))],
            (returned, maps, filled, bases, bank),
            800_000_000,
            "down",
        )
    return jnp.swapaxes(result, 1, 2)


def solution(mesh):
    in_specs = (P(None, None, "dev"), P(None, "dev"), P(None, "dev"), P(), P())
    out_specs = P(None, None, "dev")
    return jax.shard_map(transform, mesh=mesh, in_specs=in_specs, out_specs=out_specs, check_vma=False)
```

```python
import functools

import jax
import jax.numpy as jnp
from jax import lax
from jax.experimental import pallas as pl
from jax.experimental.pallas import tpu as pltpu
from jax.sharding import PartitionSpec as P

PER = 128
PARENTS = 16
DEGREE = 10
CELLS = 1000
PLANE = 100
SLOTS = 256
GROUPS = ((0,), (1,))
COUNT = len(GROUPS[0])
HEIGHT = 8 * COUNT
ROWS = PARENTS
WIDE = COUNT * 20 * ROWS
LIMIT = 50_000_000
FULL = 63_400_000
TAKE = 0
PLACE = 4
UP_ROW, BOTH_ROW, DOWN_ROW, PLANE_ROW, DOWN_PLANE, BANK_USED = (0, 320, 960, 1600, 2624, 2880)
BANK = 8448
SPLITS = 10496
LEVEL_ROOM = 10 // COUNT
BASE_ROOM = 18 // COUNT
CORNER = 20

highest = lax.Precision.HIGHEST
f32 = jnp.float32
bf16 = jnp.bfloat16
VMEM = pl.BlockSpec(memory_space=pltpu.VMEM)
SMEM = pl.BlockSpec(memory_space=pltpu.SMEM)
HBM = pl.BlockSpec(memory_space=pltpu.HBM)
DMA = pltpu.SemaphoreType.DMA


def leaf_range(height):
    if height == 0:
        return (0, PER)
    return (PER + 7 * PARENTS * (height - 1), 7 * PARENTS)


def split(value):
    high = value.astype(bf16)
    return high, (value - high.astype(f32)).astype(bf16)


def product(left, right):
    dot = functools.partial(jnp.dot, preferred_element_type=f32)
    return dot(left[0], right[0]) + (dot(left[0], right[1]) + dot(left[1], right[0]))


def windows(chunks):
    lane = lax.broadcasted_iota(jnp.int32, (ROWS, 128), 1)
    result = []
    for i in range(DEGREE):
        first, offset = divmod(PLANE * i, 128)
        value = chunks[first]
        if offset:
            value = pltpu.roll(value, 128 - offset, 1)
            if offset + PLANE > 128:
                later = pltpu.roll(chunks[first + 1], 128 - offset, 1)
                value = jnp.where(lane < 128 - offset, value, later)
        result.append(value)
    return result


def merge(parts):
    lane = lax.broadcasted_iota(jnp.int32, (ROWS, 128), 1)
    result = []
    for part in range(8):
        value = None
        for i in range(DEGREE):
            start = PLANE * i - 128 * part
            if start >= 128 or start + PLANE <= 0:
                continue
            piece = parts[i]
            if start % 128:
                piece = pltpu.roll(piece, start % 128, 1)
            if value is None:
                value = piece
            else:
                value = jnp.where(lane < start, value, piece)
        if part == 7:
            value = jnp.where(lane < CELLS - 896, value, 0.0)
        result.append(value)
    return result


def pack_rows(rows, start, number, flat_ref):
    for first in range(start, start + number, 8):
        for n in range(COUNT):
            for part in range(8):
                if part < 7:
                    value = rows[n, first : first + 8, 128 * part : 128 * part + 128]
                else:
                    value = rows[n, first : first + 8, 896:CELLS]
                    value = jnp.concatenate([value, jnp.zeros((8, 1024 - CELLS), f32)], axis=1)
                flat_ref[pl.ds(first * HEIGHT + n * 8 + part, 8, stride=HEIGHT), :] = value


def block(flat, index):
    return flat[index * HEIGHT : (index + 1) * HEIGHT, :]


def fetch(pairs, sems):
    copies = [pltpu.make_async_copy(source, target, sems.at[i]) for i, (source, target) in enumerate(pairs)]
    for copy in copies:
        copy.start()
    return copies


def first_kernel(orbital, send_ref, leaves_ref, out_ref, send, rows, flat, sems):
    quarter = PER // 4
    pairs = [(send_ref, send)]
    for i in range(4):
        span = slice(i * quarter, (i + 1) * quarter)
        pairs.append((leaves_ref.at[orbital : orbital + COUNT, span, :], rows.at[:, span, :]))
    copies = fetch(pairs, sems)
    for i in range(4):
        copies[i + 1].wait()
        pack_rows(rows, i * quarter, quarter, flat)
    copies[0].wait()
    for slot in range(SLOTS):
        start = pl.multiple_of(jnp.minimum(send[0, slot], PER - 1) * HEIGHT, HEIGHT)
        out_ref[slot] = flat[pl.ds(start, HEIGHT), :]


def rest_kernel(orbital, maps, leaves_ref, out_ref, rows, flat, filled, sems):
    number = 7 * PARENTS
    pairs = []
    for i in range(3):
        span = slice(i * number, (i + 1) * number)
        source = leaves_ref.at[orbital : orbital + COUNT, PER + i * number : PER + (i + 1) * number, :]
        pairs.append((source, rows.at[:, span, :]))
    copies = fetch(pairs, sems)
    outs = []
    for i in range(3):
        copies[i].wait()
        pack_rows(rows, i * number, number, flat)
        for child in range(number):
            filled[i, maps[TAKE + i + 1, PARENTS + child]] = block(flat, i * number + child)
        out = pltpu.make_async_copy(filled.at[i], out_ref.at[i, 0:SLOTS], sems.at[3 + i])
        out.start()
        outs.append(out)
    for out in outs:
        out.wait()


def one_hot(dims, axis, index):
    return (lax.broadcasted_iota(jnp.int32, dims, axis) == index).astype(f32)


def plane_index(dims, axis, size):
    position = lax.broadcasted_iota(jnp.int32, dims, axis)
    w, cell = (position >> 7, position & 127)
    j = (cell * 205) >> 11
    k = cell - DEGREE * j
    if size > DEGREE:
        j, k = (j + DEGREE * (w >> 1), k + DEGREE * (w & 1))
    dead = cell >= PLANE
    return jnp.where(dead, -1, j), jnp.where(dead, -1, k)


def exact(left, right, dims=((1,), (0,))):
    return lax.dot_general(left, right, (dims, ((), ())), precision=highest, preferred_element_type=f32)


def planes(filters, outs, ins):
    rows, columns = ((ins // DEGREE) ** 2 * 128, (outs // DEGREE) ** 2 * 128)
    factors = []
    for left, right in zip(plane_index((rows, ins), 0, ins), plane_index((outs, columns), 1, outs)):
        half = exact(one_hot((rows, ins), 1, left), filters, ((1,), (1,)))
        factors.append(exact(half, one_hot((outs, columns), 0, right)))
    return split(factors[0] * factors[1])


def spread(filters, outs, ins):
    rows, columns = (outs * ROWS, ins * ROWS)
    left = one_hot((rows, outs), 1, lax.broadcasted_iota(jnp.int32, (rows, outs), 0) >> 4)
    right = one_hot((ins, columns), 0, lax.broadcasted_iota(jnp.int32, (ins, columns), 1) >> 4)
    row = lax.broadcasted_iota(jnp.int32, (rows, columns), 0) & (ROWS - 1)
    column = lax.broadcasted_iota(jnp.int32, (rows, columns), 1) & (ROWS - 1)
    return split(jnp.where(row == column, exact(exact(left, filters), right), 0.0))


def weight_kernel(up_ref, down_ref, bank_ref, bank, sem):
    both = exact(down_ref[...], up_ref[...])
    up, down = (up_ref[0:DEGREE, :], down_ref[:, 0:DEGREE])
    sizes = ((up, 10, 20), (both, 20, 20), (down, 20, 10))
    plane_values = [planes(*size) for size in sizes]
    row_values = [spread(*size) for size in sizes]
    for i in range(2):
        bank[PLANE_ROW + 512 * i : PLANE_ROW + 512 * (i + 1), 512:640] = plane_values[0][i]
        bank[PLANE_ROW + 512 * i : PLANE_ROW + 512 * (i + 1), 0:512] = plane_values[1][i]
        bank[DOWN_PLANE + 128 * i : DOWN_PLANE + 128 * (i + 1), 0:512] = plane_values[2][i]
        bank[UP_ROW + 160 * i : UP_ROW + 160 * (i + 1), 0:320] = row_values[0][i]
        bank[BOTH_ROW + 320 * i : BOTH_ROW + 320 * (i + 1), 0:320] = row_values[1][i]
        bank[DOWN_ROW + 320 * i : DOWN_ROW + 320 * (i + 1), 0:160] = row_values[2][i]
    copy = pltpu.make_async_copy(bank, bank_ref.at[0:BANK_USED, :], sem)
    copy.start()
    copy.wait()


def section(bank_ref, start, rows, first, columns):
    return [bank_ref.at[start + i * rows : start + (i + 1) * rows, first : first + columns] for i in range(2)]


def up_weights(bank_ref):
    return section(bank_ref, PLANE_ROW, 512, 512, 128) + section(bank_ref, UP_ROW, 160, 0, 384)


def both_weights(bank_ref):
    return section(bank_ref, PLANE_ROW, 512, 0, 512) + section(bank_ref, BOTH_ROW, 320, 0, 384)


def down_weights(bank_ref):
    return section(bank_ref, DOWN_PLANE, 128, 0, 512) + section(bank_ref, DOWN_ROW, 320, 0, 256)


def split_children(splits_ref, height):
    return section(splits_ref, 2 * WIDE * height, WIDE, 0, 512)


def window_octants(placed, high_ref, low_ref):
    for n in range(COUNT):
        for octant in range(8):
            first = (n * 8 + octant) * 8
            chunks = [placed[(first + part) * ROWS : (first + part + 1) * ROWS, :] for part in range(8)]
            x, w = divmod(octant, 4)
            for i, value in enumerate(windows(chunks)):
                high, low = split(value)
                start = (n * 20 + x * DEGREE + i) * ROWS
                high_ref[start : start + ROWS, w * 128 : w * 128 + 128] = high
                low_ref[start : start + ROWS, w * 128 : w * 128 + 128] = low


def place_children(height, maps, arrived_ref, placed):
    for child in range(PER):
        octant, parent = (child % 8, child // 8)
        slot = maps[PLACE + height, child]
        for n in range(COUNT):
            value = arrived_ref[slot, n * 8 : n * 8 + 8, :]
            placed[pl.ds((n * 8 + octant) * 8 * ROWS + parent, 8, stride=ROWS), :] = value


def filtered(data, weights):
    half = split(product(data, (weights[0][...], weights[1][...])))
    depth = half[0].shape[0] // COUNT
    rows = (weights[2][:, :depth], weights[3][:, :depth])
    return [product(rows, tuple(one[n * depth : (n + 1) * depth] for one in half)) for n in range(COUNT)]


def up_kernel(height, arrived_ref, maps_ref, bank_ref, filled_ref, *rest):
    out_ref, state_ref, kept_ref, maps, corner, high, low, placed, blocks, v0, v1, v2, v3, sems = rest[-14:]
    weights = (v0, v1, v2, v3)
    pairs = [(maps_ref, maps)] + list(zip(up_weights(bank_ref), weights)) + [(filled_ref.at[height, 0:SLOTS], out_ref)]
    copies = fetch(pairs, sems)
    copies[0].wait()
    place_children(height, maps, arrived_ref, placed)
    window_octants(placed, high, low)
    targets = split_children(kept_ref, height)
    outs = [pltpu.make_async_copy(high, targets[0], sems.at[6]), pltpu.make_async_copy(low, targets[1], sems.at[7])]
    for out in outs:
        out.start()
    for copy in copies[1:5]:
        copy.wait()
    values = filtered((high[...], low[...]), weights)
    per = CORNER // COUNT
    for n in range(COUNT):
        corner[n * per : (n + 1) * per] = values[n].reshape(per, HEIGHT, 128)
    out = pltpu.make_async_copy(corner, state_ref.at[height, SLOTS : SLOTS + CORNER], sems.at[8])
    out.start()
    outs.append(out)
    for n in range(COUNT):
        parts = [values[n][i * ROWS : (i + 1) * ROWS, :] for i in range(DEGREE)]
        for part, chunk in enumerate(merge(parts)):
            blocks[pl.ds(n * 8 + part, PARENTS, stride=HEIGHT), :] = chunk
    copies[5].wait()
    for child in range(PARENTS):
        out_ref[maps[TAKE + height + 1, child]] = block(blocks, child)
    for out in outs:
        out.wait()


def emit(height, maps, refined, blocks, out_ref):
    for octant in range(8):
        x, w = divmod(octant, 4)
        for n in range(COUNT):
            parts = []
            for i in range(DEGREE):
                start = (n * 20 + x * DEGREE + i) * ROWS
                parts.append(refined[start : start + ROWS, w * 128 : w * 128 + 128])
            for part, value in enumerate(merge(parts)):
                blocks[pl.ds(octant * HEIGHT + n * 8 + part, PARENTS, stride=8 * HEIGHT), :] = value
    for child in range(PER):
        out_ref[maps[PLACE + height, child]] = block(blocks, child)


def keep(refined, values):
    depth = WIDE // COUNT
    for n in range(COUNT):
        refined[n * depth : (n + 1) * depth, :] = values[n]


def top_kernel(height, arrived_ref, maps_ref, bank_ref, out_ref, *scratch):
    maps, high, low, placed, refined, blocks, v0, v1, v2, v3, sems = scratch
    weights = (v0, v1, v2, v3)
    copies = fetch([(maps_ref, maps)] + list(zip(both_weights(bank_ref), weights)), sems)
    copies[0].wait()
    place_children(height, maps, arrived_ref, placed)
    window_octants(placed, high, low)
    for copy in copies[1:]:
        copy.wait()
    keep(refined, filtered((high[...], low[...]), weights))
    emit(height, maps, refined, blocks, out_ref)


def base_kernel(bank_ref, splits_ref, out_ref, *scratch):
    data, weights, refined, sems = (scratch[0:6], scratch[6:10], scratch[10], scratch[11])
    pairs = list(zip(both_weights(bank_ref), weights))
    for height in range(3):
        pairs += list(zip(split_children(splits_ref, height), data[2 * height : 2 * height + 2]))
    copies = fetch(pairs, sems)
    for copy in copies[:4]:
        copy.wait()
    outs = []
    for i in range(3):
        copies[4 + 2 * i].wait()
        copies[5 + 2 * i].wait()
        keep(refined.at[i], filtered((data[2 * i][...], data[2 * i + 1][...]), weights))
        out = pltpu.make_async_copy(refined.at[i], out_ref.at[i], sems.at[10 + i])
        out.start()
        outs.append(out)
    for out in outs:
        out.wait()


def down_kernel(height, returned_ref, maps_ref, state_ref, base_ref, bank_ref, out_ref, *scratch):
    maps, corner, base, placed, delta, refined, blocks, v0, v1, v2, v3, sems = scratch
    weights = (v0, v1, v2, v3)
    pairs = [(maps_ref, maps), (state_ref.at[height, SLOTS : SLOTS + CORNER], corner)]
    pairs += list(zip(down_weights(bank_ref), weights)) + [(base_ref.at[height], base)]
    copies = fetch(pairs, sems)
    copies[0].wait()
    for child in range(PARENTS):
        slot = maps[TAKE + height + 1, child]
        for n in range(COUNT):
            placed[pl.ds(n * 8 * ROWS + child, 8, stride=ROWS), :] = returned_ref[slot, n * 8 : n * 8 + 8, :]
    lane = lax.broadcasted_iota(jnp.int32, (ROWS, 128), 1)
    copies[1].wait()
    per = ROWS // HEIGHT
    for n in range(COUNT):
        chunks = [placed[(n * 8 + part) * ROWS : (n * 8 + part + 1) * ROWS, :] for part in range(8)]
        for i, value in enumerate(windows(chunks)):
            start = (n * DEGREE + i) * per
            change = value - corner[start : start + per].reshape(ROWS, 128)
            start = (n * DEGREE + i) * ROWS
            delta[start : start + ROWS, :] = jnp.where(lane < PLANE, change, 0.0)
    for copy in copies[2:6]:
        copy.wait()
    values = filtered(split(delta[...]), weights)
    copies[6].wait()
    depth = WIDE // COUNT
    keep(refined, [base[n * depth : (n + 1) * depth, :] + values[n] for n in range(COUNT)])
    emit(height, maps, refined, blocks, out_ref)


def store_kernel(height, orbital, returned_ref, maps_ref, *rest):
    out_ref, maps, flat, rows, sems = rest[-5:]
    start, number = leaf_range(height)
    skip = PER - number
    copy = fetch([(maps_ref, maps)], sems)[0]
    copy.wait()
    outs = []
    step = 16
    for base in range(0, number, step):
        for child in range(base, base + step):
            flat[child * HEIGHT : (child + 1) * HEIGHT, :] = returned_ref[maps[TAKE + height, child + skip]]
        for first in range(base, base + step, 8):
            for n in range(COUNT):
                for part in range(8):
                    value = flat[pl.ds(first * HEIGHT + n * 8 + part, 8, stride=HEIGHT), :]
                    if part < 7:
                        rows[n, first : first + 8, 128 * part : 128 * part + 128] = value
                    else:
                        rows[n, first : first + 8, 896:CELLS] = value[:, : CELLS - 896]
        span = slice(base, base + step)
        target = out_ref.at[orbital : orbital + COUNT, start + base : start + base + step, :]
        out = pltpu.make_async_copy(rows.at[:, span, :], target, sems.at[1 + base // step])
        out.start()
        outs.append(out)
    for out in outs:
        out.wait()


def shape(*dims, dtype=f32):
    return jax.ShapeDtypeStruct(dims, dtype)


def call(kernel, out_shape, in_specs, out_specs, scratch, operands, flops, name, aliases=None, limit=LIMIT):
    moved = sum(4 * one.size for one in operands)
    return pl.pallas_call(
        kernel,
        out_shape=out_shape,
        in_specs=in_specs,
        out_specs=out_specs,
        scratch_shapes=scratch,
        input_output_aliases=aliases or {},
        compiler_params=pltpu.CompilerParams(vmem_limit_bytes=limit),
        cost_estimate=pl.CostEstimate(flops=flops, bytes_accessed=moved, transcendentals=0),
        name=name,
    )(*operands)


def invert(mapping):
    match = mapping[:, None, :] == jnp.arange(PER, dtype=jnp.int32)[None, :, None]
    return jnp.sum(jnp.where(match, jnp.arange(mapping.shape[1], dtype=jnp.int32)[None, None, :], 0), axis=2)


def exchange(blocks):
    return lax.all_to_all(blocks, "dev", split_axis=0, concat_axis=0, tiled=True)


def flat(number):
    return pltpu.VMEM((number * HEIGHT, 128), f32)


def halves(*dims):
    return [pltpu.VMEM(one, bf16) for one in dims for _ in range(2)]


class Chain:
    def __init__(self, orbital, rows, send_slot):
        self.orbital = orbital
        self.rows = rows
        self.slots = shape(SLOTS, HEIGHT, 128)
        self.placed = pltpu.VMEM((COUNT * 8 * 8 * ROWS, 128), f32)
        self.going = call(
            functools.partial(first_kernel, orbital),
            self.slots,
            [HBM, HBM],
            VMEM,
            [pltpu.SMEM(send_slot.shape, jnp.int32), pltpu.VMEM((COUNT, PER, CELLS), f32), flat(PER), DMA((5,))],
            (send_slot, rows),
            0,
            "pack_first",
            limit=FULL,
        )

    def swap(self):
        self.arrived = exchange(self.going)

    def prepare(self, maps, bank):
        self.maps, self.bank = (maps, bank)
        self.maps_smem = pltpu.SMEM(maps.shape, jnp.int32)
        self.filled = call(
            functools.partial(rest_kernel, self.orbital),
            shape(LEVEL_ROOM, SLOTS + CORNER, HEIGHT, 128),
            [SMEM, HBM],
            HBM,
            [pltpu.VMEM((COUNT, 336, CELLS), f32), flat(336), pltpu.VMEM((3, SLOTS, HEIGHT, 128), f32), DMA((6,))],
            (maps, self.rows),
            0,
            "pack_rest",
            limit=FULL,
        )
        self.splits = None

    def up(self, height):
        weights = halves((512, 128), (160, 384))
        scratch = [self.maps_smem, pltpu.VMEM((CORNER, HEIGHT, 128), f32)] + halves((WIDE, 512))
        scratch += [self.placed, flat(PARENTS)] + weights + [DMA((9,))]
        operands = (self.arrived, self.maps, self.bank, self.filled)
        aliases = {3: 1}
        if self.splits is not None:
            operands += (self.splits,)
            aliases[4] = 2
        self.going, self.filled, self.splits = call(
            functools.partial(up_kernel, height),
            (self.slots, shape(*self.filled.shape), shape(SPLITS, 512, dtype=bf16)),
            [VMEM] + [HBM] * (len(operands) - 1),
            (VMEM, HBM, HBM),
            scratch,
            operands,
            300_000_000,
            "up",
            aliases,
        )

    def base(self):
        self.bases = call(
            base_kernel,
            shape(BASE_ROOM, WIDE, 512),
            [HBM, HBM],
            HBM,
            halves((WIDE, 512)) * 3 + halves((512, 512), (320, 384)) + [pltpu.VMEM((3, WIDE, 512), f32), DMA((13,))],
            (self.bank, self.splits),
            3_600_000_000,
            "base",
            limit=FULL,
        )

    def top(self, height):
        scratch = [self.maps_smem] + halves((WIDE, 512)) + [self.placed, pltpu.VMEM((WIDE, 512), f32), flat(PER)]
        scratch += halves((512, 512), (320, 384)) + [DMA((5,))]
        self.going = call(
            functools.partial(top_kernel, height),
            self.slots,
            [VMEM, HBM, HBM],
            VMEM,
            scratch,
            (self.arrived, self.maps, self.bank),
            1_200_000_000,
            "top",
        )

    def down(self, height):
        scratch = [self.maps_smem, pltpu.VMEM((CORNER, HEIGHT, 128), f32), pltpu.VMEM((WIDE, 512), f32)]
        scratch += [pltpu.VMEM((COUNT * 8 * ROWS, 128), f32), pltpu.VMEM((WIDE // 2, 128), f32)]
        scratch += [pltpu.VMEM((WIDE, 512), f32), flat(PER)] + halves((128, 512), (320, 256)) + [DMA((7,))]
        self.going = call(
            functools.partial(down_kernel, height),
            self.slots,
            [VMEM] + [HBM] * 4,
            VMEM,
            scratch,
            (self.arrived, self.maps, self.filled, self.bases, self.bank),
            400_000_000,
            "down",
        )

    def store(self, height, result):
        start, number = leaf_range(height)
        final = shape(2, PER + 336, CELLS)
        scratch = [self.maps_smem, flat(number), pltpu.VMEM((COUNT, number, CELLS), f32), DMA((1 + number // 16,))]
        kernel = functools.partial(store_kernel, height, self.orbital)
        operands = (self.arrived, self.maps) if result is None else (self.arrived, self.maps, result)
        specs = [VMEM, HBM, HBM][: len(operands)]
        aliases = None if result is None else {2: 0}
        return call(kernel, final, specs, HBM, scratch, operands, 0, "store", aliases)


def transform(leaves, send_slot, recv_slot, filter_up, filter_down):
    levels = send_slot.shape[0]
    rows = jnp.swapaxes(leaves, 1, 2)
    chains = [Chain(group[0], rows, send_slot) for group in GROUPS]
    for chain in chains:
        chain.swap()
    maps = jnp.concatenate([invert(send_slot), invert(recv_slot)], axis=0)
    bank = call(
        weight_kernel,
        shape(BANK, 640, dtype=bf16),
        [VMEM, VMEM],
        HBM,
        [pltpu.VMEM((BANK_USED, 640), bf16), DMA],
        (filter_up, filter_down),
        50_000_000,
        "weights",
        limit=FULL,
    )
    for chain in chains:
        chain.prepare(maps, bank)
    for height in range(levels - 1):
        for chain in chains:
            chain.up(height)
            chain.swap()
    height = levels - 1
    for chain in chains:
        chain.base()
        chain.top(height)
        chain.swap()
    result = None
    while True:
        for chain in chains:
            result = chain.store(height, result)
            if height > 0:
                chain.down(height - 1)
                chain.swap()
        if height == 0:
            break
        height -= 1
    return jnp.swapaxes(result, 1, 2)


def solution(mesh):
    in_specs = (P(None, None, "dev"), P(None, "dev"), P(None, "dev"), P(), P())
    out_specs = P(None, None, "dev")
    return jax.shard_map(transform, mesh=mesh, in_specs=in_specs, out_specs=out_specs, check_vma=False)
```

```python
import functools

import jax
import jax.numpy as jnp
from jax import lax
from jax.experimental import pallas as pl
from jax.experimental.pallas import tpu as pltpu
from jax.sharding import PartitionSpec as P

PER = 128
PARENTS = 16
DEGREE = 10
CELLS = 1000
PLANE = 100
SLOTS = 256
GROUPS = ((0, 1),)
COUNT = len(GROUPS[0])
HEIGHT = 8 * COUNT
ROWS = PARENTS
WIDE = COUNT * 20 * ROWS
LIMIT = 50_000_000
FULL = 63_400_000
TAKE = 0
PLACE = 4
UP_ROW, BOTH_ROW, DOWN_ROW, PLANE_ROW, DOWN_PLANE, BANK_USED = (0, 320, 960, 1600, 2624, 2880)
BANK = 8448
SPLITS = 10496
LEVEL_ROOM = 12 // COUNT
BASE_ROOM = 18 // COUNT

highest = lax.Precision.HIGHEST
f32 = jnp.float32
bf16 = jnp.bfloat16
VMEM = pl.BlockSpec(memory_space=pltpu.VMEM)
SMEM = pl.BlockSpec(memory_space=pltpu.SMEM)
HBM = pl.BlockSpec(memory_space=pltpu.HBM)
DMA = pltpu.SemaphoreType.DMA


def leaf_range(height):
    if height == 0:
        return (0, PER)
    return (PER + 7 * PARENTS * (height - 1), 7 * PARENTS)


def split(value):
    high = value.astype(bf16)
    return high, (value - high.astype(f32)).astype(bf16)


def product(left, right):
    dot = functools.partial(jnp.dot, preferred_element_type=f32)
    return dot(left[0], right[0]) + (dot(left[0], right[1]) + dot(left[1], right[0]))


def windows(chunks):
    lane = lax.broadcasted_iota(jnp.int32, (ROWS, 128), 1)
    result = []
    for i in range(DEGREE):
        first, offset = divmod(PLANE * i, 128)
        value = chunks[first]
        if offset:
            value = pltpu.roll(value, 128 - offset, 1)
            if offset + PLANE > 128:
                later = pltpu.roll(chunks[first + 1], 128 - offset, 1)
                value = jnp.where(lane < 128 - offset, value, later)
        result.append(value)
    return result


def merge(parts):
    lane = lax.broadcasted_iota(jnp.int32, (ROWS, 128), 1)
    result = []
    for part in range(8):
        value = None
        for i in range(DEGREE):
            start = PLANE * i - 128 * part
            if start >= 128 or start + PLANE <= 0:
                continue
            piece = parts[i]
            if start % 128:
                piece = pltpu.roll(piece, start % 128, 1)
            if value is None:
                value = piece
            else:
                value = jnp.where(lane < start, value, piece)
        if part == 7:
            value = jnp.where(lane < CELLS - 896, value, 0.0)
        result.append(value)
    return result


def pack_rows(rows, start, number, flat_ref):
    for first in range(start, start + number, 8):
        for n in range(COUNT):
            for part in range(8):
                if part < 7:
                    value = rows[n, first : first + 8, 128 * part : 128 * part + 128]
                else:
                    value = rows[n, first : first + 8, 896:CELLS]
                    value = jnp.concatenate([value, jnp.zeros((8, 1024 - CELLS), f32)], axis=1)
                flat_ref[pl.ds(first * HEIGHT + n * 8 + part, 8, stride=HEIGHT), :] = value


def block(flat, index):
    return flat[index * HEIGHT : (index + 1) * HEIGHT, :]


def fetch(pairs, sems):
    copies = [pltpu.make_async_copy(source, target, sems.at[i]) for i, (source, target) in enumerate(pairs)]
    for copy in copies:
        copy.start()
    return copies


def first_kernel(orbital, send_ref, leaves_ref, out_ref, send, rows, flat, filled, sems):
    quarter = PER // 4
    pairs = [(send_ref, send)]
    for i in range(4):
        span = slice(i * quarter, (i + 1) * quarter)
        pairs.append((leaves_ref.at[orbital : orbital + COUNT, span, :], rows.at[:, span, :]))
    copies = fetch(pairs, sems)
    for i in range(4):
        copies[i + 1].wait()
        pack_rows(rows, i * quarter, quarter, flat)
    copies[0].wait()
    outs = []
    quarter = SLOTS // 4
    for i in range(4):
        for slot in range(i * quarter, (i + 1) * quarter):
            start = pl.multiple_of(jnp.minimum(send[0, slot], PER - 1) * HEIGHT, HEIGHT)
            filled[slot] = flat[pl.ds(start, HEIGHT), :]
        span = slice(i * quarter, (i + 1) * quarter)
        out = pltpu.make_async_copy(filled.at[span], out_ref.at[span], sems.at[5 + i])
        out.start()
        outs.append(out)
    for out in outs:
        out.wait()


def rest_kernel(orbital, maps, leaves_ref, out_ref, rows, flat, filled, sems):
    number = 7 * PARENTS
    pairs = []
    for i in range(3):
        span = slice(i * number, (i + 1) * number)
        source = leaves_ref.at[orbital : orbital + COUNT, PER + i * number : PER + (i + 1) * number, :]
        pairs.append((source, rows.at[:, span, :]))
    copies = fetch(pairs, sems)
    outs = []
    for i in range(3):
        copies[i].wait()
        pack_rows(rows, i * number, number, flat)
        for child in range(number):
            filled[i, maps[TAKE + i + 1, PARENTS + child]] = block(flat, i * number + child)
        out = pltpu.make_async_copy(filled.at[i], out_ref.at[i], sems.at[3 + i])
        out.start()
        outs.append(out)
    for out in outs:
        out.wait()


def one_hot(dims, axis, index):
    return (lax.broadcasted_iota(jnp.int32, dims, axis) == index).astype(f32)


def plane_index(dims, axis, size):
    position = lax.broadcasted_iota(jnp.int32, dims, axis)
    w, cell = (position >> 7, position & 127)
    j = (cell * 205) >> 11
    k = cell - DEGREE * j
    if size > DEGREE:
        j, k = (j + DEGREE * (w >> 1), k + DEGREE * (w & 1))
    dead = cell >= PLANE
    return jnp.where(dead, -1, j), jnp.where(dead, -1, k)


def exact(left, right, dims=((1,), (0,))):
    return lax.dot_general(left, right, (dims, ((), ())), precision=highest, preferred_element_type=f32)


def planes(filters, outs, ins):
    rows, columns = ((ins // DEGREE) ** 2 * 128, (outs // DEGREE) ** 2 * 128)
    factors = []
    for left, right in zip(plane_index((rows, ins), 0, ins), plane_index((outs, columns), 1, outs)):
        half = exact(one_hot((rows, ins), 1, left), filters, ((1,), (1,)))
        factors.append(exact(half, one_hot((outs, columns), 0, right)))
    return split(factors[0] * factors[1])


def spread(filters, outs, ins):
    rows, columns = (outs * ROWS, ins * ROWS)
    left = one_hot((rows, outs), 1, lax.broadcasted_iota(jnp.int32, (rows, outs), 0) >> 4)
    right = one_hot((ins, columns), 0, lax.broadcasted_iota(jnp.int32, (ins, columns), 1) >> 4)
    row = lax.broadcasted_iota(jnp.int32, (rows, columns), 0) & (ROWS - 1)
    column = lax.broadcasted_iota(jnp.int32, (rows, columns), 1) & (ROWS - 1)
    return split(jnp.where(row == column, exact(exact(left, filters), right), 0.0))


def weight_kernel(up_ref, down_ref, bank_ref, bank, sem):
    both = exact(down_ref[...], up_ref[...])
    up, down = (up_ref[0:DEGREE, :], down_ref[:, 0:DEGREE])
    sizes = ((up, 10, 20), (both, 20, 20), (down, 20, 10))
    plane_values = [planes(*size) for size in sizes]
    row_values = [spread(*size) for size in sizes]
    for i in range(2):
        bank[PLANE_ROW + 512 * i : PLANE_ROW + 512 * (i + 1), 512:640] = plane_values[0][i]
        bank[PLANE_ROW + 512 * i : PLANE_ROW + 512 * (i + 1), 0:512] = plane_values[1][i]
        bank[DOWN_PLANE + 128 * i : DOWN_PLANE + 128 * (i + 1), 0:512] = plane_values[2][i]
        bank[UP_ROW + 160 * i : UP_ROW + 160 * (i + 1), 0:320] = row_values[0][i]
        bank[BOTH_ROW + 320 * i : BOTH_ROW + 320 * (i + 1), 0:320] = row_values[1][i]
        bank[DOWN_ROW + 320 * i : DOWN_ROW + 320 * (i + 1), 0:160] = row_values[2][i]
    copy = pltpu.make_async_copy(bank, bank_ref.at[0:BANK_USED, :], sem)
    copy.start()
    copy.wait()


def section(bank_ref, start, rows, first, columns):
    return [bank_ref.at[start + i * rows : start + (i + 1) * rows, first : first + columns] for i in range(2)]


def up_weights(bank_ref):
    return section(bank_ref, PLANE_ROW, 512, 512, 128) + section(bank_ref, UP_ROW, 160, 0, 384)


def both_weights(bank_ref):
    return section(bank_ref, PLANE_ROW, 512, 0, 512) + section(bank_ref, BOTH_ROW, 320, 0, 384)


def down_weights(bank_ref):
    return section(bank_ref, DOWN_PLANE, 128, 0, 512) + section(bank_ref, DOWN_ROW, 320, 0, 256)


def split_children(splits_ref, height):
    return section(splits_ref, 2 * WIDE * height, WIDE, 0, 512)


def window_octants(placed, high_ref, low_ref):
    for n in range(COUNT):
        for octant in range(8):
            first = (n * 8 + octant) * 8
            chunks = [placed[(first + part) * ROWS : (first + part + 1) * ROWS, :] for part in range(8)]
            x, w = divmod(octant, 4)
            for i, value in enumerate(windows(chunks)):
                high, low = split(value)
                start = (n * 20 + x * DEGREE + i) * ROWS
                high_ref[start : start + ROWS, w * 128 : w * 128 + 128] = high
                low_ref[start : start + ROWS, w * 128 : w * 128 + 128] = low


def place_children(height, maps, arrived_ref, placed):
    for child in range(PER):
        octant, parent = (child % 8, child // 8)
        slot = maps[PLACE + height, child]
        for n in range(COUNT):
            value = arrived_ref[slot, n * 8 : n * 8 + 8, :]
            placed[pl.ds((n * 8 + octant) * 8 * ROWS + parent, 8, stride=ROWS), :] = value


def filtered(data, weights):
    half = split(product(data, (weights[0][...], weights[1][...])))
    depth = half[0].shape[0] // COUNT
    rows = (weights[2][:, :depth], weights[3][:, :depth])
    return [product(rows, tuple(one[n * depth : (n + 1) * depth] for one in half)) for n in range(COUNT)]


def up_kernel(height, arrived_ref, maps_ref, bank_ref, filled_ref, *rest):
    out_ref, kept_ref, maps, high, low, placed, blocks, v0, v1, v2, v3, sems = rest[-12:]
    weights = (v0, v1, v2, v3)
    pairs = [(maps_ref, maps)] + list(zip(up_weights(bank_ref), weights)) + [(filled_ref.at[height], out_ref)]
    copies = fetch(pairs, sems)
    copies[0].wait()
    place_children(height, maps, arrived_ref, placed)
    window_octants(placed, high, low)
    targets = split_children(kept_ref, height)
    outs = [pltpu.make_async_copy(high, targets[0], sems.at[6]), pltpu.make_async_copy(low, targets[1], sems.at[7])]
    for out in outs:
        out.start()
    for copy in copies[1:5]:
        copy.wait()
    values = filtered((high[...], low[...]), weights)
    for n in range(COUNT):
        parts = [values[n][i * ROWS : (i + 1) * ROWS, :] for i in range(DEGREE)]
        for part, chunk in enumerate(merge(parts)):
            blocks[pl.ds(n * 8 + part, PARENTS, stride=HEIGHT), :] = chunk
    copies[5].wait()
    for child in range(PARENTS):
        out_ref[maps[TAKE + height + 1, child]] = block(blocks, child)
    for out in outs:
        out.wait()


def emit(height, maps, refined, blocks, out_ref):
    for octant in range(8):
        x, w = divmod(octant, 4)
        for n in range(COUNT):
            parts = []
            for i in range(DEGREE):
                start = (n * 20 + x * DEGREE + i) * ROWS
                parts.append(refined[start : start + ROWS, w * 128 : w * 128 + 128])
            for part, value in enumerate(merge(parts)):
                blocks[pl.ds(octant * HEIGHT + n * 8 + part, PARENTS, stride=8 * HEIGHT), :] = value
    for child in range(PER):
        out_ref[maps[PLACE + height, child]] = block(blocks, child)


def keep(refined, values):
    depth = WIDE // COUNT
    for n in range(COUNT):
        refined[n * depth : (n + 1) * depth, :] = values[n]


def top_kernel(height, arrived_ref, maps_ref, bank_ref, out_ref, *scratch):
    maps, high, low, placed, refined, blocks, v0, v1, v2, v3, sems = scratch
    weights = (v0, v1, v2, v3)
    copies = fetch([(maps_ref, maps)] + list(zip(both_weights(bank_ref), weights)), sems)
    copies[0].wait()
    place_children(height, maps, arrived_ref, placed)
    window_octants(placed, high, low)
    for copy in copies[1:]:
        copy.wait()
    keep(refined, filtered((high[...], low[...]), weights))
    emit(height, maps, refined, blocks, out_ref)


def base_kernel(bank_ref, splits_ref, out_ref, *scratch):
    data, weights, refined, sems = (scratch[0:6], scratch[6:18], scratch[18], scratch[19])
    both, up, down = (weights[0:4], weights[4:8], weights[8:12])
    pairs = list(zip(both_weights(bank_ref) + up_weights(bank_ref) + down_weights(bank_ref), weights))
    for height in range(3):
        pairs += list(zip(split_children(splits_ref, height), data[2 * height : 2 * height + 2]))
    copies = fetch(pairs, sems)
    for copy in copies[:12]:
        copy.wait()
    outs = []
    for i in range(3):
        copies[12 + 2 * i].wait()
        copies[13 + 2 * i].wait()
        children = (data[2 * i][...], data[2 * i + 1][...])
        corner = jnp.concatenate(filtered(children, up), axis=0)
        inner = filtered(split(corner), down)
        keep(refined.at[i], [whole - part for whole, part in zip(filtered(children, both), inner)])
        out = pltpu.make_async_copy(refined.at[i], out_ref.at[i], sems.at[18 + i])
        out.start()
        outs.append(out)
    for out in outs:
        out.wait()


def down_kernel(height, returned_ref, maps_ref, base_ref, bank_ref, out_ref, *scratch):
    maps, base, placed, high, low, refined, blocks, v0, v1, v2, v3, sems = scratch
    weights = (v0, v1, v2, v3)
    pairs = [(maps_ref, maps)] + list(zip(down_weights(bank_ref), weights)) + [(base_ref.at[height], base)]
    copies = fetch(pairs, sems)
    copies[0].wait()
    for child in range(PARENTS):
        slot = maps[TAKE + height + 1, child]
        for n in range(COUNT):
            placed[pl.ds(n * 8 * ROWS + child, 8, stride=ROWS), :] = returned_ref[slot, n * 8 : n * 8 + 8, :]
    for n in range(COUNT):
        chunks = [placed[(n * 8 + part) * ROWS : (n * 8 + part + 1) * ROWS, :] for part in range(8)]
        for i, value in enumerate(windows(chunks)):
            start = (n * DEGREE + i) * ROWS
            high[start : start + ROWS, :], low[start : start + ROWS, :] = split(value)
    for copy in copies[1:5]:
        copy.wait()
    values = filtered((high[...], low[...]), weights)
    copies[5].wait()
    depth = WIDE // COUNT
    keep(refined, [base[n * depth : (n + 1) * depth, :] + values[n] for n in range(COUNT)])
    emit(height, maps, refined, blocks, out_ref)


def store_kernel(height, orbital, returned_ref, maps_ref, *rest):
    out_ref, maps, flat, rows, sems = rest[-5:]
    start, number = leaf_range(height)
    skip = PER - number
    copy = fetch([(maps_ref, maps)], sems)[0]
    copy.wait()
    outs = []
    step = 16
    for base in range(0, number, step):
        for child in range(base, base + step):
            flat[child * HEIGHT : (child + 1) * HEIGHT, :] = returned_ref[maps[TAKE + height, child + skip]]
        for first in range(base, base + step, 8):
            for n in range(COUNT):
                for part in range(8):
                    value = flat[pl.ds(first * HEIGHT + n * 8 + part, 8, stride=HEIGHT), :]
                    if part < 7:
                        rows[n, first : first + 8, 128 * part : 128 * part + 128] = value
                    else:
                        rows[n, first : first + 8, 896:CELLS] = value[:, : CELLS - 896]
        span = slice(base, base + step)
        target = out_ref.at[orbital : orbital + COUNT, start + base : start + base + step, :]
        out = pltpu.make_async_copy(rows.at[:, span, :], target, sems.at[1 + base // step])
        out.start()
        outs.append(out)
    for out in outs:
        out.wait()


def shape(*dims, dtype=f32):
    return jax.ShapeDtypeStruct(dims, dtype)


def call(kernel, out_shape, in_specs, out_specs, scratch, operands, flops, name, aliases=None, limit=LIMIT):
    moved = sum(4 * one.size for one in operands)
    return pl.pallas_call(
        kernel,
        out_shape=out_shape,
        in_specs=in_specs,
        out_specs=out_specs,
        scratch_shapes=scratch,
        input_output_aliases=aliases or {},
        compiler_params=pltpu.CompilerParams(vmem_limit_bytes=limit),
        cost_estimate=pl.CostEstimate(flops=flops, bytes_accessed=moved, transcendentals=0),
        name=name,
    )(*operands)


def invert(mapping):
    match = mapping[:, None, :] == jnp.arange(PER, dtype=jnp.int32)[None, :, None]
    return jnp.sum(jnp.where(match, jnp.arange(mapping.shape[1], dtype=jnp.int32)[None, None, :], 0), axis=2)


def exchange(blocks):
    return lax.all_to_all(blocks, "dev", split_axis=0, concat_axis=0, tiled=True)


def flat(number):
    return pltpu.VMEM((number * HEIGHT, 128), f32)


def halves(*dims):
    return [pltpu.VMEM(one, bf16) for one in dims for _ in range(2)]


class Chain:
    def __init__(self, orbital, rows, send_slot):
        self.orbital = orbital
        self.rows = rows
        self.slots = shape(SLOTS, HEIGHT, 128)
        self.placed = pltpu.VMEM((COUNT * 8 * 8 * ROWS, 128), f32)
        self.going = call(
            functools.partial(first_kernel, orbital),
            self.slots,
            [HBM, HBM],
            HBM,
            [pltpu.SMEM(send_slot.shape, jnp.int32), pltpu.VMEM((COUNT, PER, CELLS), f32), flat(PER)]
            + [pltpu.VMEM((SLOTS, HEIGHT, 128), f32), DMA((9,))],
            (send_slot, rows),
            0,
            "pack_first",
            limit=FULL,
        )

    def swap(self):
        self.arrived = exchange(self.going)

    def prepare(self, maps, bank):
        self.maps, self.bank = (maps, bank)
        self.maps_smem = pltpu.SMEM(maps.shape, jnp.int32)
        self.filled = call(
            functools.partial(rest_kernel, self.orbital),
            shape(LEVEL_ROOM, SLOTS, HEIGHT, 128),
            [SMEM, HBM],
            HBM,
            [pltpu.VMEM((COUNT, 336, CELLS), f32), flat(336), pltpu.VMEM((3, SLOTS, HEIGHT, 128), f32), DMA((6,))],
            (maps, self.rows),
            0,
            "pack_rest",
            limit=FULL,
        )
        self.splits = None

    def up(self, height):
        weights = halves((512, 128), (160, 384))
        scratch = [self.maps_smem] + halves((WIDE, 512)) + [self.placed, flat(PARENTS)] + weights + [DMA((8,))]
        operands = (self.arrived, self.maps, self.bank, self.filled)
        aliases = {}
        if self.splits is not None:
            operands += (self.splits,)
            aliases[4] = 1
        self.going, self.splits = call(
            functools.partial(up_kernel, height),
            (self.slots, shape(SPLITS, 512, dtype=bf16)),
            [VMEM] + [HBM] * (len(operands) - 1),
            (VMEM, HBM),
            scratch,
            operands,
            300_000_000,
            "up",
            aliases,
        )

    def base(self):
        self.bases = call(
            base_kernel,
            shape(BASE_ROOM, WIDE, 512),
            [HBM, HBM],
            HBM,
            halves((WIDE, 512)) * 3
            + halves((512, 512), (320, 384), (512, 128), (160, 384), (128, 512), (320, 256))
            + [pltpu.VMEM((3, WIDE, 512), f32), DMA((21,))],
            (self.bank, self.splits),
            3_600_000_000,
            "base",
            limit=FULL,
        )

    def top(self, height):
        scratch = [self.maps_smem] + halves((WIDE, 512)) + [self.placed, pltpu.VMEM((WIDE, 512), f32), flat(PER)]
        scratch += halves((512, 512), (320, 384)) + [DMA((5,))]
        self.going = call(
            functools.partial(top_kernel, height),
            self.slots,
            [VMEM, HBM, HBM],
            VMEM,
            scratch,
            (self.arrived, self.maps, self.bank),
            1_200_000_000,
            "top",
        )

    def down(self, height):
        scratch = [self.maps_smem, pltpu.VMEM((WIDE, 512), f32), pltpu.VMEM((COUNT * 8 * ROWS, 128), f32)]
        scratch += halves((WIDE // 2, 128)) + [pltpu.VMEM((WIDE, 512), f32), flat(PER)]
        scratch += halves((128, 512), (320, 256)) + [DMA((6,))]
        self.going = call(
            functools.partial(down_kernel, height),
            self.slots,
            [VMEM] + [HBM] * 3,
            VMEM,
            scratch,
            (self.arrived, self.maps, self.bases, self.bank),
            400_000_000,
            "down",
        )

    def store(self, height, result):
        start, number = leaf_range(height)
        final = shape(2, PER + 336, CELLS)
        scratch = [self.maps_smem, flat(number), pltpu.VMEM((COUNT, number, CELLS), f32), DMA((1 + number // 16,))]
        kernel = functools.partial(store_kernel, height, self.orbital)
        operands = (self.arrived, self.maps) if result is None else (self.arrived, self.maps, result)
        specs = [VMEM, HBM, HBM][: len(operands)]
        aliases = None if result is None else {2: 0}
        return call(kernel, final, specs, HBM, scratch, operands, 0, "store", aliases)


def transform(leaves, send_slot, recv_slot, filter_up, filter_down):
    levels = send_slot.shape[0]
    rows = jnp.swapaxes(leaves, 1, 2)
    chains = [Chain(group[0], rows, send_slot) for group in GROUPS]
    for chain in chains:
        chain.swap()
    maps = jnp.concatenate([invert(send_slot), invert(recv_slot)], axis=0)
    bank = call(
        weight_kernel,
        shape(BANK, 640, dtype=bf16),
        [VMEM, VMEM],
        HBM,
        [pltpu.VMEM((BANK_USED, 640), bf16), DMA],
        (filter_up, filter_down),
        50_000_000,
        "weights",
        limit=FULL,
    )
    for chain in chains:
        chain.prepare(maps, bank)
    for height in range(levels - 1):
        for chain in chains:
            chain.up(height)
            chain.swap()
    height = levels - 1
    for chain in chains:
        chain.base()
        chain.top(height)
        chain.swap()
    result = None
    while True:
        for chain in chains:
            result = chain.store(height, result)
            if height > 0:
                chain.down(height - 1)
                chain.swap()
        if height == 0:
            break
        height -= 1
    return jnp.swapaxes(result, 1, 2)


def solution(mesh):
    in_specs = (P(None, None, "dev"), P(None, "dev"), P(None, "dev"), P(), P())
    out_specs = P(None, None, "dev")
    return jax.shard_map(transform, mesh=mesh, in_specs=in_specs, out_specs=out_specs, check_vma=False)
```

```python
import functools

import jax
import jax.numpy as jnp
from jax import lax
from jax.experimental import pallas as pl
from jax.experimental.pallas import tpu as pltpu
from jax.sharding import PartitionSpec as P

PER = 128
PARENTS = 16
DEGREE = 10
CELLS = 1000
PLANE = 100
SLOTS = 256
GROUPS = ((0, 1),)
COUNT = len(GROUPS[0])
HEIGHT = 8 * COUNT
ROWS = PARENTS
WIDE = COUNT * 20 * ROWS
LIMIT = 50_000_000
FULL = 63_400_000
TAKE = 0
PLACE = 4
UP_ROW, BOTH_ROW, DOWN_ROW, BOTH_PLANE, UP_PLANE, DOWN_PLANE, BANK_USED = (0, 160, 480, 800, 1312, 1824, 2080)
BANK = 5376
SPLITS = 10496
LEVEL_ROOM = 12 // COUNT
BASE_ROOM = 18 // COUNT

highest = lax.Precision.HIGHEST
f32 = jnp.float32
bf16 = jnp.bfloat16
VMEM = pl.BlockSpec(memory_space=pltpu.VMEM)
SMEM = pl.BlockSpec(memory_space=pltpu.SMEM)
HBM = pl.BlockSpec(memory_space=pltpu.HBM)
DMA = pltpu.SemaphoreType.DMA


def leaf_range(height):
    if height == 0:
        return (0, PER)
    return (PER + 7 * PARENTS * (height - 1), 7 * PARENTS)


def split(value):
    high = value.astype(bf16)
    return high, (value - high.astype(f32)).astype(bf16)


def dot(left, right):
    return jnp.dot(left, right, preferred_element_type=f32)


def windows(chunks):
    lane = lax.broadcasted_iota(jnp.int32, (ROWS, 128), 1)
    result = []
    for i in range(DEGREE):
        first, offset = divmod(PLANE * i, 128)
        value = chunks[first]
        if offset:
            value = pltpu.roll(value, 128 - offset, 1)
            if offset + PLANE > 128:
                later = pltpu.roll(chunks[first + 1], 128 - offset, 1)
                value = jnp.where(lane < 128 - offset, value, later)
        result.append(value)
    return result


def merge(parts):
    lane = lax.broadcasted_iota(jnp.int32, (ROWS, 128), 1)
    result = []
    for part in range(8):
        value = None
        for i in range(DEGREE):
            start = PLANE * i - 128 * part
            if start >= 128 or start + PLANE <= 0:
                continue
            piece = parts[i]
            if start % 128:
                piece = pltpu.roll(piece, start % 128, 1)
            if value is None:
                value = piece
            else:
                value = jnp.where(lane < start, value, piece)
        if part == 7:
            value = jnp.where(lane < CELLS - 896, value, 0.0)
        result.append(value)
    return result


def pack_rows(rows, start, number, flat_ref):
    for first in range(start, start + number, 8):
        for n in range(COUNT):
            for part in range(8):
                if part < 7:
                    value = rows[n, first : first + 8, 128 * part : 128 * part + 128]
                else:
                    value = rows[n, first : first + 8, 896:CELLS]
                    value = jnp.concatenate([value, jnp.zeros((8, 1024 - CELLS), f32)], axis=1)
                flat_ref[pl.ds(first * HEIGHT + n * 8 + part, 8, stride=HEIGHT), :] = value


def block(flat, index):
    return flat[index * HEIGHT : (index + 1) * HEIGHT, :]


def fetch(pairs, sems):
    copies = [pltpu.make_async_copy(source, target, sems.at[i]) for i, (source, target) in enumerate(pairs)]
    for copy in copies:
        copy.start()
    return copies


def first_kernel(orbital, send_ref, leaves_ref, out_ref, send, rows, flat, filled, sems):
    quarter = PER // 4
    pairs = [(send_ref, send)]
    for i in range(4):
        span = slice(i * quarter, (i + 1) * quarter)
        pairs.append((leaves_ref.at[orbital : orbital + COUNT, span, :], rows.at[:, span, :]))
    copies = fetch(pairs, sems)
    for i in range(4):
        copies[i + 1].wait()
        pack_rows(rows, i * quarter, quarter, flat)
    copies[0].wait()
    outs = []
    quarter = SLOTS // 4
    for i in range(4):
        for slot in range(i * quarter, (i + 1) * quarter):
            start = pl.multiple_of(jnp.minimum(send[0, slot], PER - 1) * HEIGHT, HEIGHT)
            filled[slot] = flat[pl.ds(start, HEIGHT), :]
        span = slice(i * quarter, (i + 1) * quarter)
        out = pltpu.make_async_copy(filled.at[span], out_ref.at[span], sems.at[5 + i])
        out.start()
        outs.append(out)
    for out in outs:
        out.wait()


def rest_kernel(orbital, maps, leaves_ref, out_ref, rows, flat, filled, sems):
    number = 7 * PARENTS
    pairs = []
    for i in range(3):
        span = slice(i * number, (i + 1) * number)
        source = leaves_ref.at[orbital : orbital + COUNT, PER + i * number : PER + (i + 1) * number, :]
        pairs.append((source, rows.at[:, span, :]))
    copies = fetch(pairs, sems)
    outs = []
    for i in range(3):
        copies[i].wait()
        pack_rows(rows, i * number, number, flat)
        for child in range(number):
            filled[i, maps[TAKE + i + 1, PARENTS + child]] = block(flat, i * number + child)
        out = pltpu.make_async_copy(filled.at[i], out_ref.at[i], sems.at[3 + i])
        out.start()
        outs.append(out)
    for out in outs:
        out.wait()


def one_hot(dims, axis, index):
    return (lax.broadcasted_iota(jnp.int32, dims, axis) == index).astype(f32)


def plane_index(dims, axis, size):
    position = lax.broadcasted_iota(jnp.int32, dims, axis)
    w, cell = (position >> 7, position & 127)
    j = (cell * 205) >> 11
    k = cell - DEGREE * j
    if size > DEGREE:
        j, k = (j + DEGREE * (w >> 1), k + DEGREE * (w & 1))
    dead = cell >= PLANE
    return jnp.where(dead, -1, j), jnp.where(dead, -1, k)


def exact(left, right, dims=((1,), (0,))):
    return lax.dot_general(left, right, (dims, ((), ())), precision=highest, preferred_element_type=f32)


def planes(filters, outs, ins):
    rows, columns = ((ins // DEGREE) ** 2 * 128, (outs // DEGREE) ** 2 * 128)
    factors = []
    for left, right in zip(plane_index((rows, ins), 0, ins), plane_index((outs, columns), 1, outs)):
        half = exact(one_hot((rows, ins), 1, left), filters, ((1,), (1,)))
        factors.append(exact(half, one_hot((outs, columns), 0, right)))
    return split(factors[0] * factors[1])


def spread(filters, outs, ins):
    rows, columns = (outs * ROWS, ins * ROWS)
    left = one_hot((rows, outs), 1, lax.broadcasted_iota(jnp.int32, (rows, outs), 0) >> 4)
    right = one_hot((ins, columns), 0, lax.broadcasted_iota(jnp.int32, (ins, columns), 1) >> 4)
    row = lax.broadcasted_iota(jnp.int32, (rows, columns), 0) & (ROWS - 1)
    column = lax.broadcasted_iota(jnp.int32, (rows, columns), 1) & (ROWS - 1)
    return split(jnp.where(row == column, exact(exact(left, filters), right), 0.0))


def weight_kernel(up_ref, down_ref, bank_ref, bank, sem):
    both = exact(down_ref[...], up_ref[...])
    up, down = (up_ref[0:DEGREE, :], down_ref[:, 0:DEGREE])
    sizes = ((UP_ROW, up, 10, 20), (BOTH_ROW, both, 20, 20), (DOWN_ROW, down, 20, 10))
    for start, filters, outs, ins in sizes:
        high, low = spread(filters, outs, ins)
        rows, depth = (outs * ROWS, ins * ROWS)
        for i, value in enumerate((high, high, low)):
            bank[start : start + rows, i * depth : (i + 1) * depth] = value
    high, low = planes(both, 20, 20)
    bank[BOTH_PLANE : BOTH_PLANE + 512, 0:512] = high
    bank[BOTH_PLANE : BOTH_PLANE + 512, 512:1024] = low
    high, low = planes(up, 10, 20)
    bank[UP_PLANE : UP_PLANE + 512, 0:128] = high
    bank[UP_PLANE : UP_PLANE + 512, 128:256] = low
    high, low = planes(down, 20, 10)
    bank[DOWN_PLANE : DOWN_PLANE + 128, 0:512] = high
    bank[DOWN_PLANE + 128 : DOWN_PLANE + 256, 0:512] = high
    bank[DOWN_PLANE : DOWN_PLANE + 128, 512:1024] = low
    copy = pltpu.make_async_copy(bank, bank_ref.at[0:BANK_USED, :], sem)
    copy.start()
    copy.wait()


def section(ref, start, rows, columns):
    return ref.at[start : start + rows, 0:columns]


def up_weights(bank_ref):
    return [section(bank_ref, UP_PLANE, 512, 256), section(bank_ref, UP_ROW, 160, 1024)]


def both_weights(bank_ref):
    return [section(bank_ref, BOTH_PLANE, 512, 1024), section(bank_ref, BOTH_ROW, 320, 1024)]


def down_weights(bank_ref):
    return [section(bank_ref, DOWN_PLANE, 256, 1024), section(bank_ref, DOWN_ROW, 320, 512)]


def stacked(value):
    high, low = split(value)
    return jnp.concatenate([high, low, high], axis=0)


def up_product(high, low, weights):
    plane, rows = weights
    wide = dot(high, plane[...])
    half = wide[:, 0:128] + (wide[:, 128:256] + dot(low, plane[:, 0:128]))
    depth = 20 * ROWS
    half = jnp.concatenate([half[n * depth : (n + 1) * depth] for n in range(COUNT)], axis=1)
    value = dot(rows[:, 0 : 3 * depth], stacked(half))
    return [value[:, n * 128 : (n + 1) * 128] for n in range(COUNT)]


def both_product(high, low, weights):
    plane, rows = weights
    half = dot(high, plane[:, 0:512]) + (dot(high, plane[:, 512:1024]) + dot(low, plane[:, 0:512]))
    depth = 20 * ROWS
    return [dot(rows[:, 0 : 3 * depth], stacked(half[n * depth : (n + 1) * depth])) for n in range(COUNT)]


def down_product(high, low, weights):
    plane, rows = weights
    half = dot(jnp.concatenate([high, low], axis=1), plane[:, 0:512]) + dot(high, plane[0:128, 512:1024])
    depth = DEGREE * ROWS
    return [dot(rows[:, 0 : 3 * depth], stacked(half[n * depth : (n + 1) * depth])) for n in range(COUNT)]


def split_children(splits_ref, height):
    return [section(splits_ref, (2 * height + i) * WIDE, WIDE, 512) for i in range(2)]


def window_octants(placed, high_ref, low_ref):
    for n in range(COUNT):
        for octant in range(8):
            first = (n * 8 + octant) * 8
            chunks = [placed[(first + part) * ROWS : (first + part + 1) * ROWS, :] for part in range(8)]
            x, w = divmod(octant, 4)
            for i, value in enumerate(windows(chunks)):
                high, low = split(value)
                start = (n * 20 + x * DEGREE + i) * ROWS
                high_ref[start : start + ROWS, w * 128 : w * 128 + 128] = high
                low_ref[start : start + ROWS, w * 128 : w * 128 + 128] = low


def place_children(height, maps, arrived_ref, placed):
    for child in range(PER):
        octant, parent = (child % 8, child // 8)
        slot = maps[PLACE + height, child]
        for n in range(COUNT):
            value = arrived_ref[slot, n * 8 : n * 8 + 8, :]
            placed[pl.ds((n * 8 + octant) * 8 * ROWS + parent, 8, stride=ROWS), :] = value


def up_kernel(height, arrived_ref, maps_ref, bank_ref, filled_ref, *rest):
    out_ref, kept_ref, maps, high, low, placed, blocks, v0, v1, sems = rest[-10:]
    weights = (v0, v1)
    pairs = [(maps_ref, maps)] + list(zip(up_weights(bank_ref), weights)) + [(filled_ref.at[height], out_ref)]
    copies = fetch(pairs, sems)
    copies[0].wait()
    place_children(height, maps, arrived_ref, placed)
    window_octants(placed, high, low)
    targets = split_children(kept_ref, height)
    outs = [pltpu.make_async_copy(high, targets[0], sems.at[4]), pltpu.make_async_copy(low, targets[1], sems.at[5])]
    for out in outs:
        out.start()
    for copy in copies[1:3]:
        copy.wait()
    values = up_product(high[...], low[...], weights)
    for n in range(COUNT):
        parts = [values[n][i * ROWS : (i + 1) * ROWS, :] for i in range(DEGREE)]
        for part, chunk in enumerate(merge(parts)):
            blocks[pl.ds(n * 8 + part, PARENTS, stride=HEIGHT), :] = chunk
    copies[3].wait()
    for child in range(PARENTS):
        out_ref[maps[TAKE + height + 1, child]] = block(blocks, child)
    for out in outs:
        out.wait()


def emit(height, maps, refined, blocks, out_ref):
    for octant in range(8):
        x, w = divmod(octant, 4)
        for n in range(COUNT):
            parts = []
            for i in range(DEGREE):
                start = (n * 20 + x * DEGREE + i) * ROWS
                parts.append(refined[start : start + ROWS, w * 128 : w * 128 + 128])
            for part, value in enumerate(merge(parts)):
                blocks[pl.ds(octant * HEIGHT + n * 8 + part, PARENTS, stride=8 * HEIGHT), :] = value
    for child in range(PER):
        out_ref[maps[PLACE + height, child]] = block(blocks, child)


def keep(refined, values):
    depth = WIDE // COUNT
    for n in range(COUNT):
        refined[n * depth : (n + 1) * depth, :] = values[n]


def top_kernel(height, arrived_ref, maps_ref, bank_ref, out_ref, *scratch):
    maps, high, low, placed, refined, blocks, v0, v1, sems = scratch
    weights = (v0, v1)
    copies = fetch([(maps_ref, maps)] + list(zip(both_weights(bank_ref), weights)), sems)
    copies[0].wait()
    place_children(height, maps, arrived_ref, placed)
    window_octants(placed, high, low)
    for copy in copies[1:]:
        copy.wait()
    keep(refined, both_product(high[...], low[...], weights))
    emit(height, maps, refined, blocks, out_ref)


def base_kernel(bank_ref, splits_ref, out_ref, *scratch):
    data, weights, refined, sems = (scratch[0:6], scratch[6:12], scratch[12], scratch[13])
    both, up, down = (weights[0:2], weights[2:4], weights[4:6])
    pairs = list(zip(both_weights(bank_ref) + up_weights(bank_ref) + down_weights(bank_ref), weights))
    for height in range(3):
        pairs += list(zip(split_children(splits_ref, height), data[2 * height : 2 * height + 2]))
    copies = fetch(pairs, sems)
    for copy in copies[:6]:
        copy.wait()
    outs = []
    for i in range(3):
        copies[6 + 2 * i].wait()
        copies[7 + 2 * i].wait()
        high, low = (data[2 * i][...], data[2 * i + 1][...])
        corner = jnp.concatenate(up_product(high, low, up), axis=0)
        inner = down_product(*split(corner), down)
        keep(refined.at[i], [whole - part for whole, part in zip(both_product(high, low, both), inner)])
        out = pltpu.make_async_copy(refined.at[i], out_ref.at[i], sems.at[12 + i])
        out.start()
        outs.append(out)
    for out in outs:
        out.wait()


def gather_leaves(height, first, maps, returned_ref, flat, rows, number):
    skip = PER - leaf_range(height)[1]
    for child in range(first, first + number):
        flat[child * HEIGHT : (child + 1) * HEIGHT, :] = returned_ref[maps[TAKE + height, child + skip]]
    for start in range(first, first + number, 8):
        for n in range(COUNT):
            for part in range(8):
                value = flat[pl.ds(start * HEIGHT + n * 8 + part, 8, stride=HEIGHT), :]
                if part < 7:
                    rows[n, start : start + 8, 128 * part : 128 * part + 128] = value
                else:
                    rows[n, start : start + 8, 896:CELLS] = value[:, : CELLS - 896]


def down_kernel(height, returned_ref, maps_ref, base_ref, bank_ref, *rest):
    out_ref, result_ref, maps, base, placed, high, low, refined, blocks, flat_leaves, rows, v0, v1, sems = rest[-14:]
    weights = (v0, v1)
    pairs = [(maps_ref, maps)] + list(zip(down_weights(bank_ref), weights)) + [(base_ref.at[height], base)]
    copies = fetch(pairs, sems)
    copies[0].wait()
    for child in range(PARENTS):
        slot = maps[TAKE + height + 1, child]
        for n in range(COUNT):
            placed[pl.ds(n * 8 * ROWS + child, 8, stride=ROWS), :] = returned_ref[slot, n * 8 : n * 8 + 8, :]
    for n in range(COUNT):
        chunks = [placed[(n * 8 + part) * ROWS : (n * 8 + part + 1) * ROWS, :] for part in range(8)]
        for i, value in enumerate(windows(chunks)):
            start = (n * DEGREE + i) * ROWS
            high[start : start + ROWS, :], low[start : start + ROWS, :] = split(value)
    start, number = leaf_range(height + 1)
    gather_leaves(height + 1, 0, maps, returned_ref, flat_leaves, rows, number)
    store = pltpu.make_async_copy(rows, result_ref.at[:, start : start + number, :], sems.at[4])
    store.start()
    for copy in copies[1:3]:
        copy.wait()
    values = down_product(high[...], low[...], weights)
    copies[3].wait()
    depth = WIDE // COUNT
    keep(refined, [base[n * depth : (n + 1) * depth, :] + values[n] for n in range(COUNT)])
    emit(height, maps, refined, blocks, out_ref)
    store.wait()


def store_kernel(returned_ref, maps_ref, _, out_ref, maps, flat, rows, sems):
    copy = fetch([(maps_ref, maps)], sems)[0]
    copy.wait()
    outs = []
    step = 32
    for first in range(0, PER, step):
        gather_leaves(0, first, maps, returned_ref, flat, rows, step)
        span = slice(first, first + step)
        out = pltpu.make_async_copy(rows.at[:, span, :], out_ref.at[:, span, :], sems.at[1 + first // step])
        out.start()
        outs.append(out)
    for out in outs:
        out.wait()


def shape(*dims, dtype=f32):
    return jax.ShapeDtypeStruct(dims, dtype)


def call(kernel, out_shape, in_specs, out_specs, scratch, operands, flops, name, aliases=None, limit=LIMIT):
    moved = sum(4 * one.size for one in operands)
    return pl.pallas_call(
        kernel,
        out_shape=out_shape,
        in_specs=in_specs,
        out_specs=out_specs,
        scratch_shapes=scratch,
        input_output_aliases=aliases or {},
        compiler_params=pltpu.CompilerParams(vmem_limit_bytes=limit),
        cost_estimate=pl.CostEstimate(flops=flops, bytes_accessed=moved, transcendentals=0),
        name=name,
    )(*operands)


def invert(mapping):
    match = mapping[:, None, :] == jnp.arange(PER, dtype=jnp.int32)[None, :, None]
    return jnp.sum(jnp.where(match, jnp.arange(mapping.shape[1], dtype=jnp.int32)[None, None, :], 0), axis=2)


def exchange(blocks):
    return lax.all_to_all(blocks, "dev", split_axis=0, concat_axis=0, tiled=True)


def flat(number):
    return pltpu.VMEM((number * HEIGHT, 128), f32)


def halves(*dims):
    return [pltpu.VMEM(one, bf16) for one in dims for _ in range(2)]


def single(*dims):
    return [pltpu.VMEM(one, bf16) for one in dims]


class Chain:
    def __init__(self, orbital, rows, send_slot):
        self.orbital = orbital
        self.rows = rows
        self.slots = shape(SLOTS, HEIGHT, 128)
        self.placed = pltpu.VMEM((COUNT * 8 * 8 * ROWS, 128), f32)
        self.going = call(
            functools.partial(first_kernel, orbital),
            self.slots,
            [HBM, HBM],
            HBM,
            [pltpu.SMEM(send_slot.shape, jnp.int32), pltpu.VMEM((COUNT, PER, CELLS), f32), flat(PER)]
            + [pltpu.VMEM((SLOTS, HEIGHT, 128), f32), DMA((9,))],
            (send_slot, rows),
            0,
            "pack_first",
            limit=FULL,
        )

    def swap(self):
        self.arrived = exchange(self.going)

    def prepare(self, maps, bank):
        self.maps, self.bank = (maps, bank)
        self.maps_smem = pltpu.SMEM(maps.shape, jnp.int32)
        self.filled = call(
            functools.partial(rest_kernel, self.orbital),
            shape(LEVEL_ROOM, SLOTS, HEIGHT, 128),
            [SMEM, HBM],
            HBM,
            [pltpu.VMEM((COUNT, 336, CELLS), f32), flat(336), pltpu.VMEM((3, SLOTS, HEIGHT, 128), f32), DMA((6,))],
            (maps, self.rows),
            0,
            "pack_rest",
            limit=FULL,
        )
        self.splits = None

    def up(self, height):
        weights = single((512, 256), (160, 1024))
        scratch = [self.maps_smem] + halves((WIDE, 512)) + [self.placed, flat(PARENTS)] + weights + [DMA((6,))]
        operands = (self.arrived, self.maps, self.bank, self.filled)
        aliases = {}
        if self.splits is not None:
            operands += (self.splits,)
            aliases[4] = 1
        self.going, self.splits = call(
            functools.partial(up_kernel, height),
            (self.slots, shape(SPLITS, 512, dtype=bf16)),
            [VMEM] + [HBM] * (len(operands) - 1),
            (VMEM, HBM),
            scratch,
            operands,
            300_000_000,
            "up",
            aliases,
        )

    def base(self):
        self.bases = call(
            base_kernel,
            shape(BASE_ROOM, WIDE, 512),
            [HBM, HBM],
            HBM,
            halves((WIDE, 512)) * 3
            + single((512, 1024), (320, 1024), (512, 256), (160, 1024), (256, 1024), (320, 512))
            + [pltpu.VMEM((3, WIDE, 512), f32), DMA((15,))],
            (self.bank, self.splits),
            3_600_000_000,
            "base",
            limit=FULL,
        )

    def top(self, height):
        scratch = [self.maps_smem] + halves((WIDE, 512)) + [self.placed, pltpu.VMEM((WIDE, 512), f32), flat(PER)]
        scratch += single((512, 1024), (320, 1024)) + [DMA((3,))]
        self.going = call(
            functools.partial(top_kernel, height),
            self.slots,
            [VMEM, HBM, HBM],
            VMEM,
            scratch,
            (self.arrived, self.maps, self.bank),
            1_200_000_000,
            "top",
        )

    def down(self, height, result):
        number = leaf_range(height + 1)[1]
        scratch = [self.maps_smem, pltpu.VMEM((WIDE, 512), f32), pltpu.VMEM((COUNT * 8 * ROWS, 128), f32)]
        scratch += halves((WIDE // 2, 128)) + [pltpu.VMEM((WIDE, 512), f32), flat(PER)]
        scratch += [flat(number), pltpu.VMEM((COUNT, number, CELLS), f32)]
        scratch += single((256, 1024), (320, 512)) + [DMA((5,))]
        operands = (self.arrived, self.maps, self.bases, self.bank)
        if result is not None:
            operands += (result,)
        self.going, result = call(
            functools.partial(down_kernel, height),
            (self.slots, shape(2, PER + 336, CELLS)),
            [VMEM] + [HBM] * (len(operands) - 1),
            (VMEM, HBM),
            scratch,
            operands,
            400_000_000,
            "down",
            None if result is None else {4: 1},
        )
        return result

    def store(self, result):
        return call(
            store_kernel,
            shape(*result.shape),
            [VMEM, HBM, HBM],
            HBM,
            [self.maps_smem, flat(PER), pltpu.VMEM((COUNT, PER, CELLS), f32), DMA((5,))],
            (self.arrived, self.maps, result),
            0,
            "store",
            {2: 0},
        )


def transform(leaves, send_slot, recv_slot, filter_up, filter_down):
    levels = send_slot.shape[0]
    rows = jnp.swapaxes(leaves, 1, 2)
    chains = [Chain(group[0], rows, send_slot) for group in GROUPS]
    for chain in chains:
        chain.swap()
    maps = jnp.concatenate([invert(send_slot), invert(recv_slot)], axis=0)
    bank = call(
        weight_kernel,
        shape(BANK, 1024, dtype=bf16),
        [VMEM, VMEM],
        HBM,
        [pltpu.VMEM((BANK_USED, 1024), bf16), DMA],
        (filter_up, filter_down),
        50_000_000,
        "weights",
        limit=FULL,
    )
    for chain in chains:
        chain.prepare(maps, bank)
    for height in range(levels - 1):
        for chain in chains:
            chain.up(height)
            chain.swap()
    height = levels - 1
    for chain in chains:
        chain.base()
        chain.top(height)
        chain.swap()
    result = None
    for height in reversed(range(levels - 1)):
        for chain in chains:
            result = chain.down(height, result)
            chain.swap()
    for chain in chains:
        result = chain.store(result)
    return jnp.swapaxes(result, 1, 2)


def solution(mesh):
    in_specs = (P(None, None, "dev"), P(None, "dev"), P(None, "dev"), P(), P())
    out_specs = P(None, None, "dev")
    return jax.shard_map(transform, mesh=mesh, in_specs=in_specs, out_specs=out_specs, check_vma=False)
```

```python
import functools

import jax
import jax.numpy as jnp
from jax import lax
from jax.experimental import pallas as pl
from jax.experimental.pallas import tpu as pltpu
from jax.sharding import PartitionSpec as P

PER = 128
PARENTS = 16
DEGREE = 10
CELLS = 1000
PLANE = 100
SLOTS = 256
GROUPS = ((0, 1),)
COUNT = len(GROUPS[0])
HEIGHT = 8 * COUNT
ROWS = PARENTS
WIDE = COUNT * 20 * ROWS
LIMIT = 50_000_000
FULL = 63_400_000
TAKE = 0
PLACE = 4
UP_ROW, BOTH_ROW, DOWN_ROW, BOTH_PLANE, UP_PLANE, DOWN_PLANE, BANK_USED = (0, 160, 480, 800, 1312, 1824, 2080)
BANK = 5376
SPLITS = 10496
LEVEL_ROOM = 12 // COUNT
BASE_ROOM = 18 // COUNT

highest = lax.Precision.HIGHEST
f32 = jnp.float32
bf16 = jnp.bfloat16
VMEM = pl.BlockSpec(memory_space=pltpu.VMEM)
SMEM = pl.BlockSpec(memory_space=pltpu.SMEM)
HBM = pl.BlockSpec(memory_space=pltpu.HBM)
DMA = pltpu.SemaphoreType.DMA


def leaf_range(height):
    if height == 0:
        return (0, PER)
    return (PER + 7 * PARENTS * (height - 1), 7 * PARENTS)


def split(value):
    high = value.astype(bf16)
    return high, (value - high.astype(f32)).astype(bf16)


def dot(left, right):
    return jnp.dot(left, right, preferred_element_type=f32)


def windows(chunks):
    lane = lax.broadcasted_iota(jnp.int32, (ROWS, 128), 1)
    result = []
    for i in range(DEGREE):
        first, offset = divmod(PLANE * i, 128)
        value = chunks[first]
        if offset:
            value = pltpu.roll(value, 128 - offset, 1)
            if offset + PLANE > 128:
                later = pltpu.roll(chunks[first + 1], 128 - offset, 1)
                value = jnp.where(lane < 128 - offset, value, later)
        result.append(value)
    return result


def merge(parts):
    lane = lax.broadcasted_iota(jnp.int32, (ROWS, 128), 1)
    result = []
    for part in range(8):
        value = None
        for i in range(DEGREE):
            start = PLANE * i - 128 * part
            if start >= 128 or start + PLANE <= 0:
                continue
            piece = parts[i]
            if start % 128:
                piece = pltpu.roll(piece, start % 128, 1)
            if value is None:
                value = piece
            else:
                value = jnp.where(lane < start, value, piece)
        if part == 7:
            value = jnp.where(lane < CELLS - 896, value, 0.0)
        result.append(value)
    return result


def pack_rows(rows, start, number, flat_ref):
    for first in range(start, start + number, 8):
        for n in range(COUNT):
            for part in range(8):
                if part < 7:
                    value = rows[n, first : first + 8, 128 * part : 128 * part + 128]
                else:
                    value = rows[n, first : first + 8, 896:CELLS]
                    value = jnp.concatenate([value, jnp.zeros((8, 1024 - CELLS), f32)], axis=1)
                flat_ref[pl.ds(first * HEIGHT + n * 8 + part, 8, stride=HEIGHT), :] = value


def block(flat, index):
    return flat[index * HEIGHT : (index + 1) * HEIGHT, :]


def fetch(pairs, sems):
    copies = [pltpu.make_async_copy(source, target, sems.at[i]) for i, (source, target) in enumerate(pairs)]
    for copy in copies:
        copy.start()
    return copies


def first_kernel(orbital, send_ref, leaves_ref, out_ref, send, rows, flat, filled, sems):
    quarter = PER // 4
    pairs = [(send_ref, send)]
    for i in range(4):
        span = slice(i * quarter, (i + 1) * quarter)
        pairs.append((leaves_ref.at[orbital : orbital + COUNT, span, :], rows.at[:, span, :]))
    copies = fetch(pairs, sems)
    for i in range(4):
        copies[i + 1].wait()
        pack_rows(rows, i * quarter, quarter, flat)
    copies[0].wait()
    outs = []
    quarter = SLOTS // 4
    for i in range(4):
        for slot in range(i * quarter, (i + 1) * quarter):
            start = pl.multiple_of(jnp.minimum(send[0, slot], PER - 1) * HEIGHT, HEIGHT)
            filled[slot] = flat[pl.ds(start, HEIGHT), :]
        span = slice(i * quarter, (i + 1) * quarter)
        out = pltpu.make_async_copy(filled.at[span], out_ref.at[span], sems.at[5 + i])
        out.start()
        outs.append(out)
    for out in outs:
        out.wait()


def rest_kernel(orbital, maps, leaves_ref, out_ref, rows, flat, filled, sems):
    number = 7 * PARENTS
    pairs = []
    for i in range(3):
        span = slice(i * number, (i + 1) * number)
        source = leaves_ref.at[orbital : orbital + COUNT, PER + i * number : PER + (i + 1) * number, :]
        pairs.append((source, rows.at[:, span, :]))
    copies = fetch(pairs, sems)
    outs = []
    for i in range(3):
        copies[i].wait()
        pack_rows(rows, i * number, number, flat)
        for child in range(number):
            filled[i, maps[TAKE + i + 1, PARENTS + child]] = block(flat, i * number + child)
        out = pltpu.make_async_copy(filled.at[i], out_ref.at[i], sems.at[3 + i])
        out.start()
        outs.append(out)
    for out in outs:
        out.wait()


def one_hot(dims, axis, index):
    return (lax.broadcasted_iota(jnp.int32, dims, axis) == index).astype(f32)


def plane_index(dims, axis, size):
    position = lax.broadcasted_iota(jnp.int32, dims, axis)
    w, cell = (position >> 7, position & 127)
    j = (cell * 205) >> 11
    k = cell - DEGREE * j
    if size > DEGREE:
        j, k = (j + DEGREE * (w >> 1), k + DEGREE * (w & 1))
    dead = cell >= PLANE
    return jnp.where(dead, -1, j), jnp.where(dead, -1, k)


def exact(left, right, dims=((1,), (0,))):
    return lax.dot_general(left, right, (dims, ((), ())), precision=highest, preferred_element_type=f32)


def planes(filters, outs, ins):
    rows, columns = ((ins // DEGREE) ** 2 * 128, (outs // DEGREE) ** 2 * 128)
    factors = []
    for left, right in zip(plane_index((rows, ins), 0, ins), plane_index((outs, columns), 1, outs)):
        half = exact(one_hot((rows, ins), 1, left), filters, ((1,), (1,)))
        factors.append(exact(half, one_hot((outs, columns), 0, right)))
    return split(factors[0] * factors[1])


def spread(filters, outs, ins):
    rows, columns = (outs * ROWS, ins * ROWS)
    left = one_hot((rows, outs), 1, lax.broadcasted_iota(jnp.int32, (rows, outs), 0) >> 4)
    right = one_hot((ins, columns), 0, lax.broadcasted_iota(jnp.int32, (ins, columns), 1) >> 4)
    row = lax.broadcasted_iota(jnp.int32, (rows, columns), 0) & (ROWS - 1)
    column = lax.broadcasted_iota(jnp.int32, (rows, columns), 1) & (ROWS - 1)
    return split(jnp.where(row == column, exact(exact(left, filters), right), 0.0))


def weight_kernel(up_ref, down_ref, bank_ref, bank, sem):
    both = exact(down_ref[...], up_ref[...])
    up, down = (up_ref[0:DEGREE, :], down_ref[:, 0:DEGREE])
    sizes = ((UP_ROW, up, 10, 20), (BOTH_ROW, both, 20, 20), (DOWN_ROW, down, 20, 10))
    for start, filters, outs, ins in sizes:
        high, low = spread(filters, outs, ins)
        rows, depth = (outs * ROWS, ins * ROWS)
        for i, value in enumerate((high, high, low)):
            bank[start : start + rows, i * depth : (i + 1) * depth] = value
    high, low = planes(both, 20, 20)
    bank[BOTH_PLANE : BOTH_PLANE + 512, 0:512] = high
    bank[BOTH_PLANE : BOTH_PLANE + 512, 512:1024] = low
    high, low = planes(up, 10, 20)
    bank[UP_PLANE : UP_PLANE + 512, 0:128] = high
    bank[UP_PLANE : UP_PLANE + 512, 128:256] = low
    high, low = planes(down, 20, 10)
    bank[DOWN_PLANE : DOWN_PLANE + 128, 0:512] = high
    bank[DOWN_PLANE + 128 : DOWN_PLANE + 256, 0:512] = high
    bank[DOWN_PLANE : DOWN_PLANE + 128, 512:1024] = low
    copy = pltpu.make_async_copy(bank, bank_ref.at[0:BANK_USED, :], sem)
    copy.start()
    copy.wait()


def section(ref, start, rows, columns):
    return ref.at[start : start + rows, 0:columns]


def up_weights(bank_ref):
    return [section(bank_ref, UP_PLANE, 512, 256), section(bank_ref, UP_ROW, 160, 1024)]


def both_weights(bank_ref):
    return [section(bank_ref, BOTH_PLANE, 512, 1024), section(bank_ref, BOTH_ROW, 320, 1024)]


def down_weights(bank_ref):
    return [section(bank_ref, DOWN_PLANE, 256, 1024), section(bank_ref, DOWN_ROW, 320, 512)]


def stacked(value):
    high, low = split(value)
    return jnp.concatenate([high, low, high], axis=0)


def up_product(high, low, weights):
    plane, rows = weights
    wide = dot(high, plane[...])
    half = wide[:, 0:128] + (wide[:, 128:256] + dot(low, plane[:, 0:128]))
    depth = 20 * ROWS
    half = jnp.concatenate([half[n * depth : (n + 1) * depth] for n in range(COUNT)], axis=1)
    value = dot(rows[:, 0 : 3 * depth], stacked(half))
    return [value[:, n * 128 : (n + 1) * 128] for n in range(COUNT)]


def both_product(high, low, weights):
    plane, rows = weights
    half = dot(high, plane[:, 0:512]) + (dot(high, plane[:, 512:1024]) + dot(low, plane[:, 0:512]))
    depth = 20 * ROWS
    return [dot(rows[:, 0 : 3 * depth], stacked(half[n * depth : (n + 1) * depth])) for n in range(COUNT)]


def down_product(high, low, weights):
    plane, rows = weights
    half = dot(jnp.concatenate([high, low], axis=1), plane[:, 0:512]) + dot(high, plane[0:128, 512:1024])
    depth = DEGREE * ROWS
    return [dot(rows[:, 0 : 3 * depth], stacked(half[n * depth : (n + 1) * depth])) for n in range(COUNT)]


def split_children(splits_ref, height):
    return [section(splits_ref, (2 * height + i) * WIDE, WIDE, 512) for i in range(2)]


def window_octants(placed, high_ref, low_ref):
    for n in range(COUNT):
        for octant in range(8):
            first = (n * 8 + octant) * 8
            chunks = [placed[(first + part) * ROWS : (first + part + 1) * ROWS, :] for part in range(8)]
            x, w = divmod(octant, 4)
            for i, value in enumerate(windows(chunks)):
                high, low = split(value)
                start = (n * 20 + x * DEGREE + i) * ROWS
                high_ref[start : start + ROWS, w * 128 : w * 128 + 128] = high
                low_ref[start : start + ROWS, w * 128 : w * 128 + 128] = low


def place_children(height, maps, arrived_ref, placed):
    for child in range(PER):
        octant, parent = (child % 8, child // 8)
        slot = maps[PLACE + height, child]
        for n in range(COUNT):
            value = arrived_ref[slot, n * 8 : n * 8 + 8, :]
            placed[pl.ds((n * 8 + octant) * 8 * ROWS + parent, 8, stride=ROWS), :] = value


def up_kernel(height, arrived_ref, maps_ref, bank_ref, filled_ref, *rest):
    out_ref, kept_ref, maps, high, low, placed, blocks, v0, v1, sems = rest[-10:]
    weights = (v0, v1)
    pairs = [(maps_ref, maps)] + list(zip(up_weights(bank_ref), weights)) + [(filled_ref.at[height], out_ref)]
    copies = fetch(pairs, sems)
    copies[0].wait()
    place_children(height, maps, arrived_ref, placed)
    window_octants(placed, high, low)
    targets = split_children(kept_ref, height)
    outs = [pltpu.make_async_copy(high, targets[0], sems.at[4]), pltpu.make_async_copy(low, targets[1], sems.at[5])]
    for out in outs:
        out.start()
    for copy in copies[1:3]:
        copy.wait()
    values = up_product(high[...], low[...], weights)
    for n in range(COUNT):
        parts = [values[n][i * ROWS : (i + 1) * ROWS, :] for i in range(DEGREE)]
        for part, chunk in enumerate(merge(parts)):
            blocks[pl.ds(n * 8 + part, PARENTS, stride=HEIGHT), :] = chunk
    copies[3].wait()
    for child in range(PARENTS):
        out_ref[maps[TAKE + height + 1, child]] = block(blocks, child)
    for out in outs:
        out.wait()


def emit(height, maps, refined, blocks, out_ref):
    for octant in range(8):
        x, w = divmod(octant, 4)
        for n in range(COUNT):
            parts = []
            for i in range(DEGREE):
                start = (n * 20 + x * DEGREE + i) * ROWS
                parts.append(refined[start : start + ROWS, w * 128 : w * 128 + 128])
            for part, value in enumerate(merge(parts)):
                blocks[pl.ds(octant * HEIGHT + n * 8 + part, PARENTS, stride=8 * HEIGHT), :] = value
    for child in range(PER):
        out_ref[maps[PLACE + height, child]] = block(blocks, child)


def keep(refined, values):
    depth = WIDE // COUNT
    for n in range(COUNT):
        refined[n * depth : (n + 1) * depth, :] = values[n]


def top_kernel(height, arrived_ref, maps_ref, bank_ref, out_ref, *scratch):
    maps, high, low, placed, refined, blocks, v0, v1, sems = scratch
    weights = (v0, v1)
    copies = fetch([(maps_ref, maps)] + list(zip(both_weights(bank_ref), weights)), sems)
    copies[0].wait()
    place_children(height, maps, arrived_ref, placed)
    window_octants(placed, high, low)
    for copy in copies[1:]:
        copy.wait()
    keep(refined, both_product(high[...], low[...], weights))
    emit(height, maps, refined, blocks, out_ref)


def base_kernel(bank_ref, splits_ref, out_ref, *scratch):
    data, weights, refined, sems = (scratch[0:6], scratch[6:12], scratch[12], scratch[13])
    both, up, down = (weights[0:2], weights[2:4], weights[4:6])
    pairs = list(zip(both_weights(bank_ref) + up_weights(bank_ref) + down_weights(bank_ref), weights))
    for height in range(3):
        pairs += list(zip(split_children(splits_ref, height), data[2 * height : 2 * height + 2]))
    copies = fetch(pairs, sems)
    for copy in copies[:6]:
        copy.wait()
    outs = []
    for i in range(3):
        copies[6 + 2 * i].wait()
        copies[7 + 2 * i].wait()
        high, low = (data[2 * i][...], data[2 * i + 1][...])
        corner = jnp.concatenate(up_product(high, low, up), axis=0)
        inner = down_product(*split(corner), down)
        keep(refined.at[i], [whole - part for whole, part in zip(both_product(high, low, both), inner)])
        out = pltpu.make_async_copy(refined.at[i], out_ref.at[i], sems.at[12 + i])
        out.start()
        outs.append(out)
    for out in outs:
        out.wait()


def gather_leaves(height, first, maps, returned_ref, flat, rows, number):
    skip = PER - leaf_range(height)[1]
    for child in range(first, first + number):
        flat[child * HEIGHT : (child + 1) * HEIGHT, :] = returned_ref[maps[TAKE + height, child + skip]]
    for start in range(first, first + number, 8):
        for n in range(COUNT):
            for part in range(8):
                value = flat[pl.ds(start * HEIGHT + n * 8 + part, 8, stride=HEIGHT), :]
                if part < 7:
                    rows[n, start : start + 8, 128 * part : 128 * part + 128] = value
                else:
                    rows[n, start : start + 8, 896:CELLS] = value[:, : CELLS - 896]


def down_kernel(height, returned_ref, maps_ref, base_ref, bank_ref, *rest):
    out_ref, result_ref, maps, base, placed, high, low, refined, blocks, flat_leaves, rows, v0, v1, sems = rest[-14:]
    weights = (v0, v1)
    pairs = [(maps_ref, maps)] + list(zip(down_weights(bank_ref), weights)) + [(base_ref.at[height], base)]
    copies = fetch(pairs, sems)
    copies[0].wait()
    for child in range(PARENTS):
        slot = maps[TAKE + height + 1, child]
        for n in range(COUNT):
            placed[pl.ds(n * 8 * ROWS + child, 8, stride=ROWS), :] = returned_ref[slot, n * 8 : n * 8 + 8, :]
    for n in range(COUNT):
        chunks = [placed[(n * 8 + part) * ROWS : (n * 8 + part + 1) * ROWS, :] for part in range(8)]
        for i, value in enumerate(windows(chunks)):
            start = (n * DEGREE + i) * ROWS
            high[start : start + ROWS, :], low[start : start + ROWS, :] = split(value)
    start, number = leaf_range(height + 1)
    gather_leaves(height + 1, 0, maps, returned_ref, flat_leaves, rows, number)
    store = pltpu.make_async_copy(rows, result_ref.at[:, start : start + number, :], sems.at[4])
    store.start()
    for copy in copies[1:3]:
        copy.wait()
    values = down_product(high[...], low[...], weights)
    copies[3].wait()
    depth = WIDE // COUNT
    keep(refined, [base[n * depth : (n + 1) * depth, :] + values[n] for n in range(COUNT)])
    emit(height, maps, refined, blocks, out_ref)
    store.wait()


def store_kernel(returned_ref, maps_ref, _, out_ref, maps, flat, rows, sems):
    copy = fetch([(maps_ref, maps)], sems)[0]
    copy.wait()
    outs = []
    step = 32
    for first in range(0, PER, step):
        gather_leaves(0, first, maps, returned_ref, flat, rows, step)
        span = slice(first, first + step)
        out = pltpu.make_async_copy(rows.at[:, span, :], out_ref.at[:, span, :], sems.at[1 + first // step])
        out.start()
        outs.append(out)
    for out in outs:
        out.wait()


def shape(*dims, dtype=f32):
    return jax.ShapeDtypeStruct(dims, dtype)


def call(kernel, out_shape, in_specs, out_specs, scratch, operands, flops, name, aliases=None, limit=LIMIT):
    moved = sum(4 * one.size for one in operands)
    return pl.pallas_call(
        kernel,
        out_shape=out_shape,
        in_specs=in_specs,
        out_specs=out_specs,
        scratch_shapes=scratch,
        input_output_aliases=aliases or {},
        compiler_params=pltpu.CompilerParams(vmem_limit_bytes=limit),
        cost_estimate=pl.CostEstimate(flops=flops, bytes_accessed=moved, transcendentals=0),
        name=name,
    )(*operands)


def invert(mapping):
    match = mapping[:, None, :] == jnp.arange(PER, dtype=jnp.int32)[None, :, None]
    return jnp.sum(jnp.where(match, jnp.arange(mapping.shape[1], dtype=jnp.int32)[None, None, :], 0), axis=2)


def exchange(blocks):
    size = lax.axis_size("dev")
    groups = [list(range(core, size, 2)) for core in range(2)]
    other = 1 - lax.axis_index("dev") % 2
    crossed = lax.all_to_all(blocks, "dev", split_axis=0, concat_axis=0, axis_index_groups=groups, tiled=True)
    crossed = crossed.reshape(size // 2, 2, 2, HEIGHT, 128)
    given = lax.dynamic_index_in_dim(crossed, other, axis=1)
    taken = lax.ppermute(given, "dev", [(i, i ^ 1) for i in range(size)])
    joined = lax.dynamic_update_slice_in_dim(crossed, taken, other, axis=1)
    return joined.reshape(blocks.shape)


def flat(number):
    return pltpu.VMEM((number * HEIGHT, 128), f32)


def halves(*dims):
    return [pltpu.VMEM(one, bf16) for one in dims for _ in range(2)]


def single(*dims):
    return [pltpu.VMEM(one, bf16) for one in dims]


class Chain:
    def __init__(self, orbital, rows, send_slot):
        self.orbital = orbital
        self.rows = rows
        self.slots = shape(SLOTS, HEIGHT, 128)
        self.placed = pltpu.VMEM((COUNT * 8 * 8 * ROWS, 128), f32)
        self.going = call(
            functools.partial(first_kernel, orbital),
            self.slots,
            [HBM, HBM],
            HBM,
            [pltpu.SMEM(send_slot.shape, jnp.int32), pltpu.VMEM((COUNT, PER, CELLS), f32), flat(PER)]
            + [pltpu.VMEM((SLOTS, HEIGHT, 128), f32), DMA((9,))],
            (send_slot, rows),
            0,
            "pack_first",
            limit=FULL,
        )

    def swap(self):
        self.arrived = exchange(self.going)

    def prepare(self, maps, bank):
        self.maps, self.bank = (maps, bank)
        self.maps_smem = pltpu.SMEM(maps.shape, jnp.int32)
        self.filled = call(
            functools.partial(rest_kernel, self.orbital),
            shape(LEVEL_ROOM, SLOTS, HEIGHT, 128),
            [SMEM, HBM],
            HBM,
            [pltpu.VMEM((COUNT, 336, CELLS), f32), flat(336), pltpu.VMEM((3, SLOTS, HEIGHT, 128), f32), DMA((6,))],
            (maps, self.rows),
            0,
            "pack_rest",
            limit=FULL,
        )
        self.splits = None

    def up(self, height):
        weights = single((512, 256), (160, 1024))
        scratch = [self.maps_smem] + halves((WIDE, 512)) + [self.placed, flat(PARENTS)] + weights + [DMA((6,))]
        operands = (self.arrived, self.maps, self.bank, self.filled)
        aliases = {}
        if self.splits is not None:
            operands += (self.splits,)
            aliases[4] = 1
        self.going, self.splits = call(
            functools.partial(up_kernel, height),
            (self.slots, shape(SPLITS, 512, dtype=bf16)),
            [VMEM] + [HBM] * (len(operands) - 1),
            (VMEM, HBM),
            scratch,
            operands,
            300_000_000,
            "up",
            aliases,
        )

    def base(self):
        self.bases = call(
            base_kernel,
            shape(BASE_ROOM, WIDE, 512),
            [HBM, HBM],
            HBM,
            halves((WIDE, 512)) * 3
            + single((512, 1024), (320, 1024), (512, 256), (160, 1024), (256, 1024), (320, 512))
            + [pltpu.VMEM((3, WIDE, 512), f32), DMA((15,))],
            (self.bank, self.splits),
            3_600_000_000,
            "base",
            limit=FULL,
        )

    def top(self, height):
        scratch = [self.maps_smem] + halves((WIDE, 512)) + [self.placed, pltpu.VMEM((WIDE, 512), f32), flat(PER)]
        scratch += single((512, 1024), (320, 1024)) + [DMA((3,))]
        self.going = call(
            functools.partial(top_kernel, height),
            self.slots,
            [VMEM, HBM, HBM],
            VMEM,
            scratch,
            (self.arrived, self.maps, self.bank),
            1_200_000_000,
            "top",
        )

    def down(self, height, result):
        number = leaf_range(height + 1)[1]
        scratch = [self.maps_smem, pltpu.VMEM((WIDE, 512), f32), pltpu.VMEM((COUNT * 8 * ROWS, 128), f32)]
        scratch += halves((WIDE // 2, 128)) + [pltpu.VMEM((WIDE, 512), f32), flat(PER)]
        scratch += [flat(number), pltpu.VMEM((COUNT, number, CELLS), f32)]
        scratch += single((256, 1024), (320, 512)) + [DMA((5,))]
        operands = (self.arrived, self.maps, self.bases, self.bank)
        if result is not None:
            operands += (result,)
        self.going, result = call(
            functools.partial(down_kernel, height),
            (self.slots, shape(2, PER + 336, CELLS)),
            [VMEM] + [HBM] * (len(operands) - 1),
            (VMEM, HBM),
            scratch,
            operands,
            400_000_000,
            "down",
            None if result is None else {4: 1},
        )
        return result

    def store(self, result):
        return call(
            store_kernel,
            shape(*result.shape),
            [VMEM, HBM, HBM],
            HBM,
            [self.maps_smem, flat(PER), pltpu.VMEM((COUNT, PER, CELLS), f32), DMA((5,))],
            (self.arrived, self.maps, result),
            0,
            "store",
            {2: 0},
        )


def transform(leaves, send_slot, recv_slot, filter_up, filter_down):
    levels = send_slot.shape[0]
    rows = jnp.swapaxes(leaves, 1, 2)
    chains = [Chain(group[0], rows, send_slot) for group in GROUPS]
    for chain in chains:
        chain.swap()
    maps = jnp.concatenate([invert(send_slot), invert(recv_slot)], axis=0)
    bank = call(
        weight_kernel,
        shape(BANK, 1024, dtype=bf16),
        [VMEM, VMEM],
        HBM,
        [pltpu.VMEM((BANK_USED, 1024), bf16), DMA],
        (filter_up, filter_down),
        50_000_000,
        "weights",
        limit=FULL,
    )
    for chain in chains:
        chain.prepare(maps, bank)
    for height in range(levels - 1):
        for chain in chains:
            chain.up(height)
            chain.swap()
    height = levels - 1
    for chain in chains:
        chain.base()
        chain.top(height)
        chain.swap()
    result = None
    for height in reversed(range(levels - 1)):
        for chain in chains:
            result = chain.down(height, result)
            chain.swap()
    for chain in chains:
        result = chain.store(result)
    return jnp.swapaxes(result, 1, 2)


def solution(mesh):
    in_specs = (P(None, None, "dev"), P(None, "dev"), P(None, "dev"), P(), P())
    out_specs = P(None, None, "dev")
    return jax.shard_map(transform, mesh=mesh, in_specs=in_specs, out_specs=out_specs, check_vma=False)
```

```python
import functools

import jax
import jax.numpy as jnp
import numpy as np
from jax import lax
from jax.experimental import pallas as pl
from jax.experimental.pallas import tpu as pltpu
from jax.sharding import PartitionSpec as P

PER = 128
PARENTS = 16
DEGREE = 10
CELLS = 1000
PLANE = 100
SLOTS = 256
DEVICES = 128
ORDER = [59 * position % DEVICES for position in range(DEVICES)]
SLOT_ORDER = [2 * device + r for device in ORDER for r in range(2)]
POSITION = np.argsort(SLOT_ORDER).astype(np.int32)
GROUPS = ((0, 1),)
COUNT = len(GROUPS[0])
HEIGHT = 8 * COUNT
ROWS = PARENTS
WIDE = COUNT * 20 * ROWS
LIMIT = 50_000_000
FULL = 63_400_000
TAKE = 0
PLACE = 4
UP_ROW, BOTH_ROW, DOWN_ROW, BOTH_PLANE, UP_PLANE, DOWN_PLANE, BANK_USED = (0, 160, 480, 800, 1312, 1824, 2080)
BANK = 5376
SPLITS = 10496
LEVEL_ROOM = 12 // COUNT
BASE_ROOM = 18 // COUNT

highest = lax.Precision.HIGHEST
f32 = jnp.float32
bf16 = jnp.bfloat16
VMEM = pl.BlockSpec(memory_space=pltpu.VMEM)
SMEM = pl.BlockSpec(memory_space=pltpu.SMEM)
HBM = pl.BlockSpec(memory_space=pltpu.HBM)
DMA = pltpu.SemaphoreType.DMA


def leaf_range(height):
    if height == 0:
        return (0, PER)
    return (PER + 7 * PARENTS * (height - 1), 7 * PARENTS)


def split(value):
    high = value.astype(bf16)
    return high, (value - high.astype(f32)).astype(bf16)


def dot(left, right):
    return jnp.dot(left, right, preferred_element_type=f32)


def windows(chunks):
    lane = lax.broadcasted_iota(jnp.int32, (ROWS, 128), 1)
    result = []
    for i in range(DEGREE):
        first, offset = divmod(PLANE * i, 128)
        value = chunks[first]
        if offset:
            value = pltpu.roll(value, 128 - offset, 1)
            if offset + PLANE > 128:
                later = pltpu.roll(chunks[first + 1], 128 - offset, 1)
                value = jnp.where(lane < 128 - offset, value, later)
        result.append(value)
    return result


def merge(parts):
    lane = lax.broadcasted_iota(jnp.int32, (ROWS, 128), 1)
    result = []
    for part in range(8):
        value = None
        for i in range(DEGREE):
            start = PLANE * i - 128 * part
            if start >= 128 or start + PLANE <= 0:
                continue
            piece = parts[i]
            if start % 128:
                piece = pltpu.roll(piece, start % 128, 1)
            if value is None:
                value = piece
            else:
                value = jnp.where(lane < start, value, piece)
        if part == 7:
            value = jnp.where(lane < CELLS - 896, value, 0.0)
        result.append(value)
    return result


def pack_rows(rows, start, number, flat_ref):
    for first in range(start, start + number, 8):
        for n in range(COUNT):
            for part in range(8):
                if part < 7:
                    value = rows[n, first : first + 8, 128 * part : 128 * part + 128]
                else:
                    value = rows[n, first : first + 8, 896:CELLS]
                    value = jnp.concatenate([value, jnp.zeros((8, 1024 - CELLS), f32)], axis=1)
                flat_ref[pl.ds(first * HEIGHT + n * 8 + part, 8, stride=HEIGHT), :] = value


def block(flat, index):
    return flat[index * HEIGHT : (index + 1) * HEIGHT, :]


def fetch(pairs, sems):
    copies = [pltpu.make_async_copy(source, target, sems.at[i]) for i, (source, target) in enumerate(pairs)]
    for copy in copies:
        copy.start()
    return copies


def first_kernel(orbital, send_ref, leaves_ref, out_ref, send, rows, flat, filled, sems):
    quarter = PER // 4
    pairs = [(send_ref, send)]
    for i in range(4):
        span = slice(i * quarter, (i + 1) * quarter)
        pairs.append((leaves_ref.at[orbital : orbital + COUNT, span, :], rows.at[:, span, :]))
    copies = fetch(pairs, sems)
    for i in range(4):
        copies[i + 1].wait()
        pack_rows(rows, i * quarter, quarter, flat)
    copies[0].wait()
    outs = []
    quarter = SLOTS // 4
    for i in range(4):
        for slot in range(i * quarter, (i + 1) * quarter):
            start = pl.multiple_of(jnp.minimum(send[0, SLOT_ORDER[slot]], PER - 1) * HEIGHT, HEIGHT)
            filled[slot] = flat[pl.ds(start, HEIGHT), :]
        span = slice(i * quarter, (i + 1) * quarter)
        out = pltpu.make_async_copy(filled.at[span], out_ref.at[span], sems.at[5 + i])
        out.start()
        outs.append(out)
    for out in outs:
        out.wait()


def rest_kernel(orbital, maps, leaves_ref, out_ref, rows, flat, filled, sems):
    number = 7 * PARENTS
    pairs = []
    for i in range(3):
        span = slice(i * number, (i + 1) * number)
        source = leaves_ref.at[orbital : orbital + COUNT, PER + i * number : PER + (i + 1) * number, :]
        pairs.append((source, rows.at[:, span, :]))
    copies = fetch(pairs, sems)
    outs = []
    for i in range(3):
        copies[i].wait()
        pack_rows(rows, i * number, number, flat)
        for child in range(number):
            filled[i, maps[TAKE + i + 1, PARENTS + child]] = block(flat, i * number + child)
        out = pltpu.make_async_copy(filled.at[i], out_ref.at[i], sems.at[3 + i])
        out.start()
        outs.append(out)
    for out in outs:
        out.wait()


def one_hot(dims, axis, index):
    return (lax.broadcasted_iota(jnp.int32, dims, axis) == index).astype(f32)


def plane_index(dims, axis, size):
    position = lax.broadcasted_iota(jnp.int32, dims, axis)
    w, cell = (position >> 7, position & 127)
    j = (cell * 205) >> 11
    k = cell - DEGREE * j
    if size > DEGREE:
        j, k = (j + DEGREE * (w >> 1), k + DEGREE * (w & 1))
    dead = cell >= PLANE
    return jnp.where(dead, -1, j), jnp.where(dead, -1, k)


def exact(left, right, dims=((1,), (0,))):
    return lax.dot_general(left, right, (dims, ((), ())), precision=highest, preferred_element_type=f32)


def planes(filters, outs, ins):
    rows, columns = ((ins // DEGREE) ** 2 * 128, (outs // DEGREE) ** 2 * 128)
    factors = []
    for left, right in zip(plane_index((rows, ins), 0, ins), plane_index((outs, columns), 1, outs)):
        half = exact(one_hot((rows, ins), 1, left), filters, ((1,), (1,)))
        factors.append(exact(half, one_hot((outs, columns), 0, right)))
    return split(factors[0] * factors[1])


def spread(filters, outs, ins):
    rows, columns = (outs * ROWS, ins * ROWS)
    left = one_hot((rows, outs), 1, lax.broadcasted_iota(jnp.int32, (rows, outs), 0) >> 4)
    right = one_hot((ins, columns), 0, lax.broadcasted_iota(jnp.int32, (ins, columns), 1) >> 4)
    row = lax.broadcasted_iota(jnp.int32, (rows, columns), 0) & (ROWS - 1)
    column = lax.broadcasted_iota(jnp.int32, (rows, columns), 1) & (ROWS - 1)
    return split(jnp.where(row == column, exact(exact(left, filters), right), 0.0))


def weight_kernel(up_ref, down_ref, bank_ref, bank, sem):
    both = exact(down_ref[...], up_ref[...])
    up, down = (up_ref[0:DEGREE, :], down_ref[:, 0:DEGREE])
    sizes = ((UP_ROW, up, 10, 20), (BOTH_ROW, both, 20, 20), (DOWN_ROW, down, 20, 10))
    for start, filters, outs, ins in sizes:
        high, low = spread(filters, outs, ins)
        rows, depth = (outs * ROWS, ins * ROWS)
        for i, value in enumerate((high, high, low)):
            bank[start : start + rows, i * depth : (i + 1) * depth] = value
    high, low = planes(both, 20, 20)
    bank[BOTH_PLANE : BOTH_PLANE + 512, 0:512] = high
    bank[BOTH_PLANE : BOTH_PLANE + 512, 512:1024] = low
    high, low = planes(up, 10, 20)
    bank[UP_PLANE : UP_PLANE + 512, 0:128] = high
    bank[UP_PLANE : UP_PLANE + 512, 128:256] = low
    high, low = planes(down, 20, 10)
    bank[DOWN_PLANE : DOWN_PLANE + 128, 0:512] = high
    bank[DOWN_PLANE + 128 : DOWN_PLANE + 256, 0:512] = high
    bank[DOWN_PLANE : DOWN_PLANE + 128, 512:1024] = low
    copy = pltpu.make_async_copy(bank, bank_ref.at[0:BANK_USED, :], sem)
    copy.start()
    copy.wait()


def section(ref, start, rows, columns):
    return ref.at[start : start + rows, 0:columns]


def up_weights(bank_ref):
    return [section(bank_ref, UP_PLANE, 512, 256), section(bank_ref, UP_ROW, 160, 1024)]


def both_weights(bank_ref):
    return [section(bank_ref, BOTH_PLANE, 512, 1024), section(bank_ref, BOTH_ROW, 320, 1024)]


def down_weights(bank_ref):
    return [section(bank_ref, DOWN_PLANE, 256, 1024), section(bank_ref, DOWN_ROW, 320, 512)]


def stacked(value):
    high, low = split(value)
    return jnp.concatenate([high, low, high], axis=0)


def up_product(high, low, weights):
    plane, rows = weights
    wide = dot(high, plane[...])
    half = wide[:, 0:128] + (wide[:, 128:256] + dot(low, plane[:, 0:128]))
    depth = 20 * ROWS
    half = jnp.concatenate([half[n * depth : (n + 1) * depth] for n in range(COUNT)], axis=1)
    value = dot(rows[:, 0 : 3 * depth], stacked(half))
    return [value[:, n * 128 : (n + 1) * 128] for n in range(COUNT)]


def both_product(high, low, weights):
    plane, rows = weights
    half = dot(high, plane[:, 0:512]) + (dot(high, plane[:, 512:1024]) + dot(low, plane[:, 0:512]))
    depth = 20 * ROWS
    return [dot(rows[:, 0 : 3 * depth], stacked(half[n * depth : (n + 1) * depth])) for n in range(COUNT)]


def down_product(high, low, weights):
    plane, rows = weights
    half = dot(jnp.concatenate([high, low], axis=1), plane[:, 0:512]) + dot(high, plane[0:128, 512:1024])
    depth = DEGREE * ROWS
    return [dot(rows[:, 0 : 3 * depth], stacked(half[n * depth : (n + 1) * depth])) for n in range(COUNT)]


def split_children(splits_ref, height):
    return [section(splits_ref, (2 * height + i) * WIDE, WIDE, 512) for i in range(2)]


def window_octants(placed, high_ref, low_ref):
    for n in range(COUNT):
        for octant in range(8):
            first = (n * 8 + octant) * 8
            chunks = [placed[(first + part) * ROWS : (first + part + 1) * ROWS, :] for part in range(8)]
            x, w = divmod(octant, 4)
            for i, value in enumerate(windows(chunks)):
                high, low = split(value)
                start = (n * 20 + x * DEGREE + i) * ROWS
                high_ref[start : start + ROWS, w * 128 : w * 128 + 128] = high
                low_ref[start : start + ROWS, w * 128 : w * 128 + 128] = low


def place_children(height, maps, arrived_ref, placed):
    for child in range(PER):
        octant, parent = (child % 8, child // 8)
        slot = maps[PLACE + height, child]
        for n in range(COUNT):
            value = arrived_ref[slot, n * 8 : n * 8 + 8, :]
            placed[pl.ds((n * 8 + octant) * 8 * ROWS + parent, 8, stride=ROWS), :] = value


def up_kernel(height, arrived_ref, maps_ref, bank_ref, filled_ref, *rest):
    out_ref, kept_ref, maps, high, low, placed, blocks, v0, v1, sems = rest[-10:]
    weights = (v0, v1)
    pairs = [(maps_ref, maps)] + list(zip(up_weights(bank_ref), weights)) + [(filled_ref.at[height], out_ref)]
    copies = fetch(pairs, sems)
    copies[0].wait()
    place_children(height, maps, arrived_ref, placed)
    window_octants(placed, high, low)
    targets = split_children(kept_ref, height)
    outs = [pltpu.make_async_copy(high, targets[0], sems.at[4]), pltpu.make_async_copy(low, targets[1], sems.at[5])]
    for out in outs:
        out.start()
    for copy in copies[1:3]:
        copy.wait()
    values = up_product(high[...], low[...], weights)
    for n in range(COUNT):
        parts = [values[n][i * ROWS : (i + 1) * ROWS, :] for i in range(DEGREE)]
        for part, chunk in enumerate(merge(parts)):
            blocks[pl.ds(n * 8 + part, PARENTS, stride=HEIGHT), :] = chunk
    copies[3].wait()
    for child in range(PARENTS):
        out_ref[maps[TAKE + height + 1, child]] = block(blocks, child)
    for out in outs:
        out.wait()


def emit(height, maps, refined, blocks, out_ref):
    for octant in range(8):
        x, w = divmod(octant, 4)
        for n in range(COUNT):
            parts = []
            for i in range(DEGREE):
                start = (n * 20 + x * DEGREE + i) * ROWS
                parts.append(refined[start : start + ROWS, w * 128 : w * 128 + 128])
            for part, value in enumerate(merge(parts)):
                blocks[pl.ds(octant * HEIGHT + n * 8 + part, PARENTS, stride=8 * HEIGHT), :] = value
    for child in range(PER):
        out_ref[maps[PLACE + height, child]] = block(blocks, child)


def keep(refined, values):
    depth = WIDE // COUNT
    for n in range(COUNT):
        refined[n * depth : (n + 1) * depth, :] = values[n]


def top_kernel(height, arrived_ref, maps_ref, bank_ref, out_ref, *scratch):
    maps, high, low, placed, refined, blocks, v0, v1, sems = scratch
    weights = (v0, v1)
    copies = fetch([(maps_ref, maps)] + list(zip(both_weights(bank_ref), weights)), sems)
    copies[0].wait()
    place_children(height, maps, arrived_ref, placed)
    window_octants(placed, high, low)
    for copy in copies[1:]:
        copy.wait()
    keep(refined, both_product(high[...], low[...], weights))
    emit(height, maps, refined, blocks, out_ref)


def base_kernel(bank_ref, splits_ref, out_ref, *scratch):
    data, weights, refined, sems = (scratch[0:6], scratch[6:12], scratch[12], scratch[13])
    both, up, down = (weights[0:2], weights[2:4], weights[4:6])
    pairs = list(zip(both_weights(bank_ref) + up_weights(bank_ref) + down_weights(bank_ref), weights))
    for height in range(3):
        pairs += list(zip(split_children(splits_ref, height), data[2 * height : 2 * height + 2]))
    copies = fetch(pairs, sems)
    for copy in copies[:6]:
        copy.wait()
    outs = []
    for i in range(3):
        copies[6 + 2 * i].wait()
        copies[7 + 2 * i].wait()
        high, low = (data[2 * i][...], data[2 * i + 1][...])
        corner = jnp.concatenate(up_product(high, low, up), axis=0)
        inner = down_product(*split(corner), down)
        keep(refined.at[i], [whole - part for whole, part in zip(both_product(high, low, both), inner)])
        out = pltpu.make_async_copy(refined.at[i], out_ref.at[i], sems.at[12 + i])
        out.start()
        outs.append(out)
    for out in outs:
        out.wait()


def gather_leaves(height, first, maps, returned_ref, flat, rows, number):
    skip = PER - leaf_range(height)[1]
    for child in range(first, first + number):
        flat[child * HEIGHT : (child + 1) * HEIGHT, :] = returned_ref[maps[TAKE + height, child + skip]]
    for start in range(first, first + number, 8):
        for n in range(COUNT):
            for part in range(8):
                value = flat[pl.ds(start * HEIGHT + n * 8 + part, 8, stride=HEIGHT), :]
                if part < 7:
                    rows[n, start : start + 8, 128 * part : 128 * part + 128] = value
                else:
                    rows[n, start : start + 8, 896:CELLS] = value[:, : CELLS - 896]


def down_kernel(height, returned_ref, maps_ref, base_ref, bank_ref, *rest):
    out_ref, result_ref, maps, base, placed, high, low, refined, blocks, flat_leaves, rows, v0, v1, sems = rest[-14:]
    weights = (v0, v1)
    pairs = [(maps_ref, maps)] + list(zip(down_weights(bank_ref), weights)) + [(base_ref.at[height], base)]
    copies = fetch(pairs, sems)
    copies[0].wait()
    for child in range(PARENTS):
        slot = maps[TAKE + height + 1, child]
        for n in range(COUNT):
            placed[pl.ds(n * 8 * ROWS + child, 8, stride=ROWS), :] = returned_ref[slot, n * 8 : n * 8 + 8, :]
    for n in range(COUNT):
        chunks = [placed[(n * 8 + part) * ROWS : (n * 8 + part + 1) * ROWS, :] for part in range(8)]
        for i, value in enumerate(windows(chunks)):
            start = (n * DEGREE + i) * ROWS
            high[start : start + ROWS, :], low[start : start + ROWS, :] = split(value)
    start, number = leaf_range(height + 1)
    gather_leaves(height + 1, 0, maps, returned_ref, flat_leaves, rows, number)
    store = pltpu.make_async_copy(rows, result_ref.at[:, start : start + number, :], sems.at[4])
    store.start()
    for copy in copies[1:3]:
        copy.wait()
    values = down_product(high[...], low[...], weights)
    copies[3].wait()
    depth = WIDE // COUNT
    keep(refined, [base[n * depth : (n + 1) * depth, :] + values[n] for n in range(COUNT)])
    emit(height, maps, refined, blocks, out_ref)
    store.wait()


def store_kernel(returned_ref, maps_ref, _, out_ref, maps, flat, rows, sems):
    copy = fetch([(maps_ref, maps)], sems)[0]
    copy.wait()
    outs = []
    step = 32
    for first in range(0, PER, step):
        gather_leaves(0, first, maps, returned_ref, flat, rows, step)
        span = slice(first, first + step)
        out = pltpu.make_async_copy(rows.at[:, span, :], out_ref.at[:, span, :], sems.at[1 + first // step])
        out.start()
        outs.append(out)
    for out in outs:
        out.wait()


def shape(*dims, dtype=f32):
    return jax.ShapeDtypeStruct(dims, dtype)


def call(kernel, out_shape, in_specs, out_specs, scratch, operands, flops, name, aliases=None, limit=LIMIT):
    moved = sum(4 * one.size for one in operands)
    return pl.pallas_call(
        kernel,
        out_shape=out_shape,
        in_specs=in_specs,
        out_specs=out_specs,
        scratch_shapes=scratch,
        input_output_aliases=aliases or {},
        compiler_params=pltpu.CompilerParams(vmem_limit_bytes=limit),
        cost_estimate=pl.CostEstimate(flops=flops, bytes_accessed=moved, transcendentals=0),
        name=name,
    )(*operands)


def invert(mapping):
    match = mapping[:, None, :] == jnp.arange(PER, dtype=jnp.int32)[None, :, None]
    return jnp.sum(jnp.where(match, POSITION[None, None, :], 0), axis=2)


def exchange(blocks):
    if lax.axis_size("dev") == 1:
        return blocks
    return lax.all_to_all(blocks, "dev", split_axis=0, concat_axis=0, axis_index_groups=[ORDER], tiled=True)


def flat(number):
    return pltpu.VMEM((number * HEIGHT, 128), f32)


def halves(*dims):
    return [pltpu.VMEM(one, bf16) for one in dims for _ in range(2)]


def single(*dims):
    return [pltpu.VMEM(one, bf16) for one in dims]


class Chain:
    def __init__(self, orbital, rows, send_slot):
        self.orbital = orbital
        self.rows = rows
        self.slots = shape(SLOTS, HEIGHT, 128)
        self.placed = pltpu.VMEM((COUNT * 8 * 8 * ROWS, 128), f32)
        self.going = call(
            functools.partial(first_kernel, orbital),
            self.slots,
            [HBM, HBM],
            HBM,
            [pltpu.SMEM(send_slot.shape, jnp.int32), pltpu.VMEM((COUNT, PER, CELLS), f32), flat(PER)]
            + [pltpu.VMEM((SLOTS, HEIGHT, 128), f32), DMA((9,))],
            (send_slot, rows),
            0,
            "pack_first",
            limit=FULL,
        )

    def swap(self):
        self.arrived = exchange(self.going)

    def prepare(self, maps, bank):
        self.maps, self.bank = (maps, bank)
        self.maps_smem = pltpu.SMEM(maps.shape, jnp.int32)
        self.filled = call(
            functools.partial(rest_kernel, self.orbital),
            shape(LEVEL_ROOM, SLOTS, HEIGHT, 128),
            [SMEM, HBM],
            HBM,
            [pltpu.VMEM((COUNT, 336, CELLS), f32), flat(336), pltpu.VMEM((3, SLOTS, HEIGHT, 128), f32), DMA((6,))],
            (maps, self.rows),
            0,
            "pack_rest",
            limit=FULL,
        )
        self.splits = None

    def up(self, height):
        weights = single((512, 256), (160, 1024))
        scratch = [self.maps_smem] + halves((WIDE, 512)) + [self.placed, flat(PARENTS)] + weights + [DMA((6,))]
        operands = (self.arrived, self.maps, self.bank, self.filled)
        aliases = {}
        if self.splits is not None:
            operands += (self.splits,)
            aliases[4] = 1
        self.going, self.splits = call(
            functools.partial(up_kernel, height),
            (self.slots, shape(SPLITS, 512, dtype=bf16)),
            [VMEM] + [HBM] * (len(operands) - 1),
            (VMEM, HBM),
            scratch,
            operands,
            300_000_000,
            "up",
            aliases,
        )

    def base(self):
        self.bases = call(
            base_kernel,
            shape(BASE_ROOM, WIDE, 512),
            [HBM, HBM],
            HBM,
            halves((WIDE, 512)) * 3
            + single((512, 1024), (320, 1024), (512, 256), (160, 1024), (256, 1024), (320, 512))
            + [pltpu.VMEM((3, WIDE, 512), f32), DMA((15,))],
            (self.bank, self.splits),
            3_600_000_000,
            "base",
            limit=FULL,
        )

    def top(self, height):
        scratch = [self.maps_smem] + halves((WIDE, 512)) + [self.placed, pltpu.VMEM((WIDE, 512), f32), flat(PER)]
        scratch += single((512, 1024), (320, 1024)) + [DMA((3,))]
        self.going = call(
            functools.partial(top_kernel, height),
            self.slots,
            [VMEM, HBM, HBM],
            VMEM,
            scratch,
            (self.arrived, self.maps, self.bank),
            1_200_000_000,
            "top",
        )

    def down(self, height, result):
        number = leaf_range(height + 1)[1]
        scratch = [self.maps_smem, pltpu.VMEM((WIDE, 512), f32), pltpu.VMEM((COUNT * 8 * ROWS, 128), f32)]
        scratch += halves((WIDE // 2, 128)) + [pltpu.VMEM((WIDE, 512), f32), flat(PER)]
        scratch += [flat(number), pltpu.VMEM((COUNT, number, CELLS), f32)]
        scratch += single((256, 1024), (320, 512)) + [DMA((5,))]
        operands = (self.arrived, self.maps, self.bases, self.bank)
        if result is not None:
            operands += (result,)
        self.going, result = call(
            functools.partial(down_kernel, height),
            (self.slots, shape(2, PER + 336, CELLS)),
            [VMEM] + [HBM] * (len(operands) - 1),
            (VMEM, HBM),
            scratch,
            operands,
            400_000_000,
            "down",
            None if result is None else {4: 1},
        )
        return result

    def store(self, result):
        return call(
            store_kernel,
            shape(*result.shape),
            [VMEM, HBM, HBM],
            HBM,
            [self.maps_smem, flat(PER), pltpu.VMEM((COUNT, PER, CELLS), f32), DMA((5,))],
            (self.arrived, self.maps, result),
            0,
            "store",
            {2: 0},
        )


def transform(leaves, send_slot, recv_slot, filter_up, filter_down):
    levels = send_slot.shape[0]
    rows = jnp.swapaxes(leaves, 1, 2)
    chains = [Chain(group[0], rows, send_slot) for group in GROUPS]
    for chain in chains:
        chain.swap()
    maps = jnp.concatenate([invert(send_slot), invert(recv_slot)], axis=0)
    bank = call(
        weight_kernel,
        shape(BANK, 1024, dtype=bf16),
        [VMEM, VMEM],
        HBM,
        [pltpu.VMEM((BANK_USED, 1024), bf16), DMA],
        (filter_up, filter_down),
        50_000_000,
        "weights",
        limit=FULL,
    )
    for chain in chains:
        chain.prepare(maps, bank)
    for height in range(levels - 1):
        for chain in chains:
            chain.up(height)
            chain.swap()
    height = levels - 1
    for chain in chains:
        chain.base()
        chain.top(height)
        chain.swap()
    result = None
    for height in reversed(range(levels - 1)):
        for chain in chains:
            result = chain.down(height, result)
            chain.swap()
    for chain in chains:
        result = chain.store(result)
    return jnp.swapaxes(result, 1, 2)


def solution(mesh):
    in_specs = (P(None, None, "dev"), P(None, "dev"), P(None, "dev"), P(), P())
    out_specs = P(None, None, "dev")
    return jax.shard_map(transform, mesh=mesh, in_specs=in_specs, out_specs=out_specs, check_vma=False)
```

```python
import functools

import jax
import jax.numpy as jnp
from jax import lax
from jax.experimental import pallas as pl
from jax.experimental.pallas import tpu as pltpu
from jax.sharding import PartitionSpec as P

PER = 128
PARENTS = 16
DEGREE = 10
CELLS = 1000
PLANE = 100
SLOTS = 256
GROUPS = ((0, 1),)
COUNT = len(GROUPS[0])
HEIGHT = 8 * COUNT
ROWS = PARENTS
WIDE = COUNT * 20 * ROWS
LIMIT = 50_000_000
FULL = 63_400_000
TAKE = 0
PLACE = 4
UP_ROW, BOTH_ROW, DOWN_ROW, BOTH_PLANE, UP_PLANE, DOWN_PLANE, BANK_USED = (0, 160, 480, 800, 1312, 1824, 2080)
BANK = 5376
SPLITS = 10496
LEVEL_ROOM = 12 // COUNT
BASE_ROOM = 18 // COUNT

highest = lax.Precision.HIGHEST
f32 = jnp.float32
bf16 = jnp.bfloat16
VMEM = pl.BlockSpec(memory_space=pltpu.VMEM)
SMEM = pl.BlockSpec(memory_space=pltpu.SMEM)
HBM = pl.BlockSpec(memory_space=pltpu.HBM)
DMA = pltpu.SemaphoreType.DMA


def leaf_range(height):
    if height == 0:
        return (0, PER)
    return (PER + 7 * PARENTS * (height - 1), 7 * PARENTS)


def split(value):
    high = value.astype(bf16)
    return high, (value - high.astype(f32)).astype(bf16)


def dot(left, right):
    return jnp.dot(left, right, preferred_element_type=f32)


def windows(chunks):
    lane = lax.broadcasted_iota(jnp.int32, (ROWS, 128), 1)
    result = []
    for i in range(DEGREE):
        first, offset = divmod(PLANE * i, 128)
        value = chunks[first]
        if offset:
            value = pltpu.roll(value, 128 - offset, 1)
            if offset + PLANE > 128:
                later = pltpu.roll(chunks[first + 1], 128 - offset, 1)
                value = jnp.where(lane < 128 - offset, value, later)
        result.append(value)
    return result


def merge(parts):
    lane = lax.broadcasted_iota(jnp.int32, (ROWS, 128), 1)
    result = []
    for part in range(8):
        value = None
        for i in range(DEGREE):
            start = PLANE * i - 128 * part
            if start >= 128 or start + PLANE <= 0:
                continue
            piece = parts[i]
            if start % 128:
                piece = pltpu.roll(piece, start % 128, 1)
            if value is None:
                value = piece
            else:
                value = jnp.where(lane < start, value, piece)
        if part == 7:
            value = jnp.where(lane < CELLS - 896, value, 0.0)
        result.append(value)
    return result


def pack_rows(rows, start, number, flat_ref):
    for first in range(start, start + number, 8):
        for n in range(COUNT):
            for part in range(8):
                if part < 7:
                    value = rows[n, first : first + 8, 128 * part : 128 * part + 128]
                else:
                    value = rows[n, first : first + 8, 896:CELLS]
                    value = jnp.concatenate([value, jnp.zeros((8, 1024 - CELLS), f32)], axis=1)
                flat_ref[pl.ds(first * HEIGHT + n * 8 + part, 8, stride=HEIGHT), :] = value


def block(flat, index):
    return flat[index * HEIGHT : (index + 1) * HEIGHT, :]


def fetch(pairs, sems):
    copies = [pltpu.make_async_copy(source, target, sems.at[i]) for i, (source, target) in enumerate(pairs)]
    for copy in copies:
        copy.start()
    return copies


def first_kernel(orbital, send_ref, leaves_ref, out_ref, send, rows, flat, filled, sems):
    quarter = PER // 4
    pairs = [(send_ref, send)]
    for i in range(4):
        span = slice(i * quarter, (i + 1) * quarter)
        pairs.append((leaves_ref.at[orbital : orbital + COUNT, span, :], rows.at[:, span, :]))
    copies = fetch(pairs, sems)
    for i in range(4):
        copies[i + 1].wait()
        pack_rows(rows, i * quarter, quarter, flat)
    copies[0].wait()
    outs = []
    quarter = SLOTS // 4
    for i in range(4):
        for slot in range(i * quarter, (i + 1) * quarter):
            start = pl.multiple_of(jnp.minimum(send[0, slot], PER - 1) * HEIGHT, HEIGHT)
            filled[slot] = flat[pl.ds(start, HEIGHT), :]
        span = slice(i * quarter, (i + 1) * quarter)
        out = pltpu.make_async_copy(filled.at[span], out_ref.at[span], sems.at[5 + i])
        out.start()
        outs.append(out)
    for out in outs:
        out.wait()


def rest_kernel(orbital, maps, leaves_ref, out_ref, rows, flat, filled, sems):
    number = 7 * PARENTS
    pairs = []
    for i in range(3):
        span = slice(i * number, (i + 1) * number)
        source = leaves_ref.at[orbital : orbital + COUNT, PER + i * number : PER + (i + 1) * number, :]
        pairs.append((source, rows.at[:, span, :]))
    copies = fetch(pairs, sems)
    outs = []
    for i in range(3):
        copies[i].wait()
        pack_rows(rows, i * number, number, flat)
        for child in range(number):
            filled[i, maps[TAKE + i + 1, PARENTS + child]] = block(flat, i * number + child)
        out = pltpu.make_async_copy(filled.at[i], out_ref.at[i], sems.at[3 + i])
        out.start()
        outs.append(out)
    for out in outs:
        out.wait()


def one_hot(dims, axis, index):
    return (lax.broadcasted_iota(jnp.int32, dims, axis) == index).astype(f32)


def plane_index(dims, axis, size):
    position = lax.broadcasted_iota(jnp.int32, dims, axis)
    w, cell = (position >> 7, position & 127)
    j = (cell * 205) >> 11
    k = cell - DEGREE * j
    if size > DEGREE:
        j, k = (j + DEGREE * (w >> 1), k + DEGREE * (w & 1))
    dead = cell >= PLANE
    return jnp.where(dead, -1, j), jnp.where(dead, -1, k)


def exact(left, right, dims=((1,), (0,))):
    return lax.dot_general(left, right, (dims, ((), ())), precision=highest, preferred_element_type=f32)


def planes(filters, outs, ins):
    rows, columns = ((ins // DEGREE) ** 2 * 128, (outs // DEGREE) ** 2 * 128)
    factors = []
    for left, right in zip(plane_index((rows, ins), 0, ins), plane_index((outs, columns), 1, outs)):
        half = exact(one_hot((rows, ins), 1, left), filters, ((1,), (1,)))
        factors.append(exact(half, one_hot((outs, columns), 0, right)))
    return split(factors[0] * factors[1])


def spread(filters, outs, ins):
    rows, columns = (outs * ROWS, ins * ROWS)
    left = one_hot((rows, outs), 1, lax.broadcasted_iota(jnp.int32, (rows, outs), 0) >> 4)
    right = one_hot((ins, columns), 0, lax.broadcasted_iota(jnp.int32, (ins, columns), 1) >> 4)
    row = lax.broadcasted_iota(jnp.int32, (rows, columns), 0) & (ROWS - 1)
    column = lax.broadcasted_iota(jnp.int32, (rows, columns), 1) & (ROWS - 1)
    return split(jnp.where(row == column, exact(exact(left, filters), right), 0.0))


def weight_kernel(up_ref, down_ref, bank_ref, bank, sem):
    both = exact(down_ref[...], up_ref[...])
    up, down = (up_ref[0:DEGREE, :], down_ref[:, 0:DEGREE])
    sizes = ((UP_ROW, up, 10, 20), (BOTH_ROW, both, 20, 20), (DOWN_ROW, down, 20, 10))
    for start, filters, outs, ins in sizes:
        high, low = spread(filters, outs, ins)
        rows, depth = (outs * ROWS, ins * ROWS)
        for i, value in enumerate((high, high, low)):
            bank[start : start + rows, i * depth : (i + 1) * depth] = value
    high, low = planes(both, 20, 20)
    bank[BOTH_PLANE : BOTH_PLANE + 512, 0:512] = high
    bank[BOTH_PLANE : BOTH_PLANE + 512, 512:1024] = low
    high, low = planes(up, 10, 20)
    bank[UP_PLANE : UP_PLANE + 512, 0:128] = high
    bank[UP_PLANE : UP_PLANE + 512, 128:256] = low
    high, low = planes(down, 20, 10)
    bank[DOWN_PLANE : DOWN_PLANE + 128, 0:512] = high
    bank[DOWN_PLANE + 128 : DOWN_PLANE + 256, 0:512] = high
    bank[DOWN_PLANE : DOWN_PLANE + 128, 512:1024] = low
    copy = pltpu.make_async_copy(bank, bank_ref.at[0:BANK_USED, :], sem)
    copy.start()
    copy.wait()


def section(ref, start, rows, columns):
    return ref.at[start : start + rows, 0:columns]


def up_weights(bank_ref):
    return [section(bank_ref, UP_PLANE, 512, 256), section(bank_ref, UP_ROW, 160, 1024)]


def both_weights(bank_ref):
    return [section(bank_ref, BOTH_PLANE, 512, 1024), section(bank_ref, BOTH_ROW, 320, 1024)]


def down_weights(bank_ref):
    return [section(bank_ref, DOWN_PLANE, 256, 1024), section(bank_ref, DOWN_ROW, 320, 512)]


def stacked(value):
    high, low = split(value)
    return jnp.concatenate([high, low, high], axis=0)


def up_product(high, low, weights):
    plane, rows = weights
    wide = dot(high, plane[...])
    half = wide[:, 0:128] + (wide[:, 128:256] + dot(low, plane[:, 0:128]))
    depth = 20 * ROWS
    half = jnp.concatenate([half[n * depth : (n + 1) * depth] for n in range(COUNT)], axis=1)
    value = dot(rows[:, 0 : 3 * depth], stacked(half))
    return [value[:, n * 128 : (n + 1) * 128] for n in range(COUNT)]


def both_product(high, low, weights):
    plane, rows = weights
    half = dot(high, plane[:, 0:512]) + (dot(high, plane[:, 512:1024]) + dot(low, plane[:, 0:512]))
    depth = 20 * ROWS
    return [dot(rows[:, 0 : 3 * depth], stacked(half[n * depth : (n + 1) * depth])) for n in range(COUNT)]


def down_product(high, low, weights):
    plane, rows = weights
    half = dot(jnp.concatenate([high, low], axis=1), plane[:, 0:512]) + dot(high, plane[0:128, 512:1024])
    depth = DEGREE * ROWS
    return [dot(rows[:, 0 : 3 * depth], stacked(half[n * depth : (n + 1) * depth])) for n in range(COUNT)]


def split_children(splits_ref, height):
    return [section(splits_ref, (2 * height + i) * WIDE, WIDE, 512) for i in range(2)]


def window_octants(placed, high_ref, low_ref):
    for n in range(COUNT):
        for octant in range(8):
            first = (n * 8 + octant) * 8
            chunks = [placed[(first + part) * ROWS : (first + part + 1) * ROWS, :] for part in range(8)]
            x, w = divmod(octant, 4)
            for i, value in enumerate(windows(chunks)):
                high, low = split(value)
                start = (n * 20 + x * DEGREE + i) * ROWS
                high_ref[start : start + ROWS, w * 128 : w * 128 + 128] = high
                low_ref[start : start + ROWS, w * 128 : w * 128 + 128] = low


def place_children(height, maps, arrived_ref, placed):
    for child in range(PER):
        octant, parent = (child % 8, child // 8)
        slot = maps[PLACE + height, child]
        for n in range(COUNT):
            value = arrived_ref[slot, n * 8 : n * 8 + 8, :]
            placed[pl.ds((n * 8 + octant) * 8 * ROWS + parent, 8, stride=ROWS), :] = value


def up_kernel(height, arrived_ref, maps_ref, bank_ref, filled_ref, *rest):
    out_ref, kept_ref, maps, high, low, placed, blocks, v0, v1, sems = rest[-10:]
    weights = (v0, v1)
    pairs = [(maps_ref, maps)] + list(zip(up_weights(bank_ref), weights)) + [(filled_ref.at[height], out_ref)]
    copies = fetch(pairs, sems)
    copies[0].wait()
    place_children(height, maps, arrived_ref, placed)
    window_octants(placed, high, low)
    targets = split_children(kept_ref, height)
    outs = [pltpu.make_async_copy(high, targets[0], sems.at[4]), pltpu.make_async_copy(low, targets[1], sems.at[5])]
    for out in outs:
        out.start()
    for copy in copies[1:3]:
        copy.wait()
    values = up_product(high[...], low[...], weights)
    for n in range(COUNT):
        parts = [values[n][i * ROWS : (i + 1) * ROWS, :] for i in range(DEGREE)]
        for part, chunk in enumerate(merge(parts)):
            blocks[pl.ds(n * 8 + part, PARENTS, stride=HEIGHT), :] = chunk
    copies[3].wait()
    for child in range(PARENTS):
        out_ref[maps[TAKE + height + 1, child]] = block(blocks, child)
    for out in outs:
        out.wait()


def emit(height, maps, refined, blocks, out_ref):
    for octant in range(8):
        x, w = divmod(octant, 4)
        for n in range(COUNT):
            parts = []
            for i in range(DEGREE):
                start = (n * 20 + x * DEGREE + i) * ROWS
                parts.append(refined[start : start + ROWS, w * 128 : w * 128 + 128])
            for part, value in enumerate(merge(parts)):
                blocks[pl.ds(octant * HEIGHT + n * 8 + part, PARENTS, stride=8 * HEIGHT), :] = value
    for child in range(PER):
        out_ref[maps[PLACE + height, child]] = block(blocks, child)


def keep(refined, values):
    depth = WIDE // COUNT
    for n in range(COUNT):
        refined[n * depth : (n + 1) * depth, :] = values[n]


def top_kernel(height, arrived_ref, maps_ref, bank_ref, out_ref, *scratch):
    maps, high, low, placed, refined, blocks, v0, v1, sems = scratch
    weights = (v0, v1)
    copies = fetch([(maps_ref, maps)] + list(zip(both_weights(bank_ref), weights)), sems)
    copies[0].wait()
    place_children(height, maps, arrived_ref, placed)
    window_octants(placed, high, low)
    for copy in copies[1:]:
        copy.wait()
    keep(refined, both_product(high[...], low[...], weights))
    emit(height, maps, refined, blocks, out_ref)


def base_kernel(bank_ref, splits_ref, out_ref, *scratch):
    data, weights, refined, sems = (scratch[0:6], scratch[6:12], scratch[12], scratch[13])
    both, up, down = (weights[0:2], weights[2:4], weights[4:6])
    pairs = list(zip(both_weights(bank_ref) + up_weights(bank_ref) + down_weights(bank_ref), weights))
    for height in range(3):
        pairs += list(zip(split_children(splits_ref, height), data[2 * height : 2 * height + 2]))
    copies = fetch(pairs, sems)
    for copy in copies[:6]:
        copy.wait()
    outs = []
    for i in range(3):
        copies[6 + 2 * i].wait()
        copies[7 + 2 * i].wait()
        high, low = (data[2 * i][...], data[2 * i + 1][...])
        corner = jnp.concatenate(up_product(high, low, up), axis=0)
        inner = down_product(*split(corner), down)
        keep(refined.at[i], [whole - part for whole, part in zip(both_product(high, low, both), inner)])
        out = pltpu.make_async_copy(refined.at[i], out_ref.at[i], sems.at[12 + i])
        out.start()
        outs.append(out)
    for out in outs:
        out.wait()


def gather_leaves(height, first, maps, returned_ref, flat, rows, number):
    skip = PER - leaf_range(height)[1]
    for child in range(first, first + number):
        flat[child * HEIGHT : (child + 1) * HEIGHT, :] = returned_ref[maps[TAKE + height, child + skip]]
    for start in range(first, first + number, 8):
        for n in range(COUNT):
            for part in range(8):
                value = flat[pl.ds(start * HEIGHT + n * 8 + part, 8, stride=HEIGHT), :]
                if part < 7:
                    rows[n, start : start + 8, 128 * part : 128 * part + 128] = value
                else:
                    rows[n, start : start + 8, 896:CELLS] = value[:, : CELLS - 896]


def down_kernel(height, returned_ref, maps_ref, base_ref, bank_ref, *rest):
    out_ref, result_ref, maps, base, placed, high, low, refined, blocks, flat_leaves, rows, v0, v1, sems = rest[-14:]
    weights = (v0, v1)
    pairs = [(maps_ref, maps)] + list(zip(down_weights(bank_ref), weights)) + [(base_ref.at[height], base)]
    copies = fetch(pairs, sems)
    copies[0].wait()
    for child in range(PARENTS):
        slot = maps[TAKE + height + 1, child]
        for n in range(COUNT):
            placed[pl.ds(n * 8 * ROWS + child, 8, stride=ROWS), :] = returned_ref[slot, n * 8 : n * 8 + 8, :]
    for n in range(COUNT):
        chunks = [placed[(n * 8 + part) * ROWS : (n * 8 + part + 1) * ROWS, :] for part in range(8)]
        for i, value in enumerate(windows(chunks)):
            start = (n * DEGREE + i) * ROWS
            high[start : start + ROWS, :], low[start : start + ROWS, :] = split(value)
    for copy in copies[1:3]:
        copy.wait()
    values = down_product(high[...], low[...], weights)
    start, number = leaf_range(height + 1)
    gather_leaves(height + 1, 0, maps, returned_ref, flat_leaves, rows, number)
    store = pltpu.make_async_copy(rows, result_ref.at[:, start : start + number, :], sems.at[4])
    store.start()
    copies[3].wait()
    depth = WIDE // COUNT
    keep(refined, [base[n * depth : (n + 1) * depth, :] + values[n] for n in range(COUNT)])
    emit(height, maps, refined, blocks, out_ref)
    store.wait()


def store_kernel(returned_ref, maps_ref, _, out_ref, maps, flat, rows, sems):
    copy = fetch([(maps_ref, maps)], sems)[0]
    copy.wait()
    outs = []
    step = 32
    for first in range(0, PER, step):
        gather_leaves(0, first, maps, returned_ref, flat, rows, step)
        span = slice(first, first + step)
        out = pltpu.make_async_copy(rows.at[:, span, :], out_ref.at[:, span, :], sems.at[1 + first // step])
        out.start()
        outs.append(out)
    for out in outs:
        out.wait()


def shape(*dims, dtype=f32):
    return jax.ShapeDtypeStruct(dims, dtype)


def call(kernel, out_shape, in_specs, out_specs, scratch, operands, flops, name, aliases=None, limit=LIMIT):
    moved = sum(4 * one.size for one in operands)
    return pl.pallas_call(
        kernel,
        out_shape=out_shape,
        in_specs=in_specs,
        out_specs=out_specs,
        scratch_shapes=scratch,
        input_output_aliases=aliases or {},
        compiler_params=pltpu.CompilerParams(vmem_limit_bytes=limit),
        cost_estimate=pl.CostEstimate(flops=flops, bytes_accessed=moved, transcendentals=0),
        name=name,
    )(*operands)


def invert(mapping):
    match = mapping[:, None, :] == jnp.arange(PER, dtype=jnp.int32)[None, :, None]
    return jnp.sum(jnp.where(match, jnp.arange(mapping.shape[1], dtype=jnp.int32)[None, None, :], 0), axis=2)


def exchange(blocks):
    return lax.all_to_all(blocks, "dev", split_axis=0, concat_axis=0, tiled=True)


def flat(number, spare=HEIGHT):
    return pltpu.VMEM((number * HEIGHT + spare, 128), f32)


def halves(*dims):
    return [pltpu.VMEM(one, bf16) for one in dims for _ in range(2)]


def single(*dims):
    return [pltpu.VMEM(one, bf16) for one in dims]


class Chain:
    def __init__(self, orbital, rows, send_slot):
        self.orbital = orbital
        self.rows = rows
        self.slots = shape(SLOTS, HEIGHT, 128)
        self.placed = pltpu.VMEM((COUNT * 8 * 8 * ROWS + ROWS, 128), f32)
        self.going = call(
            functools.partial(first_kernel, orbital),
            self.slots,
            [HBM, HBM],
            HBM,
            [pltpu.SMEM(send_slot.shape, jnp.int32), pltpu.VMEM((COUNT, PER, CELLS), f32), flat(PER)]
            + [pltpu.VMEM((SLOTS, HEIGHT, 128), f32), DMA((9,))],
            (send_slot, rows),
            0,
            "pack_first",
            limit=FULL,
        )

    def swap(self):
        self.arrived = exchange(self.going)

    def prepare(self, maps, bank):
        self.maps, self.bank = (maps, bank)
        self.maps_smem = pltpu.SMEM(maps.shape, jnp.int32)
        self.filled = call(
            functools.partial(rest_kernel, self.orbital),
            shape(LEVEL_ROOM, SLOTS, HEIGHT, 128),
            [SMEM, HBM],
            HBM,
            [pltpu.VMEM((COUNT, 336, CELLS), f32), flat(336), pltpu.VMEM((3, SLOTS, HEIGHT, 128), f32), DMA((6,))],
            (maps, self.rows),
            0,
            "pack_rest",
            limit=FULL,
        )
        self.splits = None

    def up(self, height):
        weights = single((512, 256), (160, 1024))
        scratch = [self.maps_smem] + halves((WIDE, 512)) + [self.placed, flat(PARENTS)] + weights + [DMA((6,))]
        operands = (self.arrived, self.maps, self.bank, self.filled)
        aliases = {}
        if self.splits is not None:
            operands += (self.splits,)
            aliases[4] = 1
        self.going, self.splits = call(
            functools.partial(up_kernel, height),
            (self.slots, shape(SPLITS, 512, dtype=bf16)),
            [VMEM] + [HBM] * (len(operands) - 1),
            (VMEM, HBM),
            scratch,
            operands,
            300_000_000,
            "up",
            aliases,
        )

    def base(self):
        self.bases = call(
            base_kernel,
            shape(BASE_ROOM, WIDE, 512),
            [HBM, HBM],
            HBM,
            halves((WIDE, 512)) * 3
            + single((512, 1024), (320, 1024), (512, 256), (160, 1024), (256, 1024), (320, 512))
            + [pltpu.VMEM((3, WIDE, 512), f32), DMA((15,))],
            (self.bank, self.splits),
            3_600_000_000,
            "base",
            limit=FULL,
        )

    def top(self, height):
        scratch = [self.maps_smem] + halves((WIDE, 512)) + [self.placed, pltpu.VMEM((WIDE, 512), f32), flat(PER, 8 * HEIGHT)]
        scratch += single((512, 1024), (320, 1024)) + [DMA((3,))]
        self.going = call(
            functools.partial(top_kernel, height),
            self.slots,
            [VMEM, HBM, HBM],
            VMEM,
            scratch,
            (self.arrived, self.maps, self.bank),
            1_200_000_000,
            "top",
        )

    def down(self, height, result):
        number = leaf_range(height + 1)[1]
        scratch = [self.maps_smem, pltpu.VMEM((WIDE, 512), f32), pltpu.VMEM((COUNT * 8 * ROWS + ROWS, 128), f32)]
        scratch += halves((WIDE // 2, 128)) + [pltpu.VMEM((WIDE, 512), f32), flat(PER, 8 * HEIGHT)]
        scratch += [flat(number), pltpu.VMEM((COUNT, number, CELLS), f32)]
        scratch += single((256, 1024), (320, 512)) + [DMA((5,))]
        operands = (self.arrived, self.maps, self.bases, self.bank)
        if result is not None:
            operands += (result,)
        self.going, result = call(
            functools.partial(down_kernel, height),
            (self.slots, shape(2, PER + 336, CELLS)),
            [VMEM] + [HBM] * (len(operands) - 1),
            (VMEM, HBM),
            scratch,
            operands,
            400_000_000,
            "down",
            None if result is None else {4: 1},
        )
        return result

    def store(self, result):
        return call(
            store_kernel,
            shape(*result.shape),
            [VMEM, HBM, HBM],
            HBM,
            [self.maps_smem, flat(PER), pltpu.VMEM((COUNT, PER, CELLS), f32), DMA((5,))],
            (self.arrived, self.maps, result),
            0,
            "store",
            {2: 0},
        )


def transform(leaves, send_slot, recv_slot, filter_up, filter_down):
    levels = send_slot.shape[0]
    rows = jnp.swapaxes(leaves, 1, 2)
    chains = [Chain(group[0], rows, send_slot) for group in GROUPS]
    for chain in chains:
        chain.swap()
    maps = jnp.concatenate([invert(send_slot), invert(recv_slot)], axis=0)
    bank = call(
        weight_kernel,
        shape(BANK, 1024, dtype=bf16),
        [VMEM, VMEM],
        HBM,
        [pltpu.VMEM((BANK_USED, 1024), bf16), DMA],
        (filter_up, filter_down),
        50_000_000,
        "weights",
        limit=FULL,
    )
    for chain in chains:
        chain.prepare(maps, bank)
    for height in range(levels - 1):
        for chain in chains:
            chain.up(height)
            chain.swap()
    height = levels - 1
    for chain in chains:
        chain.base()
        chain.top(height)
        chain.swap()
    result = None
    for height in reversed(range(levels - 1)):
        for chain in chains:
            result = chain.down(height, result)
            chain.swap()
    for chain in chains:
        result = chain.store(result)
    return jnp.swapaxes(result, 1, 2)


def solution(mesh):
    in_specs = (P(None, None, "dev"), P(None, "dev"), P(None, "dev"), P(), P())
    out_specs = P(None, None, "dev")
    return jax.shard_map(transform, mesh=mesh, in_specs=in_specs, out_specs=out_specs, check_vma=False)
```
